32 devices in a mesh: dp: 8 (over z, x), seq: 4 (over y, core).
Axes of the slice: x: 2, y: 2, z: 4, core: 2. Of those that a mesh axis runs over, the one named last changes fastest.
Arguments:
- hidden_in: bfloat16 [16, 1024, 768], P('dp', 'seq'), may hold values from -6 to 6
- passage_lengths: int32 [16, 8], P('dp'), may hold values from 0 to 512, as said below
- w_qkv: bfloat16 [768, 2304], replicated, may hold values from -0.3125 to 0.3125
- b_query: bfloat16 [768], replicated, may hold values from -3 to 3
- b_value: bfloat16 [768], replicated, may hold values from -3 to 3
- w_attn_out: bfloat16 [768, 768], replicated, may hold values from -0.875 to 0.875
- b_attn_out: bfloat16 [768], replicated, may hold values from -3 to 3
- gain_attn: bfloat16 [768], replicated, may hold values from 0.5 to 1.5
- bias_attn: bfloat16 [768], replicated, may hold values from -3 to 3
- w_inner: bfloat16 [768, 3072], replicated, may hold values from -0.21875 to 0.21875
- b_inner: bfloat16 [3072], replicated, may hold values from -3 to 3
- w_outer: bfloat16 [3072, 768], replicated, may hold values from -0.15625 to 0.15625
- b_outer: bfloat16 [768], replicated, may hold values from -3 to 3
- gain_ffn: bfloat16 [768], replicated, may hold values from 0.5 to 1.5
- bias_ffn: bfloat16 [768], replicated, may hold values from -3 to 3
- grad_out: bfloat16 [16, 1024, 768], P('dp', 'seq'), may hold values from -6 to 6
Outputs:
- out: float32 [16, 1024, 768], P('dp', 'seq')
- pooled: float32 [16, 8, 768], P('dp')
- grad_in: float32 [16, 1024, 768], P('dp', 'seq')
- grad_w_qkv: float32 [768, 2304], P('dp')
- grad_b_query: float32 [768], P('dp')
- grad_b_value: float32 [768], P('dp')
- grad_w_attn_out: float32 [768, 768], P('dp')
- grad_b_attn_out: float32 [768], P('dp')
- grad_gain_attn: float32 [768], P('dp')
- grad_bias_attn: float32 [768], P('dp')
- grad_w_inner: float32 [768, 3072], P('dp')
- grad_b_inner: float32 [3072], P('dp')
- grad_w_outer: float32 [3072, 768], P('dp')
- grad_b_outer: float32 [768], P('dp')
- grad_gain_ffn: float32 [768], P('dp')
- grad_bias_ffn: float32 [768], P('dp')
The draws below stay inside these ranges and needn't reach their ends.
Inputs may be any that keep to these rules, and one draw needn't show every extreme that they name: `passage_lengths`: each row lists its passages' lengths in order, each 20 or more, then zeros; a row's lengths sum to at most 1024, and its later positions are padding.
All inputs are finite; a program needn't handle non-finite values.
Results may differ from the reference program's by a relative error of at most 0.02.
Values may be sent and summed in bfloat16 or wider, within the bound.
No kernel may reach another device: no remote copies, remote signals or barrier semaphores. Data moves between devices by JAX's collectives and lax.ppermute only.
A program may use at most 192 MiB of HBM per device.

```python
import jax
import jax.numpy as jnp
from jax import lax

D = 768
HEADS = 12
HEAD_DIM = 64
FF = 3072
ROWS_DEV = 2
LEN = 1024
SLOTS = 8
PASS_MIN = 20
ROWS = 16


def draw_passage_lengths(key, part):
    key = jax.random.fold_in(key, 11)
    len_key, pad_key, pick_key = jax.random.split(key, 3)
    raw_len = jax.random.randint(len_key, (ROWS, SLOTS), PASS_MIN, LEN // 2 + 1, dtype=jnp.int32)
    run_ends = jnp.cumsum(raw_len, axis=1, dtype=jnp.int32)
    row_limit = LEN - jax.random.randint(pad_key, (ROWS, 1), 0, LEN // 8 + 1, dtype=jnp.int32)
    short_rows = jnp.where(run_ends <= row_limit, raw_len, 0)
    chosen = jax.random.randint(pick_key, (ROWS // ROWS_DEV, 1), 0, ROWS_DEV, dtype=jnp.int32)
    row_place = jnp.arange(ROWS_DEV, dtype=jnp.int32)[None, :]
    long_flag = (row_place == chosen).reshape(ROWS, 1)
    slot_place = jnp.arange(SLOTS, dtype=jnp.int32)[None, :]
    long_rows = jnp.where(slot_place == 0, LEN // 2, jnp.where(slot_place == 1, LEN // 2 - LEN // 16, 0))
    return jnp.where(long_flag, long_rows, short_rows).astype(jnp.int32)


def steps_of(own_key, dims, pieces, smallest, largest):
    factor_of, own = 1.0, jax.random.fold_in(own_key, 6)
    for dim, shards_of in pieces:
        steps = jnp.exp(jax.random.uniform(jax.random.fold_in(own, dim), (shards_of,), jnp.float32, smallest / len(pieces), largest / len(pieces)))
        factor_of = factor_of * jnp.repeat(steps, dims[dim] // shards_of).reshape([-1 if axis == dim else 1 for axis in range(len(dims))])
    return factor_of


def bell_draw(own_key, dims, scale, limit, pieces=(), kind=jnp.bfloat16):
    array = scale * jax.random.normal(own_key, dims, jnp.float32)
    if pieces:
        array = array * steps_of(own_key, dims, pieces, -0.22, 0.18)
    return jnp.clip(array, -limit, limit).astype(kind)


def setup_inputs(seed: int = 0) -> dict:
    key_of = jax.random.split(jax.random.key(seed), 17)
    return {
        "hidden_in": bell_draw(key_of[0], (ROWS, LEN, D), 1.0, 6.0, ((0, 8), (1, 4))),
        "passage_lengths": draw_passage_lengths(jax.random.fold_in(key_of[16], 71), 0),
        "w_qkv": bell_draw(key_of[2], (D, 3 * D), (D // 2) ** -0.5, 0.3125),
        "b_query": bell_draw(key_of[3], (D,), 0.5, 3.0),
        "b_value": bell_draw(key_of[4], (D,), 0.5, 3.0),
        "w_attn_out": bell_draw(key_of[5], (D, D), (D // 16) ** -0.5, 0.875),
        "b_attn_out": bell_draw(key_of[6], (D,), 0.5, 3.0),
        "gain_attn": jnp.clip(1.0 + 0.1 * jax.random.normal(key_of[7], (D,), jnp.float32), 0.5, 1.5).astype(jnp.bfloat16),
        "bias_attn": bell_draw(key_of[8], (D,), 0.5, 3.0),
        "w_inner": bell_draw(key_of[9], (D, FF), D ** -0.5, 0.21875),
        "b_inner": bell_draw(key_of[10], (FF,), 0.5, 3.0),
        "w_outer": bell_draw(key_of[11], (FF, D), (FF // 2) ** -0.5, 0.15625),
        "b_outer": bell_draw(key_of[12], (D,), 0.5, 3.0),
        "gain_ffn": jnp.clip(1.0 + 0.1 * jax.random.normal(key_of[13], (D,), jnp.float32), 0.5, 1.5).astype(jnp.bfloat16),
        "bias_ffn": bell_draw(key_of[14], (D,), 0.5, 3.0),
        "grad_out": bell_draw(key_of[15], (ROWS, LEN, D), 1.0, 6.0, ((0, 8), (1, 4))),
    }


PRECISE = lax.Precision.HIGHEST

@jax.custom_vjp
def low(v):
    return lax.optimization_barrier(v.astype(jnp.bfloat16)).astype(jnp.float32)

@jax.custom_vjp
def low_back(v):
    return v

def low_keep(v):
    return (low(v), None)

def low_pass(kept, grad):
    return (grad,)

def back_keep(v):
    return (v, None)

def back_low(kept, grad):
    return (low(grad),)
low.defvjp(low_keep, low_pass)
low_back.defvjp(back_keep, back_low)

def both_ways(values):
    return low(low_back(values))

def matmul(left, right):
    return jnp.dot(left, right, precision=PRECISE, preferred_element_type=jnp.float32)

def layer_norm(inputs, gain_vec, shift_vec):
    centre = inputs - lax.optimization_barrier(jnp.mean(inputs, axis=-1, keepdims=True))
    spread = lax.optimization_barrier(jnp.mean(centre * centre, axis=-1, keepdims=True))
    return centre * lax.rsqrt(spread + 1e-12) * gain_vec + shift_vec

def segment_ids(lengths):
    pass_ends = jnp.cumsum(lengths, dtype=jnp.int32)
    positions = jnp.arange(LEN, dtype=jnp.int32)
    return lax.optimization_barrier(jnp.sum((positions[:, None] >= pass_ends[None, :]).astype(jnp.int32), axis=1, dtype=jnp.int32))

def attend(queries, keys_in, values_in, segments):
    head_shape = (LEN, HEADS, HEAD_DIM)
    scores = jnp.einsum('qhd,khd->hqk', queries.reshape(head_shape), keys_in.reshape(head_shape), precision=PRECISE) * HEAD_DIM ** (-0.5)
    scores = low_back(scores)
    same_seg = segments[:, None] == segments[None, :]
    scores = jnp.where(same_seg[None], scores, -1e+30)
    row_max = lax.optimization_barrier(jnp.max(scores, axis=-1, keepdims=True))
    exp_scores = jnp.exp(scores - row_max)
    prob_low = low(exp_scores / lax.optimization_barrier(jnp.sum(exp_scores, axis=-1, keepdims=True)))
    mixed = jnp.einsum('hqk,khd->qhd', prob_low, values_in.reshape(head_shape), precision=PRECISE)
    return mixed.reshape(LEN, D)

def row_layer(hidden, params, segments):
    w_qkv, b_query, b_value, w_attn_out, b_attn_out, gain_attn, bias_attn, w_inner, b_inner, w_outer, b_outer, gain_ffn, bias_ffn = params
    packed = matmul(hidden, w_qkv)
    queries = both_ways(packed[:, :D] + b_query)
    keys_in = both_ways(packed[:, D:2 * D])
    values_in = both_ways(packed[:, 2 * D:] + b_value)
    mixed = both_ways(attend(queries, keys_in, values_in, segments))
    branch = low_back(matmul(mixed, w_attn_out) + b_attn_out)
    norm_first = layer_norm(hidden + branch, gain_attn, bias_attn)
    inner_pre = low_back(matmul(low(norm_first), w_inner) + b_inner)
    active = low(jax.nn.gelu(inner_pre, approximate=False))
    second = low_back(matmul(active, w_outer) + b_outer)
    return layer_norm(norm_first + second, gain_ffn, bias_ffn)

def reference(hidden_in, passage_lengths, w_qkv, b_query, b_value, w_attn_out, b_attn_out, gain_attn, bias_attn, w_inner, b_inner, w_outer, b_outer, gain_ffn, bias_ffn, grad_out):
    params = tuple((weight.astype(jnp.float32) for weight in (w_qkv, b_query, b_value, w_attn_out, b_attn_out, gain_attn, bias_attn, w_inner, b_inner, w_outer, b_outer, gain_ffn, bias_ffn)))

    def row_step(grad_totals, row_data):
        hidden, cotangent, lengths = row_data
        segments = segment_ids(lengths)

        def layer_of(inputs, weights):
            return row_layer(inputs, weights, segments)
        output, pullback = jax.vjp(layer_of, hidden.astype(jnp.float32), params)
        grad_hidden, grad_params = pullback(cotangent.astype(jnp.float32))
        onehot = (jnp.arange(SLOTS, dtype=jnp.int32)[:, None] == segments[None, :]).astype(jnp.float32)
        sums = matmul(onehot, output)
        pooled = sums / jnp.maximum(lengths.astype(jnp.float32), 1.0)[:, None]
        grad_totals = jax.tree.map(jnp.add, grad_totals, grad_params)
        return (grad_totals, (output, pooled, grad_hidden))
    zeros = jax.tree.map(jnp.zeros_like, params)
    grad_totals, (outputs, pooled, grad_in) = lax.scan(row_step, zeros, (hidden_in, grad_out, passage_lengths))
    return (outputs, pooled, grad_in, grad_totals[0], grad_totals[1], grad_totals[2], grad_totals[3], grad_totals[4], grad_totals[5], grad_totals[6], grad_totals[7], grad_totals[8], grad_totals[9], grad_totals[10], grad_totals[11], grad_totals[12])
```

```python
import functools
import math

import jax
import jax.numpy as jnp
from jax import lax
from jax.experimental import pallas as pl
from jax.experimental.pallas import tpu as pltpu
from jax.sharding import PartitionSpec as P

LOW = jnp.bfloat16
F32 = jnp.float32
HEADS = 12
HEAD_DIM = 64
LANES = 128
VMEM = 56 * 1024 * 1024
MASKED = -1e30
EPS = 1e-12
HALF_ROOT = math.sqrt(0.5)
PHI_SCALE = 1.0 / math.sqrt(2.0 * math.pi)


def dot(left, right):
    return jnp.dot(left, right, preferred_element_type=F32)


def dot_nt(left, right):
    return lax.dot_general(left, right, (((1,), (1,)), ((), ())), preferred_element_type=F32)


def dot_tn(left, right):
    return lax.dot_general(left, right, (((0,), (0,)), ((), ())), preferred_element_type=F32)


def turned(block):
    return block.astype(F32).T.astype(LOW)


def head_lanes(rows, head):
    lane = lax.broadcasted_iota(jnp.int32, (rows, LANES), 1)
    return (lane >= HEAD_DIM) if head else (lane < HEAD_DIM)


def spread(column, width):
    return jnp.concatenate([column] * (width // LANES), axis=1)


def attend_kernel(need, q_ref, k_ref, v_ref, segk_ref, segq_ref, o_ref, ot_ref, lse_ref,
                  qt, vt, km, mx, tot, acc, *, block, count):
    tokens = block * count
    for i in range(count):
        rows = pl.ds(i * block, block)
        qt[:, rows] = turned(q_ref[rows, :])
        vt[:, rows] = turned(v_ref[rows, :])
    for h in range(2):
        km[h] = jnp.where(head_lanes(tokens, h), k_ref[...], jnp.zeros((), LOW))

    def over_queries(qb, carry):
        cols = pl.ds(pl.multiple_of(qb * block, block), block)
        mx[...] = jnp.full(mx.shape, MASKED, F32)
        tot[...] = jnp.zeros(tot.shape, F32)
        acc[...] = jnp.zeros(acc.shape, F32)

        def over_keys(kb, carry):
            @pl.when(need[qb * count + kb] > 0)
            def _():
                rows = pl.ds(pl.multiple_of(kb * block, block), block)
                same = spread(segk_ref[rows, :], block) == segq_ref[0:1, cols]
                qtb = qt[:, cols]
                for h in range(2):
                    half = pl.ds(h * HEAD_DIM, HEAD_DIM)
                    s = dot(km[h, rows, :], qtb)
                    s = jnp.where(same, s, MASKED)
                    m_old = mx[h : h + 1, :]
                    m_new = jnp.maximum(m_old, jnp.max(s, axis=0, keepdims=True))
                    p = jnp.exp(s - m_new)
                    alpha = jnp.exp(m_old - m_new)
                    mx[h : h + 1, :] = m_new
                    tot[h : h + 1, :] = alpha * tot[h : h + 1, :] + jnp.sum(p, axis=0, keepdims=True)
                    acc[half, :] = alpha * acc[half, :] + dot(vt[half, rows], p.astype(LOW))
            return carry

        lax.fori_loop(0, count, over_keys, 0)
        total = tot[0:2, :]
        inv = 1.0 / total
        full = jnp.concatenate(
            [acc[0:HEAD_DIM, :] * inv[0:1, :], acc[HEAD_DIM:, :] * inv[1:2, :]], axis=0
        )
        ot_ref[:, cols] = full.astype(LOW)
        o_ref[cols, :] = full.T.astype(LOW)
        lse_ref[0, 0:2, cols] = mx[0:2, :] + jnp.log(total)
        return carry

    lax.fori_loop(0, count, over_queries, 0)


def attend(packed, seg_col, seg_row, need, pairs, block):
    tokens = packed.shape[0]
    count = tokens // block
    width = pairs * LANES
    return pl.pallas_call(
        functools.partial(attend_kernel, block=block, count=count),
        grid_spec=pltpu.PrefetchScalarGridSpec(
            num_scalar_prefetch=1,
            grid=(pairs,),
            in_specs=[
                pl.BlockSpec((tokens, LANES), lambda j, n: (0, j)),
                pl.BlockSpec((tokens, LANES), lambda j, n: (0, j + pairs)),
                pl.BlockSpec((tokens, LANES), lambda j, n: (0, j + 2 * pairs)),
                pl.BlockSpec((tokens, LANES), lambda j, n: (0, 0)),
                pl.BlockSpec((8, tokens), lambda j, n: (0, 0)),
            ],
            out_specs=[
                pl.BlockSpec((tokens, LANES), lambda j, n: (0, j)),
                pl.BlockSpec((LANES, tokens), lambda j, n: (j, 0)),
                pl.BlockSpec((1, 8, tokens), lambda j, n: (j, 0, 0)),
            ],
            scratch_shapes=[
                pltpu.VMEM((LANES, tokens), LOW),
                pltpu.VMEM((LANES, tokens), LOW),
                pltpu.VMEM((2, tokens, LANES), LOW),
                pltpu.VMEM((8, block), F32),
                pltpu.VMEM((8, block), F32),
                pltpu.VMEM((LANES, block), F32),
            ],
        ),
        out_shape=[
            jax.ShapeDtypeStruct((tokens, width), LOW),
            jax.ShapeDtypeStruct((width, tokens), LOW),
            jax.ShapeDtypeStruct((pairs, 8, tokens), F32),
        ],
        compiler_params=pltpu.CompilerParams(vmem_limit_bytes=VMEM),
        cost_estimate=pl.CostEstimate(flops=2 * tokens * tokens * width * 2, bytes_accessed=8 * tokens * width, transcendentals=tokens * tokens * 2 * pairs),
        name="attend",
    )(need, packed, packed, packed, seg_col, seg_row)


def attend_back_kernel(need, q_ref, k_ref, v_ref, do_ref, ot_ref, lse_ref, segk_ref, segq_ref,
                       dq_ref, dk_ref, dv_ref, qt, dot_t, kt, km, vm, qm, dom, cen, dqt, dk, dv,
                       *, block, count):
    tokens = block * count
    zero = jnp.zeros((), LOW)
    for i in range(count):
        rows = pl.ds(i * block, block)
        qt[:, rows] = turned(q_ref[rows, :])
        kt[:, rows] = turned(k_ref[rows, :])
        do_t = do_ref[rows, :].astype(F32).T
        dot_t[:, rows] = do_t.astype(LOW)
        both = do_t * ot_ref[:, rows].astype(F32)
        cen[0:1, rows] = jnp.sum(both[0:HEAD_DIM, :], axis=0, keepdims=True)
        cen[1:2, rows] = jnp.sum(both[HEAD_DIM:, :], axis=0, keepdims=True)
    for h in range(2):
        lanes = head_lanes(tokens, h)
        km[h] = jnp.where(lanes, k_ref[...], zero)
        vm[h] = jnp.where(lanes, v_ref[...], zero)
        qm[h] = jnp.where(lanes, q_ref[...], zero)
        dom[h] = jnp.where(lanes, do_ref[...], zero)
    dqt[...] = jnp.zeros(dqt.shape, F32)
    dk[...] = jnp.zeros(dk.shape, F32)
    dv[...] = jnp.zeros(dv.shape, F32)

    def over_queries(qb, carry):
        cols = pl.ds(pl.multiple_of(qb * block, block), block)

        def over_keys(kb, carry):
            @pl.when(need[qb * count + kb] > 0)
            def _():
                rows = pl.ds(pl.multiple_of(kb * block, block), block)
                same = spread(segk_ref[rows, :], block) == segq_ref[0:1, cols]
                qtb = qt[:, cols]
                dob = dot_t[:, cols]
                dk_add = jnp.zeros((block, LANES), F32)
                dv_add = jnp.zeros((block, LANES), F32)
                for h in range(2):
                    half = pl.ds(h * HEAD_DIM, HEAD_DIM)
                    s = dot(km[h, rows, :], qtb)
                    s = jnp.where(same, s, MASKED)
                    p = jnp.exp(s - lse_ref[0, h : h + 1, cols])
                    dp = dot(vm[h, rows, :], dob)
                    ds = (p * (dp - cen[h : h + 1, cols])).astype(LOW)
                    dv_add += dot(p.astype(LOW), dom[h, cols, :])
                    dk_add += dot(ds, qm[h, cols, :])
                    dqt[half, cols] += dot(kt[half, rows], ds)
                dv[rows, :] += dv_add
                dk[rows, :] += dk_add
            return carry

        lax.fori_loop(0, count, over_keys, 0)
        return carry

    lax.fori_loop(0, count, over_queries, 0)
    dk_ref[...] = dk[...].astype(LOW)
    dv_ref[...] = dv[...].astype(LOW)
    for i in range(count):
        rows = pl.ds(i * block, block)
        dq_ref[rows, :] = (dqt[:, rows].T * HEAD_DIM ** (-0.5)).astype(LOW)


def attend_back(packed, grads, ot, lse, seg_col, seg_row, need, pairs, block):
    tokens = packed.shape[0]
    count = tokens // block
    width = pairs * LANES
    return pl.pallas_call(
        functools.partial(attend_back_kernel, block=block, count=count),
        grid_spec=pltpu.PrefetchScalarGridSpec(
            num_scalar_prefetch=1,
            grid=(pairs,),
            in_specs=[
                pl.BlockSpec((tokens, LANES), lambda j, n: (0, j)),
                pl.BlockSpec((tokens, LANES), lambda j, n: (0, j + pairs)),
                pl.BlockSpec((tokens, LANES), lambda j, n: (0, j + 2 * pairs)),
                pl.BlockSpec((tokens, LANES), lambda j, n: (0, j)),
                pl.BlockSpec((LANES, tokens), lambda j, n: (j, 0)),
                pl.BlockSpec((1, 8, tokens), lambda j, n: (j, 0, 0)),
                pl.BlockSpec((tokens, LANES), lambda j, n: (0, 0)),
                pl.BlockSpec((8, tokens), lambda j, n: (0, 0)),
            ],
            out_specs=[pl.BlockSpec((tokens, LANES), lambda j, n: (0, j))] * 3,
            scratch_shapes=[
                pltpu.VMEM((LANES, tokens), LOW),
                pltpu.VMEM((LANES, tokens), LOW),
                pltpu.VMEM((LANES, tokens), LOW),
                pltpu.VMEM((2, tokens, LANES), LOW),
                pltpu.VMEM((2, tokens, LANES), LOW),
                pltpu.VMEM((2, tokens, LANES), LOW),
                pltpu.VMEM((2, tokens, LANES), LOW),
                pltpu.VMEM((8, tokens), F32),
                pltpu.VMEM((LANES, tokens), F32),
                pltpu.VMEM((tokens, LANES), F32),
                pltpu.VMEM((tokens, LANES), F32),
            ],
        ),
        out_shape=[jax.ShapeDtypeStruct((tokens, width), LOW)] * 3,
        compiler_params=pltpu.CompilerParams(vmem_limit_bytes=VMEM),
        cost_estimate=pl.CostEstimate(flops=2 * tokens * tokens * width * 5, bytes_accessed=20 * tokens * width, transcendentals=tokens * tokens * 2 * pairs),
        name="attend_back",
    )(need, packed, packed, packed, grads, ot, lse, seg_col, seg_row)


def row_mean(values):
    return jnp.mean(values, axis=-1, keepdims=True)


def normal(values):
    centre = values - row_mean(values)
    scale = lax.rsqrt(row_mean(centre * centre) + EPS)
    return centre * scale, scale


def normal_back(hat, scale, grads):
    return scale * (grads - row_mean(grads) - hat * row_mean(grads * hat))


def column_total(values):
    return jnp.sum(values, axis=0, keepdims=True)


def feed_kernel(x_ref, o_ref, wa_ref, ba_ref, ga_ref, sa_ref, wi_ref, bi_ref, wo_ref, bo_ref,
                gf_ref, sf_ref, go_ref, seg_ref,
                g_ref, gp_ref, yl_ref, yt_ref, hat_ref, scale_ref, out_ref, dh_ref, dz_ref, dzt_ref,
                small_ref, pool_ref, yl, acc):
    step = pl.program_id(0)

    @pl.when(step == 0)
    def _():
        h1 = x_ref[...].astype(F32) + dot(o_ref[...], wa_ref[...]) + ba_ref[...].astype(F32)
        hat, scale = normal(h1)
        y1 = hat * ga_ref[...].astype(F32) + sa_ref[...].astype(F32)
        hat_ref[...] = hat
        scale_ref[...] = jnp.broadcast_to(scale, scale_ref.shape)
        y1_low = y1.astype(LOW)
        yl[...] = y1_low
        yl_ref[...] = y1_low
        yt_ref[...] = y1.T.astype(LOW)
        acc[...] = y1 + bo_ref[...].astype(F32)

    u = dot(yl[...], wi_ref[...]) + bi_ref[...].astype(F32)
    cdf = 0.5 * (1.0 + lax.erf(u * HALF_ROOT))
    g = (u * cdf).astype(LOW)
    g_ref[...] = g
    gp_ref[...] = (cdf + u * (PHI_SCALE * jnp.exp(-0.5 * u * u))).astype(LOW)
    acc[...] += dot(g, wo_ref[...])

    @pl.when(step == pl.num_programs(0) - 1)
    def _():
        hat, scale = normal(acc[...])
        gain = gf_ref[...].astype(F32)
        out = hat * gain + sf_ref[...].astype(F32)
        out_ref[...] = out
        dy = go_ref[...].astype(F32)
        dh = normal_back(hat, scale, dy * gain)
        dh_ref[...] = dh
        dz = dh.astype(LOW)
        dz_ref[...] = dz
        dzt_ref[...] = dh.T.astype(LOW)
        small_ref[...] = jnp.zeros(small_ref.shape, F32)
        small_ref[0:1, :] = column_total(dy * hat)
        small_ref[1:2, :] = column_total(dy)
        small_ref[2:3, :] = column_total(dz.astype(F32))
        slots = pool_ref.shape[0]
        tokens = out.shape[0]
        place = lax.broadcasted_iota(jnp.int32, (slots, tokens), 0)
        onehot = (place == seg_ref[0:1, :]).astype(LOW)
        high = out.astype(LOW)
        rest = (out - high.astype(F32)).astype(LOW)
        pool_ref[...] = dot(onehot, high) + dot(onehot, rest)


def feed(x, o, wa, ba, ga, sa, wi, bi, wo, bo, gf, sf, go, seg_row, slots, block):
    tokens, dim = x.shape
    wide = wi.shape[1]
    whole = lambda a: pl.BlockSpec(a.shape, lambda i: (0,) * a.ndim)
    vec = lambda a: a.reshape(1, -1)
    ins = (x, o, wa, vec(ba), vec(ga), vec(sa), wi, vec(bi), wo, vec(bo), vec(gf), vec(sf), go, seg_row)
    specs = [whole(a) for a in ins]
    specs[6] = pl.BlockSpec((dim, block), lambda i: (0, i))
    specs[7] = pl.BlockSpec((1, block), lambda i: (0, i))
    specs[8] = pl.BlockSpec((block, dim), lambda i: (i, 0))
    outs = [
        ((tokens, wide), LOW, (tokens, block), lambda i: (0, i)),
        ((tokens, wide), LOW, (tokens, block), lambda i: (0, i)),
        ((tokens, dim), LOW, None, None),
        ((dim, tokens), LOW, None, None),
        ((tokens, dim), F32, None, None),
        ((tokens, LANES), F32, None, None),
        ((tokens, dim), F32, None, None),
        ((tokens, dim), F32, None, None),
        ((tokens, dim), LOW, None, None),
        ((dim, tokens), LOW, None, None),
        ((8, dim), F32, None, None),
        ((slots, dim), F32, None, None),
    ]
    return pl.pallas_call(
        feed_kernel,
        grid=(wide // block,),
        in_specs=specs,
        out_specs=[
            pl.BlockSpec(b or s, m or (lambda i: (0, 0))) for s, _, b, m in outs
        ],
        out_shape=[jax.ShapeDtypeStruct(s, t) for s, t, _, _ in outs],
        scratch_shapes=[pltpu.VMEM((tokens, dim), LOW), pltpu.VMEM((tokens, dim), F32)],
        compiler_params=pltpu.CompilerParams(vmem_limit_bytes=VMEM),
        cost_estimate=pl.CostEstimate(flops=4 * tokens * dim * wide + 2 * tokens * dim * dim, bytes_accessed=4 * dim * wide + 4 * tokens * wide + 30 * tokens * dim, transcendentals=2 * tokens * wide),
        name="feed",
    )(*ins)


def outer_kernel(dzt_ref, g_ref, out_ref):
    out_ref[0] = dot(dzt_ref[...], g_ref[...]).astype(LOW)


def outer_grads(dzt, g, block):
    dim, tokens = dzt.shape
    wide = g.shape[1]
    count = wide // block
    return pl.pallas_call(
        outer_kernel,
        grid=(count,),
        in_specs=[
            pl.BlockSpec((dim, tokens), lambda i: (0, 0)),
            pl.BlockSpec((tokens, block), lambda i: (0, i)),
        ],
        out_specs=pl.BlockSpec((1, dim, block), lambda i: (i, 0, 0)),
        out_shape=jax.ShapeDtypeStruct((count, dim, block), LOW),
        compiler_params=pltpu.CompilerParams(vmem_limit_bytes=VMEM),
        cost_estimate=pl.CostEstimate(flops=2 * tokens * dim * wide, bytes_accessed=2 * dim * wide + 2 * tokens * (wide + dim), transcendentals=0),
        name="outer_grads",
    )(dzt, g)


def inner_kernel(dz_ref, gp_ref, yt_ref, wo_ref, wi_ref, dh_ref, hat_ref, scale_ref, ga_ref, wa_ref,
                 grad_ref, bias_ref, dsum_ref, da_ref, do_ref, small_ref, acc):
    step = pl.program_id(0)

    @pl.when(step == 0)
    def _():
        acc[...] = dh_ref[...]

    du = (dot_nt(dz_ref[...], wo_ref[...]) * gp_ref[...].astype(F32)).astype(LOW)
    grad_ref[0] = dot(yt_ref[...], du).astype(LOW)
    bias_ref[...] = column_total(du.astype(F32))
    acc[...] += dot_nt(du, wi_ref[...])

    @pl.when(step == pl.num_programs(0) - 1)
    def _():
        hat = hat_ref[...]
        dy = acc[...]
        dh = normal_back(hat, scale_ref[:, 0:1], dy * ga_ref[...].astype(F32))
        dsum_ref[...] = dh
        da = dh.astype(LOW)
        da_ref[...] = da
        do_ref[...] = dot_nt(da, wa_ref[...]).astype(LOW)
        small_ref[...] = jnp.zeros(small_ref.shape, F32)
        small_ref[0:1, :] = column_total(dy * hat)
        small_ref[1:2, :] = column_total(dy)
        small_ref[2:3, :] = column_total(da.astype(F32))


def inner_grads(dz, gp, yt, wo, wi, dh, hat, scale, ga, wa, block):
    tokens, dim = dz.shape
    wide = wi.shape[1]
    count = wide // block
    whole = lambda a: pl.BlockSpec(a.shape, lambda i: (0,) * a.ndim)
    ins = (dz, gp, yt, wo, wi, dh, hat, scale, ga.reshape(1, -1), wa)
    specs = [whole(a) for a in ins]
    specs[1] = pl.BlockSpec((tokens, block), lambda i: (0, i))
    specs[3] = pl.BlockSpec((block, dim), lambda i: (i, 0))
    specs[4] = pl.BlockSpec((dim, block), lambda i: (0, i))
    outs = [
        ((count, dim, block), LOW, (1, dim, block), lambda i: (i, 0, 0)),
        ((1, wide), F32, (1, block), lambda i: (0, i)),
        ((tokens, dim), F32, None, None),
        ((tokens, dim), LOW, None, None),
        ((tokens, dim), LOW, None, None),
        ((8, dim), F32, None, None),
    ]
    return pl.pallas_call(
        inner_kernel,
        grid=(count,),
        in_specs=specs,
        out_specs=[pl.BlockSpec(b or s, m or (lambda i: (0, 0))) for s, _, b, m in outs],
        out_shape=[jax.ShapeDtypeStruct(s, t) for s, t, _, _ in outs],
        scratch_shapes=[pltpu.VMEM((tokens, dim), F32)],
        compiler_params=pltpu.CompilerParams(vmem_limit_bytes=VMEM),
        cost_estimate=pl.CostEstimate(flops=6 * tokens * dim * wide + 2 * tokens * dim * dim, bytes_accessed=6 * dim * wide + 2 * tokens * wide + 24 * tokens * dim, transcendentals=0),
        name="inner_grads",
    )(*ins)


def swap(values, name, mask):
    size = lax.axis_size(name)
    return lax.ppermute(values, name, [(i, i ^ mask) for i in range(size)])


def bit_masks(size):
    return [1 << b for b in range(size.bit_length() - 1)]


def total_of(parts, index, axis):
    picked = [lax.dynamic_slice_in_dim(p, index, 1, axis) for p in parts]
    return sum(p.astype(F32) for p in picked)


def halve(parts, name, mask, axis):
    bit = (lax.axis_index(name) // mask) % 2
    sent = total_of(parts, 1 - bit, axis).astype(LOW)
    got = swap(sent, name, mask)
    kept = [lax.dynamic_slice_in_dim(p, bit, 1, axis) for p in parts]
    return kept + [got]


def add_up(parts):
    return sum(p.astype(F32) for p in parts)


def both_sides(piece, name, mask, axis):
    got = swap(piece, name, mask)
    bit = (lax.axis_index(name) // mask) % 2
    first = jnp.where(bit == 0, piece, got)
    second = jnp.where(bit == 0, got, piece)
    return jnp.concatenate([first, second], axis=axis)


def split_bits(size):
    return (2,) * (size.bit_length() - 1)


def reduce_whole(grads, order, n_dp, n_seq):
    tail = grads.shape[2:]
    dp_bits, seq_bits = len(split_bits(n_dp)), len(split_bits(n_seq))
    parts = [grads.reshape(split_bits(n_dp) + split_bits(n_seq) + tail)]
    done = []
    for name, mask in order:
        bit = mask.bit_length() - 1
        axis = dp_bits - 1 - bit if name == "dp" else dp_bits + seq_bits - 1 - bit
        parts = halve(parts, name, mask, axis)
        if name == "seq":
            done.append((mask, axis))
    piece = add_up(parts).astype(LOW)
    for mask, axis in sorted(done, reverse=True):
        piece = both_sides(piece, "seq", mask, axis)
    return piece.reshape((piece.size // (tail[0] * tail[1]),) + tail)


def body(hidden_in, passage_lengths, w_qkv, b_query, b_value, w_attn_out, b_attn_out, gain_attn,
         bias_attn, w_inner, b_inner, w_outer, b_outer, gain_ffn, bias_ffn, grad_out):
    rows, chunk, dim = hidden_in.shape
    n_dp, n_seq = lax.axis_size("dp"), lax.axis_size("seq")
    wide = w_inner.shape[1]
    slots = passage_lengths.shape[1]
    group = n_seq // rows
    seq = lax.axis_index("seq")
    side, member = seq // group, seq % group
    mine = rows * chunk
    tokens = group * mine
    heads = HEADS // group
    cols = heads * HEAD_DIM
    pairs = (heads + 1) // 2
    padded = pairs * LANES
    block = 256
    row_at = lambda a, d: lax.dynamic_index_in_dim(a, side ^ d, 0, keepdims=False)
    head_cols = lambda a, m, start, axis: lax.dynamic_slice_in_dim(a, start + m * cols, cols, axis)
    widen = lambda a: jnp.pad(a, ((0, 0),) * (a.ndim - 1) + ((0, padded - cols),)) if padded > cols else a

    hidden = jnp.concatenate(
        [row_at(hidden_in, 0)] + [swap(row_at(hidden_in, d), "seq", d * group) for d in range(1, rows)], axis=0
    )
    cotangent = jnp.concatenate(
        [row_at(grad_out, 0)] + [swap(row_at(grad_out, d), "seq", d * group) for d in range(1, rows)], axis=0
    )
    hidden_all = jnp.concatenate([hidden] + [swap(hidden, "seq", e) for e in range(1, group)], axis=0)
    start = jnp.concatenate(
        [((side ^ d) * group + (member ^ e)) * chunk + jnp.arange(chunk, dtype=jnp.int32)
         for e in range(group) for d in range(rows)]
    )
    ends = jnp.cumsum(row_at(passage_lengths, 0), dtype=jnp.int32)
    segs = jnp.sum((start[:, None] >= ends[None, :]).astype(jnp.int32), axis=1, dtype=jnp.int32)
    seg_col = jnp.broadcast_to(segs[:, None], (tokens, LANES))
    seg_row = jnp.broadcast_to(segs[None, :], (8, tokens))
    per_block = segs.reshape(tokens // block, block)
    low_seg, high_seg = jnp.min(per_block, axis=1), jnp.max(per_block, axis=1)
    need = (
        jnp.maximum(low_seg[:, None], low_seg[None, :]) <= jnp.minimum(high_seg[:, None], high_seg[None, :])
    ).astype(jnp.int32).reshape(-1)

    scale = HEAD_DIM ** (-0.5)
    three = lambda m: [head_cols(w_qkv, m, i * dim, 1) for i in range(3)]
    w_q, w_k, w_v = three(member)
    w_local = jnp.concatenate([widen(w_q * scale), widen(w_k), widen(w_v)], axis=1)
    b_local = jnp.concatenate(
        [widen(head_cols(b_query, member, 0, 0) * scale), jnp.zeros((padded,), LOW), widen(head_cols(b_value, member, 0, 0))]
    )
    packed = (dot(hidden_all, w_local) + b_local.astype(F32)).astype(LOW)
    o_local, o_turned, lse = attend(packed, seg_col, seg_row, need, pairs, block)

    def to_columns(parts):
        whole = jnp.zeros((mine, dim), LOW)
        for e, part in enumerate(parts):
            whole = lax.dynamic_update_slice_in_dim(whole, part, (member ^ e) * cols, 1)
        return whole

    def by_member(local):
        split = local.reshape(group, mine, -1)
        return [split[0]] + [swap(split[e], "seq", e) for e in range(1, group)]

    o_full = to_columns([p[:, :cols] for p in by_member(o_local)])
    seg_mine = seg_row[:, :mine]
    (g_low, g_slope, y1_low, y1_turned, hat, hat_scale, out_mine, dh2, dz, dz_turned, small_two, pool) = feed(
        hidden, o_full, w_attn_out, b_attn_out, gain_attn, bias_attn, w_inner, b_inner, w_outer,
        b_outer, gain_ffn, bias_ffn, cotangent, seg_mine, slots, 768)

    for e in bit_masks(group):
        pool = pool + swap(pool, "seq", e)
    pool = pool.astype(LOW)

    def place(own, others):
        stack = jnp.zeros((rows,) + own.shape, F32)
        stack = lax.dynamic_update_index_in_dim(stack, own.astype(F32), side, 0)
        for d, other in enumerate(others, 1):
            stack = lax.dynamic_update_index_in_dim(stack, other.astype(F32), side ^ d, 0)
        return stack

    out_got = [swap(jnp.concatenate([out_mine[d * chunk:(d + 1) * chunk].astype(LOW), pool]), "seq", d * group)
               for d in range(1, rows)]
    out = place(out_mine[:chunk], [a[:chunk] for a in out_got])
    sums = place(pool, [a[chunk:] for a in out_got])
    pooled = sums / jnp.maximum(passage_lengths.astype(F32), 1.0)[:, :, None]

    seq_masks, dp_masks = bit_masks(n_seq), bit_masks(n_dp)
    member_masks = [("seq", m) for m in seq_masks if m < group]
    side_masks = [("seq", m) for m in seq_masks if m >= group]
    dp_stages = [("dp", m) for m in dp_masks]

    grad_outer = outer_grads(dz_turned, g_low, 384)
    outer_parts = grad_outer.reshape(grad_outer.shape[0], dim, -1)
    if outer_parts.shape[0] != n_dp:
        outer_parts = outer_parts.transpose(0, 2, 1).reshape(n_dp, wide // n_dp, dim).transpose(0, 2, 1)
    sum_outer = reduce_whole(
        outer_parts.reshape(n_dp, n_seq, dim // n_seq, wide // n_dp),
        member_masks + dp_stages[1:2] + dp_stages[:1] + side_masks + dp_stages[2:], n_dp, n_seq)
    grad_w_outer = sum_outer.reshape(dim, wide // n_dp).T.astype(F32)

    grad_inner, bias_inner, dh1, da, do_full, small_one = inner_grads(
        dz, g_slope, y1_turned, w_outer, w_inner, dh2, hat, hat_scale, gain_attn, w_attn_out, 768)
    if grad_inner.shape[0] != n_seq:
        grad_inner = grad_inner.transpose(1, 0, 2).reshape(dim, n_seq, wide // n_seq).transpose(1, 0, 2)
    inner_parts = grad_inner.reshape(n_seq, n_dp, dim // n_dp, wide // n_seq).transpose(1, 0, 2, 3)
    sum_inner = reduce_whole(inner_parts, member_masks + dp_stages[:1] + side_masks + dp_stages[1:], n_dp, n_seq)
    grad_w_inner = sum_inner.transpose(1, 0, 2).reshape(dim // n_dp, wide).astype(F32)

    do_parts = [head_cols(do_full, member ^ e, 0, 1) for e in range(group)]
    do_local = jnp.concatenate([do_parts[0]] + [swap(do_parts[e], "seq", e) for e in range(1, group)], axis=0)

    grad_attn_out = dot_tn(o_full, da).astype(LOW)
    sizes = [wide] + [dim] * 6
    vectors = jnp.concatenate(
        [v.reshape(n_dp, -1) for v in (bias_inner, small_two[0], small_two[1], small_two[2], small_one[0], small_one[1], small_one[2])],
        axis=1)
    unit = dim // n_seq
    lines = -(-vectors.shape[1] // dim)
    vectors = jnp.pad(vectors, ((0, 0), (0, lines * dim - vectors.shape[1])))
    vectors = vectors.reshape(n_dp, lines, n_seq, unit).transpose(0, 2, 1, 3).astype(LOW)
    share = dim // n_dp
    attn_parts = grad_attn_out.reshape(n_dp, share, n_seq, unit).transpose(0, 2, 1, 3)
    fill = jnp.zeros((n_dp, n_seq, -lines % 8, unit), LOW)
    sum_attn = reduce_whole(
        jnp.concatenate([attn_parts, vectors, fill], axis=2),
        member_masks + side_masks + dp_stages, n_dp, n_seq)
    grad_w_attn_out = sum_attn[:, :share].transpose(1, 0, 2).reshape(share, dim).astype(F32)
    flat = sum_attn[:, share:share + lines].transpose(1, 0, 2).reshape(-1).astype(F32)
    pieces, at = [], 0
    for size in sizes:
        pieces.append(flat[at:at + size // n_dp])
        at += size // n_dp
    (grad_b_inner, grad_gain_ffn, grad_bias_ffn, grad_b_outer, grad_gain_attn, grad_bias_attn, grad_b_attn_out) = pieces

    d_query, d_key, d_value = attend_back(
        packed, widen(do_local), o_turned, lse, seg_col, seg_row, need, pairs, block)
    d_local = jnp.concatenate([a[:, :cols] for a in (d_query, d_key, d_value)], axis=1)
    grad_qkv = dot_tn(hidden_all, d_local).astype(LOW)

    def spread_bias(values):
        local = jnp.sum(values[:, :cols].astype(F32), axis=0)
        return lax.dynamic_update_slice_in_dim(jnp.zeros((dim,), F32), local, member * cols, 0)

    biases = jnp.concatenate(
        [spread_bias(d_query).reshape(n_dp, share), spread_bias(d_value).reshape(n_dp, share)], axis=1).astype(LOW)
    part = share // rows
    extra = LANES
    need_rows = -(-biases.shape[1] // extra)
    biases = jnp.pad(biases, ((0, 0), (0, rows * part * extra - biases.shape[1]))).reshape(n_dp, rows, part, extra)
    qkv_parts = jnp.concatenate([grad_qkv.reshape(n_dp, rows, part, 3 * cols), biases], axis=3)

    def reduce_group(grads, order):
        tail = grads.shape[2:]
        dp_bits, side_bits = len(split_bits(n_dp)), len(split_bits(rows))
        parts = [grads.reshape(split_bits(n_dp) + split_bits(rows) + tail)]
        done = []
        for name, mask in order:
            bit = mask.bit_length() - 1
            if name == "dp":
                axis = dp_bits - 1 - bit
            else:
                axis = dp_bits + side_bits - 1 - (bit - group.bit_length() + 1)
                done.append((mask, axis))
            parts = halve(parts, name, mask, axis)
        piece = add_up(parts).astype(LOW)
        for mask, axis in sorted(done, reverse=True):
            piece = both_sides(piece, "seq", mask, axis)
        return piece.reshape((rows,) + tail)

    sum_qkv = reduce_group(qkv_parts, dp_stages[:1] + side_masks + dp_stages[1:]).reshape(share, 3 * cols + extra)
    everyone = [sum_qkv] + [swap(sum_qkv, "seq", e) for e in range(1, group)]
    grad_w_qkv = jnp.zeros((share, 3 * dim), F32)
    bias_sum = 0.0
    ordered = jnp.zeros((group,) + sum_qkv.shape, LOW)
    for e, got in enumerate(everyone):
        ordered = lax.dynamic_update_index_in_dim(ordered, got, member ^ e, 0)
    ordered = ordered.astype(F32)
    grad_w_qkv = jnp.concatenate(
        [ordered[m, :, i * cols:(i + 1) * cols] for i in range(3) for m in range(group)], axis=1)
    bias_sum = sum(ordered[m, :, 3 * cols:] for m in range(group)).reshape(-1)
    grad_b_query, grad_b_value = bias_sum[:share], bias_sum[share:2 * share]

    d_parts = d_local.reshape(group, mine, 3 * cols)
    d_mine = [d_parts[0]] + [swap(d_parts[e], "seq", e) for e in range(1, group)]
    grad_hidden = dh1
    for e, part_e in enumerate(d_mine):
        w_e = jnp.concatenate(three(member ^ e), axis=1)
        grad_hidden = grad_hidden + dot_nt(part_e, w_e)
    in_got = [swap(grad_hidden[d * chunk:(d + 1) * chunk].astype(LOW), "seq", d * group) for d in range(1, rows)]
    grad_in = place(grad_hidden[:chunk], in_got)

    return (out, pooled, grad_in, grad_w_qkv, grad_b_query, grad_b_value, grad_w_attn_out,
            grad_b_attn_out, grad_gain_attn, grad_bias_attn, grad_w_inner, grad_b_inner,
            grad_w_outer, grad_b_outer, grad_gain_ffn, grad_bias_ffn)


def solution(mesh):
    tokens, rows, whole = P("dp", "seq", None), P("dp", None), P()
    vector, cube = P("dp"), P("dp", None, None)
    return jax.shard_map(
        body,
        mesh=mesh,
        in_specs=(tokens, rows) + (whole,) * 13 + (tokens,),
        out_specs=(tokens, cube, tokens, rows, vector, vector, rows, vector, vector, vector, rows,
                   vector, rows, vector, vector, vector),
        check_vma=False,
    )
```

```python
import functools
import math

import jax
import jax.numpy as jnp
from jax import lax
from jax.experimental import pallas as pl
from jax.experimental.pallas import tpu as pltpu
from jax.sharding import PartitionSpec as P

LOW = jnp.bfloat16
F32 = jnp.float32
HEADS = 12
HEAD_DIM = 64
LANES = 128
MIB = 1024 * 1024
MASKED = -1e30
EPS = 1e-12
COST = 1000
SLOTS = 8
HALF_ROOT = math.sqrt(0.5)
PHI_SCALE = 1.0 / math.sqrt(2.0 * math.pi)


def dot(left, right):
    return jnp.dot(left, right, preferred_element_type=F32)


def dot_nt(left, right):
    return lax.dot_general(left, right, (((1,), (1,)), ((), ())), preferred_element_type=F32)


def dot_tn(left, right):
    return lax.dot_general(left, right, (((0,), (0,)), ((), ())), preferred_element_type=F32)


def head_lanes(rows, head):
    lane = lax.broadcasted_iota(jnp.int32, (rows, LANES), 1)
    return (lane >= HEAD_DIM) if head else (lane < HEAD_DIM)


def spread(column, width):
    return jnp.concatenate([column] * (width // LANES), axis=1)


def segments(plan, shape, axis, start=0):
    place = lax.broadcasted_iota(jnp.int32, shape, axis) + start
    return sum((place >= plan[j]).astype(jnp.int32) for j in range(SLOTS))


def whole(array, buffers=1):
    return pl.BlockSpec(array.shape, lambda *_: (0,) * array.ndim, pipeline_mode=pl.Buffered(buffers))


def kernel_call(body, name, grid, ins, in_specs, outs, scratch, flops, moved, exps=0, prefetch=(), limit=24):
    spec = pltpu.PrefetchScalarGridSpec(
        num_scalar_prefetch=len(prefetch),
        grid=grid,
        in_specs=in_specs,
        out_specs=[
            pl.BlockSpec(b, m) if b else pl.BlockSpec(s, lambda *_, n=len(s): (0,) * n, pipeline_mode=pl.Buffered(1))
            for s, _, b, m in outs
        ],
        scratch_shapes=scratch,
    )
    return pl.pallas_call(
        body,
        grid_spec=spec,
        out_shape=[jax.ShapeDtypeStruct(s, t) for s, t, _, _ in outs],
        compiler_params=pltpu.CompilerParams(vmem_limit_bytes=limit * MIB),
        cost_estimate=pl.CostEstimate(flops=int(flops) // COST, bytes_accessed=int(moved) // COST, transcendentals=int(exps) // COST),
        name=name,
    )(*prefetch, *ins)


def key_spans(count):
    return list(range(1, count + 1)) if count <= 4 else [n for n in (1, 2, 4, 8, 16) if n <= count]


def turn(block):
    return block.T.astype(LOW)


def attend_kernel(plan, *refs, block, count, near):
    chunks, refs = refs[:count], refs[count:]
    (wq_ref, wk_ref, wv_ref, vec_ref,
     om_ref, os_ref, q_ref, k_ref, v_ref, ot_ref, lse_ref, qt, vt, km, segk_ref, segq_ref) = refs

    @pl.when(pl.program_id(0) == 0)
    def _():
        segk_ref[...] = segments(plan, segk_ref.shape, 0)
        segq_ref[...] = segments(plan, segq_ref.shape, 1)

    w = jnp.concatenate([wq_ref[...], wk_ref[...], wv_ref[...]], axis=1)
    bias_q, bias_v = vec_ref[6:7, :], vec_ref[7:8, :]
    for i in range(count):
        at = pl.ds(pl.multiple_of(plan[SLOTS + i] * block, block), block)
        made = dot(chunks[i][...], w)
        q = (made[:, :LANES] + bias_q).astype(LOW).astype(F32) * HEAD_DIM ** (-0.5)
        k = made[:, LANES:2 * LANES].astype(LOW)
        v = made[:, 2 * LANES:] + bias_v
        q_ref[at, :] = q.astype(LOW)
        k_ref[at, :] = k
        v_ref[at, :] = v.astype(LOW)
        qt[:, at] = turn(q)
        vt[:, at] = turn(v)
        for h in range(2):
            km[h, at, :] = jnp.where(head_lanes(block, h), k, jnp.zeros((), LOW))

    def one_block(j, o_ref, row):
        cols = pl.ds(pl.multiple_of(plan[SLOTS + j] * block, block), block)
        for span in key_spans(count):
            @pl.when(plan[SLOTS + 2 * count + j] == span)
            def _():
                rows = pl.ds(pl.multiple_of(plan[SLOTS + count + j] * block, block), span * block)
                same = spread(segk_ref[rows, :], block) == segq_ref[0:1, cols]
                qtb = qt[:, cols]
                made = []
                for h in range(2):
                    s = jnp.where(same, dot(km[h, rows, :], qtb), MASKED)
                    top = jnp.max(s, axis=0, keepdims=True)
                    p = jnp.exp(s - top)
                    total = jnp.sum(p, axis=0, keepdims=True)
                    half = slice(h * HEAD_DIM, (h + 1) * HEAD_DIM)
                    made.append(dot(vt[half, rows], p.astype(LOW)) * (1.0 / total))
                    lse_ref[0, h:h + 1, cols] = top + jnp.log(total)
                both = jnp.concatenate(made, axis=0)
                ot_ref[:, cols] = both.astype(LOW)
                o_ref[pl.ds(pl.multiple_of(row * block, block), block), :] = turn(both)

    def near_block(j, carry):
        one_block(j, om_ref, j)
        return carry

    def far_block(j, carry):
        one_block(j, os_ref, j - near)
        return carry

    lax.fori_loop(0, near, near_block, 0)
    lax.fori_loop(near, count, far_block, 0)


def attend(plan, chunks, weights, vec, pairs, near):
    block = chunks[0].shape[0]
    count = len(chunks)
    tokens = block * count
    width = pairs * LANES
    pair = lambda j, n: (0, j)
    flat = (tokens, width)
    arrays, maps = weights
    return kernel_call(
        functools.partial(attend_kernel, block=block, count=count, near=near),
        "attend", (pairs,),
        (*chunks, *arrays, vec),
        [whole(c) for c in chunks] + [pl.BlockSpec((arrays[0].shape[0], LANES), m) for m in maps[:3]]
        + [pl.BlockSpec((vec.shape[0], LANES), maps[3])],
        [
            ((near * block, width), LOW, (near * block, LANES), pair),
            ((tokens - near * block, width), LOW, (tokens - near * block, LANES), pair),
            (flat, LOW, (tokens, LANES), pair),
            (flat, LOW, (tokens, LANES), pair),
            (flat, LOW, (tokens, LANES), pair),
            ((width, tokens), LOW, (LANES, tokens), lambda j, n: (j, 0)),
            ((pairs, 8, tokens), F32, (1, 8, tokens), lambda j, n: (j, 0, 0)),
        ],
        [pltpu.VMEM((LANES, tokens), LOW), pltpu.VMEM((LANES, tokens), LOW), pltpu.VMEM((2, tokens, LANES), LOW),
         pltpu.VMEM((tokens, LANES), jnp.int32), pltpu.VMEM((8, tokens), jnp.int32)],
        4 * tokens * tokens * width, 20 * tokens * width, 2 * tokens * tokens * pairs, (plan,), 14)


def attend_back_kernel(plan, *refs, block, count, near):
    chunks, refs = refs[:count], refs[count:]
    (q_ref, k_ref, v_ref, dm_ref, do_ref, ot_ref, lse_ref,
     gm_ref, go_ref, gw_ref, small_ref,
     qt, dt, kt, km, vm, qm, dom, cen, dq, dk, dv, segk_ref, segq_ref) = refs

    @pl.when(pl.program_id(0) == 0)
    def _():
        segk_ref[...] = segments(plan, segk_ref.shape, 0)
        segq_ref[...] = segments(plan, segq_ref.shape, 1)

    zero = jnp.zeros((), LOW)
    for i in range(count):
        at = pl.ds(pl.multiple_of(plan[SLOTS + i] * block, block), block)
        given = dm_ref[i * block:(i + 1) * block, :] if i < near else do_ref[(i - near) * block:(i - near + 1) * block, :]
        turned = given.astype(F32).T
        dt[:, at] = turned.astype(LOW)
        both = turned * ot_ref[:, at].astype(F32)
        cen[0:1, at] = jnp.sum(both[0:HEAD_DIM, :], axis=0, keepdims=True)
        cen[1:2, at] = jnp.sum(both[HEAD_DIM:, :], axis=0, keepdims=True)
        fixed = slice(i * block, (i + 1) * block)
        q, k, v = q_ref[fixed, :], k_ref[fixed, :], v_ref[fixed, :]
        qt[:, fixed] = turn(q.astype(F32))
        kt[:, fixed] = turn(k.astype(F32))
        for h in range(2):
            lanes = head_lanes(block, h)
            km[h, fixed, :] = jnp.where(lanes, k, zero)
            vm[h, fixed, :] = jnp.where(lanes, v, zero)
            qm[h, fixed, :] = jnp.where(lanes, q, zero)
            dom[h, at, :] = jnp.where(lanes, given, zero)
    dk[...] = jnp.zeros(dk.shape, F32)
    dv[...] = jnp.zeros(dv.shape, F32)

    def one_block(j, carry):
        cols = pl.ds(pl.multiple_of(j * block, block), block)
        for span in key_spans(count):
            @pl.when(plan[SLOTS + 4 * count + j] == span)
            def _():
                rows = pl.ds(pl.multiple_of(plan[SLOTS + 3 * count + j] * block, block), span * block)
                same = spread(segk_ref[rows, :], block) == segq_ref[0:1, cols]
                qtb, dtb = qt[:, cols], dt[:, cols]
                dk_add, dv_add, made = 0.0, 0.0, []
                for h in range(2):
                    half = slice(h * HEAD_DIM, (h + 1) * HEAD_DIM)
                    s = jnp.where(same, dot(km[h, rows, :], qtb), MASKED)
                    p = jnp.exp(s - lse_ref[0, h:h + 1, cols])
                    ds = (p * (dot(vm[h, rows, :], dtb) - cen[h:h + 1, cols])).astype(LOW)
                    dv_add += dot(p.astype(LOW), dom[h, cols, :])
                    dk_add += dot(ds, qm[h, cols, :])
                    made.append(dot(kt[half, rows], ds))
                dv[rows, :] += dv_add
                dk[rows, :] += dk_add
                dq[cols, :] = jnp.concatenate(made, axis=0).T * HEAD_DIM ** (-0.5)
        return carry

    lax.fori_loop(0, count, one_block, 0)
    small_ref[...] = jnp.zeros(small_ref.shape, F32)
    grads = 0.0
    for i in range(count):
        at = pl.ds(pl.multiple_of(plan[SLOTS + i] * block, block), block)
        parts = [a[at, :].astype(LOW) for a in (dq, dk, dv)]
        joined = jnp.concatenate(parts, axis=1)
        small_ref[0:1, :] += jnp.sum(parts[0].astype(F32), axis=0, keepdims=True)
        small_ref[1:2, :] += jnp.sum(parts[2].astype(F32), axis=0, keepdims=True)
        if i < near:
            gm_ref[i * block:(i + 1) * block, :] = joined
        else:
            go_ref[(i - near) * block:(i - near + 1) * block, :] = joined
        grads += dot_tn(chunks[i][...], joined)
    gw_ref[...] = grads.astype(LOW)


def attend_back(plan, chunks, q, k, v, d_mine, d_others, ot, lse, pairs, near, base):
    block = chunks[0].shape[0]
    count = len(chunks)
    tokens = block * count
    width = pairs * LANES
    dim = chunks[0].shape[1]
    pair = lambda j, n: (0, j)
    from_base = lambda j, n: (0, base + j)
    low = lambda *s: pltpu.VMEM(s, LOW)
    return kernel_call(
        functools.partial(attend_back_kernel, block=block, count=count, near=near),
        "attend_back", (pairs,),
        (*chunks, q, k, v, d_mine, d_others, ot, lse),
        [whole(c) for c in chunks] + [pl.BlockSpec((tokens, LANES), from_base)] * 3
        + [pl.BlockSpec((d_mine.shape[0], LANES), from_base), pl.BlockSpec((d_others.shape[0], LANES), from_base),
           pl.BlockSpec((LANES, tokens), lambda j, n: (base + j, 0)),
           pl.BlockSpec((1, 8, tokens), lambda j, n: (base + j, 0, 0))],
        [
            ((d_mine.shape[0], 3 * width), LOW, (d_mine.shape[0], 3 * LANES), pair),
            ((d_others.shape[0], 3 * width), LOW, (d_others.shape[0], 3 * LANES), pair),
            ((dim, 3 * width), LOW, (dim, 3 * LANES), pair),
            ((8, width), F32, (8, LANES), pair),
        ],
        [low(LANES, tokens), low(LANES, tokens), low(LANES, tokens), low(2, tokens, LANES), low(2, tokens, LANES),
         low(2, tokens, LANES), low(2, tokens, LANES), pltpu.VMEM((8, tokens), F32),
         pltpu.VMEM((tokens, LANES), F32), pltpu.VMEM((tokens, LANES), F32), pltpu.VMEM((tokens, LANES), F32),
         pltpu.VMEM((tokens, LANES), jnp.int32), pltpu.VMEM((8, tokens), jnp.int32)],
        10 * tokens * tokens * width, 30 * tokens * width, 2 * tokens * tokens * pairs, (plan,), 20)


def input_kernel(plan, *refs, group, runs, pairs, first):
    n = group * len(runs)
    d_refs, (w_ref, dh_ref, own_ref, sent_ref) = refs[:n], refs[n:]
    dim = w_ref.shape[0]
    total = dh_ref[...]
    for e in range(group):
        base = plan[first + e] * pairs
        for r, (begin, size) in enumerate(runs):
            d_ref = d_refs[e * len(runs) + r]
            for j in range(size):
                at = [(base + begin + j) * LANES + i * dim for i in range(3)]
                w = jnp.concatenate([w_ref[:, pl.ds(pl.multiple_of(a, LANES), LANES)] for a in at], axis=1)
                total += dot_nt(d_ref[:, j * 3 * LANES:(j + 1) * 3 * LANES], w)
    chunk = own_ref.shape[0]
    own_ref[...] = total[:chunk]
    sent_ref[...] = total[chunk:].astype(LOW)


def input_grads(plan, d_parts, runs, w, dh, pairs, chunk, first):
    tokens, dim = dh.shape
    ins = (*[d for parts in d_parts for d in parts], w, dh)
    return kernel_call(
        functools.partial(input_kernel, group=len(d_parts), runs=runs, pairs=pairs, first=first), "input_grads", (1,), ins,
        [whole(a) for a in ins],
        [((chunk, dim), F32, None, None), ((tokens - chunk, dim), LOW, None, None)],
        [], 6 * tokens * dim * dim, 6 * dim * dim + 10 * tokens * dim, 0, (plan,), 24)


def row_mean(values):
    return jnp.mean(values, axis=-1, keepdims=True)


def normal(values):
    centre = values - row_mean(values)
    scale = lax.rsqrt(row_mean(centre * centre) + EPS)
    return centre * scale, scale


def normal_back(hat, scale, grads):
    return scale * (grads - row_mean(grads) - hat * row_mean(grads * hat))


def head_rows(ref, owner, cols):
    return ref[pl.ds(pl.multiple_of(owner * cols, 16), cols), :]


def token_kernel(plan, *refs, group, cols, chunk, first_bias, first, count, fine):
    x_refs, o_refs, refs = refs[:2], refs[2:2 + group], refs[2 + group:]
    wa_ref, vec_ref, wi_ref, wo_ref, go_ref, gg_ref, own_ref, sent_ref, dh_ref = refs[:9]
    do_refs, refs = refs[9:9 + group], refs[9 + group:]
    if fine:
        dest, refs = [refs[3 * e:3 * e + 3] for e in range(group)], refs[3 * group:]
    else:
        (outer_ref, inner_ref, attn_ref, vector_ref), refs = refs[:4], refs[4:]
    yl, acc, g, slope, hat1, scale1, dz, attn, vectors = refs
    step = pl.program_id(0)
    tokens, dim = acc.shape
    total = lambda values: jnp.sum(values, axis=0, keepdims=True)

    def put(refs, d, r, rows, first_col, values):
        third, end = refs[0].shape[3], first_col + values.shape[1]
        for i, ref in enumerate(refs):
            low, high = max(first_col, i * third), min(end, (i + 1) * third)
            if low < high:
                ref[d, r, rows, low - i * third:high - i * third] = values[:, low - first_col:high - first_col]

    @pl.when(step == 0)
    def _():
        x = jnp.concatenate([r[...] for r in x_refs], axis=0)
        h1 = x.astype(F32) + vec_ref[0:1, :]
        for e in range(group):
            h1 += dot(o_refs[e][:, :cols], head_rows(wa_ref, plan[first + e], cols))
        hat, scale = normal(h1)
        y1 = hat * vec_ref[1:2, :] + vec_ref[2:3, :]
        hat1[...] = hat
        scale1[...] = jnp.broadcast_to(scale, scale1.shape)
        yl[...] = y1.astype(LOW)
        acc[...] = y1 + vec_ref[3:4, :]
        vectors[...] = jnp.zeros(vectors.shape, F32)

    @pl.when(step < count)
    def _():
        u = dot(yl[...], wi_ref[...]) + vec_ref[pl.ds(first_bias + step, 1), :]
        cdf = 0.5 * (1.0 + lax.erf(u * HALF_ROOT))
        low = (u * cdf).astype(LOW)
        g[step] = low
        slope[step] = (cdf + u * (PHI_SCALE * jnp.exp(-0.5 * u * u))).astype(LOW)
        acc[...] += dot(low, wo_ref[...])

    @pl.when(step == count - 1)
    def _():
        hat, scale = normal(acc[...])
        gain = vec_ref[4:5, :]
        out = hat * gain + vec_ref[5:6, :]
        high = out.astype(LOW)
        own_ref[...] = out[:chunk]
        slots = sent_ref.shape[0] - (tokens - chunk)
        place = lax.broadcasted_iota(jnp.int32, (slots, tokens), 0)
        segs = jnp.concatenate(
            [segments(plan, (slots, chunk), 1, plan[SLOTS + i] * chunk) for i in range(tokens // chunk)], axis=1)
        onehot = (place == segs).astype(LOW)
        rest = (out - high.astype(F32)).astype(LOW)
        sent_ref[:tokens - chunk, :] = high[chunk:]
        sent_ref[tokens - chunk:, :] = (dot(onehot, high) + dot(onehot, rest)).astype(LOW)
        dy = jnp.concatenate([go_ref[0], gg_ref[...]], axis=0).astype(F32)
        dh = normal_back(hat, scale, dy * gain)
        low = dh.astype(LOW)
        dz[...] = low
        acc[...] = dh
        vectors[0:1, :] = total(dy * hat)
        vectors[1:2, :] = total(dy)
        vectors[2:3, :] = total(low.astype(F32))

    @pl.when(step >= count)
    def _():
        b = plan[first + group + 1 + step - count]
        du = (dot_nt(dz[...], wo_ref[...]) * slope[b].astype(F32)).astype(LOW)
        vectors[pl.ds(8 + b, 1), :] = total(du.astype(F32))
        inner = dot_tn(yl[...], du).astype(LOW)
        if fine:
            per, unit, width = count // group, dest[0][0].shape[2] - 32, dest[0][0].shape[3] * 3 // 2
            share = unit // 2
            for e in range(group):
                member_cols = pl.ds(pl.multiple_of(plan[first + e] * (dim // group), LANES), dim // group)
                outer = dot_tn(dz[:, member_cols], g[b]).astype(LOW)
                for i in range(dim // width):
                    for r in range(per):
                        put(dest[e], b * (dim // width) + i, r, slice(0, unit), 0,
                            outer[r * unit:(r + 1) * unit, i * width:(i + 1) * width])

                @pl.when((step - count) // per == group - 1 - e)
                def _():
                    r = lax.rem(step - count, per)
                    for d in range(dest[e][0].shape[0]):
                        for half in range(2):
                            put(dest[e], d, r, slice(half * share, (half + 1) * share), width,
                                inner[d * share:(d + 1) * share, half * width:(half + 1) * width])
        else:
            outer_ref[b] = dot_tn(dz[...], g[b]).astype(LOW)
            inner_ref[b] = inner
        acc[...] += dot_nt(du, wi_ref[...])

    @pl.when(step == pl.num_programs(0) - 1)
    def _():
        hat = hat1[...]
        dy = acc[...]
        dh = normal_back(hat, scale1[:, 0:1], dy * vec_ref[1:2, :])
        dh_ref[...] = dh
        da = dh.astype(LOW)
        for e in range(group):
            made = dot_nt(da, head_rows(wa_ref, plan[first + e], cols)).astype(LOW)
            if do_refs[e].shape[1] > cols:
                do_refs[e][...] = jnp.zeros(do_refs[e].shape, LOW)
            do_refs[e][:, :cols] = made
            attn[pl.ds(pl.multiple_of(plan[first + e] * cols, 8), cols), :] = dot_tn(o_refs[e][:, :cols], da)
        vectors[3:4, :] = total(dy * hat)
        vectors[4:5, :] = total(dy)
        vectors[5:6, :] = total(da.astype(F32))
        if fine:
            n_dp, sides, unit = dest[0][0].shape[0], dest[0][0].shape[1], dest[0][0].shape[2] - 32
            for e in range(group):
                for d in range(n_dp):
                    for r in range(sides):
                        at = d * (dim // n_dp) + plan[first + e] * (24 * sides) + r * 24
                        tail = vectors[8 * r:8 * r + 8, :] if e == 0 else jnp.zeros((8, dim), F32)
                        both = jnp.concatenate([attn[pl.ds(pl.multiple_of(at, 8), 24), :], tail], axis=0)
                        put(dest[e], d, r, slice(unit, unit + 32), 0, both.astype(LOW))
        else:
            attn_ref[...] = attn[...].astype(LOW)
            vector_ref[...] = vectors[...]


def token_work(plan, x_parts, o_parts, wa, vec, wi, wo, grad_out, grad_got, cols, padded, first_bias, first, n_dp, fine):
    chunk, dim = x_parts[0].shape
    tokens = 2 * chunk
    wide = wi.shape[1]
    block = dim
    count = wide // block
    group = len(o_parts)
    ins = (*x_parts, *o_parts, wa, vec, wi, wo, grad_out, grad_got)
    specs = [whole(a) for a in ins]
    which = lambda i, n: jnp.where(i < count, i, n[first + group + 1 + jnp.maximum(i - count, 0)])
    specs[-4] = pl.BlockSpec((dim, block), lambda i, n: (0, which(i, n)))
    specs[-3] = pl.BlockSpec((block, dim), lambda i, n: (which(i, n), 0))
    specs[-2] = pl.BlockSpec((1, chunk, dim), lambda i, n: (n[first + group], 0, 0))
    outs = [
        ((chunk, dim), F32, None, None),
        ((tokens - chunk + 16, dim), LOW, None, None),
        ((tokens, dim), F32, None, None),
    ] + [((tokens, padded), LOW, None, None)] * group
    if fine:
        outs += [((n_dp, 2, dim // group // 2 + 32, 2 * (wide // n_dp) // 3), LOW, None, None)] * (3 * group)
    else:
        outs += [((count, dim, block), LOW, None, None)] * 2 + [((dim, dim), LOW, None, None), ((16, dim), F32, None, None)]
    own = lambda *s: pltpu.VMEM(s, F32)
    low = lambda *s: pltpu.VMEM(s, LOW)
    return kernel_call(
        functools.partial(token_kernel, group=group, cols=cols, chunk=chunk, first_bias=first_bias, first=first, count=count, fine=fine),
        "token_work", (2 * count,), ins, specs, outs,
        [low(tokens, dim), own(tokens, dim), low(count, tokens, block), low(count, tokens, block), own(tokens, dim),
         own(tokens, LANES), low(tokens, dim), own(dim, dim), own(16, dim)],
        12 * tokens * dim * wide, 8 * dim * wide, 2 * tokens * wide, (plan,), 58)


def swap(values, name, mask):
    size = lax.axis_size(name)
    return lax.ppermute(values, name, [(i, i ^ mask) for i in range(size)])


def after(value, *first):
    return lax.optimization_barrier((value,) + first)[0]


def add_up(parts):
    return sum(p.astype(F32) for p in parts)


def split_bits(size):
    return (2,) * (size.bit_length() - 1)


class Cut:
    def __init__(self, array, kept=()):
        self.array, self.kept = array, dict(kept)

    def pick(self, axis, index):
        return Cut(self.array, {**self.kept, axis: index})

    def value(self):
        shape = [1 if d in self.kept else n for d, n in enumerate(self.array.shape)]
        return lax.dynamic_slice(self.array, [self.kept.get(d, 0) for d in range(len(shape))], shape)


class Halving:
    def __init__(self, parts, bits):
        self.parts = [[Cut(a) for a in (p if isinstance(p, list) else [p])] for p in parts]
        self.bits = bits
        self.sides = []

    def send(self, name, mask, *first):
        axis = self.bits[name, mask]
        bit = (lax.axis_index(name) // mask) % 2
        self.sent = self.join(self.parts, first, axis, 1 - bit)
        self.got = swap(self.sent, name, mask)
        self.parts = [[c.pick(axis, bit) for c in p] for p in self.parts] + [[Cut(self.got)]]
        if name == "seq":
            self.sides.append((mask, axis))

    def join(self, parts, first=(), axis=None, index=None):
        parts = [[c if axis is None else c.pick(axis, index) for c in p] for p in parts]
        if first:
            parts[0][0] = Cut(after(parts[0][0].array, *first), parts[0][0].kept)
        fine = max(parts, key=len)
        widths = [c.array.shape[-1] for c in fine]
        edges = [sum(widths[:i]) for i in range(len(widths) + 1)]

        def cut(p, i):
            at = 0
            for c in p:
                width = c.array.shape[-1]
                if at <= edges[i] and edges[i + 1] <= at + width:
                    value = c.value()
                    return value if width == widths[i] else value[..., edges[i] - at:edges[i + 1] - at]
                at += width
            raise ValueError(widths)

        sums = [add_up([cut(p, i) for p in parts]).astype(LOW) for i in range(len(widths))]
        return sums[0] if len(sums) == 1 else jnp.concatenate(sums, axis=-1)

    def finish(self, *first):
        return self.join(self.parts, first)

    def spread(self, piece):
        for mask, axis in reversed(self.sides):
            got = swap(piece, "seq", mask)
            bit = (lax.axis_index("seq") // mask) % 2
            piece = jnp.concatenate([jnp.where(bit == 0, piece, got), jnp.where(bit == 0, got, piece)], axis=axis)
        return piece


def abreast(*chains):
    both = Halving([[c.finish() for c in chains]], chains[0].bits)
    both.sides = list(chains[0].sides)
    return both


def finish_feed_kernel(plan, *refs, first, sources):
    pieces, (outer_ref, inner_ref, attn_ref, vec_ref, turned) = refs[:len(sources)], refs[len(sources):]
    width, dim = outer_ref.shape
    share = attn_ref.shape[0]
    unit = pieces[0].shape[0] - 32
    vec_ref[...] = jnp.zeros(vec_ref.shape, F32)
    for (e, d), ref in zip(sources, pieces):
        member, side = plan[first + e], lax.rem(plan[first + 2] + d, 2)
        owner = member * 2 + side
        turned[pl.ds(pl.multiple_of(owner * unit, 8), unit), :] = ref[:unit, :width].astype(F32)
        for half in range(2):
            inner_ref[:, pl.ds(pl.multiple_of(owner * 2 * width + half * width, LANES), width)] = (
                ref[half * share:(half + 1) * share, width:].astype(F32))
        attn_ref[pl.ds(pl.multiple_of(owner * 24, 8), 24), :] = ref[unit:unit + 24, :].astype(F32)
        vec_ref[pl.ds(pl.multiple_of(side * 8, 8), 8), :] += ref[unit:, :].astype(F32)[24:, :]
    outer_ref[...] = turned[...].T


def finish_feed(plan, pieces, sources, first, width, share, wide):
    dim = pieces[0].shape[1]
    return kernel_call(
        functools.partial(finish_feed_kernel, first=first, sources=sources), "finish_feed", (1,), tuple(pieces),
        [whole(a) for a in pieces],
        [((width, dim), F32, None, None), ((share, wide), F32, None, None), ((share, dim), F32, None, None), ((16, dim), F32, None, None)],
        [pltpu.VMEM((dim, width), F32)], 0, 10 * dim * width, 0, (plan,), 24)


def finish_rest_kernel(plan, *refs, first, sources, pairs):
    pieces, (out_ref, vec_ref) = refs[:len(sources)], refs[len(sources):]
    part = pieces[0].shape[0]
    dim = out_ref.shape[1] // 3
    vec_ref[...] = jnp.zeros(vec_ref.shape, F32)
    for (e, d), ref in zip(sources, pieces):
        member, side = plan[first + e], lax.rem(plan[first + 2] + d, 2)
        rows = pl.ds(pl.multiple_of(side * part, 8), part)
        for i in range(3):
            for j in range(pairs):
                at = pl.multiple_of(i * dim + (member * pairs + j) * LANES, LANES)
                out_ref[rows, pl.ds(at, LANES)] = ref[:, (3 * j + i) * LANES:(3 * j + i + 1) * LANES].astype(F32)
        vec_ref[rows, :] += ref[:, 3 * pairs * LANES:].astype(F32)


def finish_rest(plan, pieces, sources, first, pairs, share, dim):
    return kernel_call(
        functools.partial(finish_rest_kernel, first=first, sources=sources, pairs=pairs), "finish_rest", (1,), tuple(pieces),
        [whole(a) for a in pieces],
        [((share, 3 * dim), F32, None, None), ((share, LANES), F32, None, None)], [], 0, 10 * share * dim, 0, (plan,), 24)


def by_owner(parts, member):
    stack = jnp.stack(parts)
    return [lax.dynamic_index_in_dim(stack, member ^ m, 0, keepdims=False) for m in range(len(parts))]


def body(hidden_in, passage_lengths, w_qkv, b_query, b_value, w_attn_out, b_attn_out, gain_attn,
         bias_attn, w_inner, b_inner, w_outer, b_outer, gain_ffn, bias_ffn, grad_out):
    rows, chunk, dim = hidden_in.shape
    n_dp, n_seq = lax.axis_size("dp"), lax.axis_size("seq")
    wide = w_inner.shape[1]
    slots = passage_lengths.shape[1]
    assert slots == SLOTS
    group = n_seq // rows
    seq = lax.axis_index("seq")
    side, member = seq // group, seq % group
    tokens = group * rows * chunk
    cols = HEADS // group * HEAD_DIM
    pairs = -(-cols // LANES)
    padded = pairs * LANES
    aligned = cols % LANES == 0
    count = rows * group
    share = dim // n_dp
    row_at = lambda a, d: lax.dynamic_index_in_dim(a, side ^ d, 0, keepdims=False)

    send = row_at(hidden_in, 1)
    got = swap(send, "seq", group)
    own = row_at(hidden_in, 0)
    chunks = [own, got]
    for e in range(1, group):
        chunks += [swap(own, "seq", e), swap(got, "seq", e)]
    cot_send = after(row_at(grad_out, 1), got)
    cot_got = swap(cot_send, "seq", group)

    start = jnp.stack([(side ^ d) * group + (member ^ e) for e in range(group) for d in range(rows)]).astype(jnp.int32)
    ends = jnp.cumsum(row_at(passage_lengths, 0), dtype=jnp.int32)
    segment = lambda p: jnp.sum((p[..., None] >= ends).astype(jnp.int32), axis=-1, dtype=jnp.int32)
    index = jnp.arange(count, dtype=jnp.int32)
    low_seg, high_seg = segment(index * chunk), segment(index * chunk + (chunk - 1))
    meets = (jnp.maximum(low_seg[:, None], low_seg[None, :]) <= jnp.minimum(high_seg[:, None], high_seg[None, :]))
    first_key = jnp.min(jnp.where(meets, index[None, :], count), axis=1)
    spans = jnp.max(jnp.where(meets, index[None, :], -1), axis=1) + 1 - first_key
    rounded = functools.reduce(lambda r, n: jnp.where(spans <= n, n, r), reversed(key_spans(count)), count)
    first_key = jnp.minimum(first_key, count - rounded)
    reorder = lambda a: jnp.sum(jnp.where(start[:, None] == index[None, :], a[None, :], 0), axis=1)
    per = wide // dim // group
    turns = [(member ^ e) * per + r for e in reversed(range(group)) for r in range(per)]
    members = jnp.stack([member ^ e for e in range(group)] + [side] + turns)
    plan = jnp.concatenate([ends, start, reorder(first_key), reorder(rounded), first_key, rounded, members]).astype(jnp.int32)
    first = SLOTS + 5 * count
    first_bias = 8
    vec = jnp.concatenate(
        [b_attn_out, gain_attn, bias_attn, b_outer, gain_ffn, bias_ffn, b_query, b_value, b_inner]
    ).astype(F32).reshape(-1, dim)
    blocks = dim // LANES
    if aligned:
        weights = [w_qkv] * 3, [lambda j, n, i=i: (0, i * blocks + n[first] * pairs + j) for i in range(3)] + [
            lambda j, n: (0, n[first] * pairs + j)]
        vec_heads = vec
    else:
        widen = lambda a: jnp.pad(a, ((0, 0), (0, padded - cols)))
        weights_of = lambda m: [widen(lax.dynamic_slice_in_dim(w_qkv, m * cols + i * dim, cols, 1)) for i in range(3)]
        vec_heads = widen(lax.dynamic_slice_in_dim(vec, member * cols, cols, 1))
        weights = weights_of(member), [lambda j, n: (0, j)] * 4

    o_mine, o_send, q, k, v, o_turned, lse = attend(
        plan, chunks, weights, vec_heads, pairs, rows)
    apart = lambda a: [a] if group == 2 else [a[i * rows * chunk:(i + 1) * rows * chunk] for i in range(group - 1)]
    together = lambda a: a[0] if len(a) == 1 else jnp.concatenate(a, axis=0)
    o_parts = [o_mine] + [swap(a, "seq", e) for e, a in enumerate(apart(o_send), 1)]
    fine = aligned and (wide // n_dp) % LANES == 0 and share % 16 == 0 and per == rows and share == 24 * rows * group
    out_own, out_send, dh1, *made = token_work(
        plan, chunks[:rows], o_parts, w_attn_out, vec, w_inner, w_outer, grad_out, cot_got, cols, padded,
        first_bias, first, n_dp, fine)
    do_parts, made = made[:group], made[group:]
    do_gots = [swap(do_parts[e], "seq", e) for e in range(1, group)]
    out_got = swap(out_send, "seq", group)

    dp_masks = [1 << b for b in range(len(split_bits(n_dp)))]
    bit_shape = split_bits(n_dp) + split_bits(rows)
    bits = {("dp", m): len(dp_masks) - 1 - i for i, m in enumerate(dp_masks)}
    bits["seq", group] = len(dp_masks)

    unit, width = dim // group // rows, wide // n_dp
    if fine:
        feed_parts = made
    else:
        raw_outer, raw_inner, raw_attn, raw_vectors = made
        flat = lambda a: a.reshape(group, n_dp, rows, -1)
        feed_all = jnp.concatenate([
            flat(raw_outer.transpose(1, 0, 2).reshape(group, rows, unit, n_dp, width).transpose(0, 3, 1, 2, 4)),
            flat(raw_inner.transpose(1, 0, 2).reshape(n_dp, share, group, rows, -1).transpose(2, 0, 3, 1, 4)),
            flat(raw_attn.reshape(n_dp, group, rows, -1, dim).transpose(1, 0, 2, 3, 4))], axis=3)
        vectors = jnp.broadcast_to(raw_vectors.reshape(1, rows, -1), (n_dp, rows, 16 * dim // rows)).astype(LOW)
        feed_parts = [
            jnp.concatenate([lax.dynamic_index_in_dim(feed_all, member ^ e, 0, keepdims=False),
                             vectors if e == 0 else jnp.zeros_like(vectors)], axis=2).reshape(n_dp, rows, -1, LANES)
            for e in range(group)]
    ways = 3 if fine else 1
    shaped = lambda a: a.reshape(bit_shape + a.shape[2:])
    by_way = [[feed_parts[e * ways + i] for e in range(group)] for i in range(ways)]
    feeds = [Halving([shaped(p[0])] + [shaped(swap(p[e], "seq", e)) for e in range(1, group)], bits) for p in by_way]
    stages = [("dp", 1), ("seq", group), ("dp", 2)]

    def feed_stage(n, *before):
        for i, f in enumerate(feeds):
            f.send(*stages[(n + i) % 3], *before)
        return [f.sent for f in feeds]


    runs = [(0, pairs - 1), (pairs - 1, 1)]
    part = share // rows
    packed_grads = lambda a: a.reshape(bit_shape + (part, a.shape[-1]))
    do_in = together(do_gots)
    back = lambda do, run: attend_back(
        plan, chunks, q, k, v, do_parts[0], do, o_turned, lse, run[1], rows, run[0])
    d_mine_a, d_other_a, grad_qkv_a, small_a = back(do_in, runs[0])
    sent = feed_stage(0, grad_qkv_a, out_got)
    d_gots_a = [swap(a, "seq", e) for e, a in enumerate(apart(d_other_a), 1)]
    d_mine_b, d_other_b, grad_qkv_b, small_b = back(after(do_in, *sent), runs[1])
    d_gots_b = [swap(a, "seq", e) for e, a in enumerate(apart(d_other_b), 1)]

    small_qkv = jnp.concatenate([small_a, small_b], axis=1)
    heads = lax.dynamic_update_slice_in_dim(jnp.zeros((2, dim), F32), small_qkv[:2, :cols], member * cols, 1)
    vectors = heads.reshape(2, n_dp, -1).transpose(1, 0, 2)
    vectors = jnp.pad(vectors, ((0, 0), (0, rows * part - 2), (0, LANES - share))).astype(LOW).reshape(n_dp, rows, part, LANES)
    rest_a = Halving([packed_grads(grad_qkv_a)], bits)
    rest_b = Halving([[packed_grads(grad_qkv_b), vectors.reshape(bit_shape + vectors.shape[2:])]], bits)
    rest_a.send("dp", 1, grad_qkv_b)
    rest_b.send("seq", group, rest_a.sent)

    runs_of = [[d_mine_a, d_mine_b]] + [[a, b] for a, b in zip(d_gots_a, d_gots_b)]
    if aligned:
        in_own, in_send = input_grads(plan, runs_of, runs, w_qkv, after(dh1, rest_b.sent), pairs, chunk, first)
    else:
        grad_hidden = dh1
        for e, parts in enumerate(runs_of):
            w = weights_of(member ^ e)
            d = jnp.concatenate(parts, axis=1)
            for j in range(pairs):
                w_pair = jnp.concatenate([a[:, j * LANES:(j + 1) * LANES] for a in w], axis=1)
                grad_hidden = grad_hidden + dot_nt(d[:, j * 3 * LANES:(j + 1) * 3 * LANES], w_pair)
        in_own, in_send = grad_hidden[:chunk], grad_hidden[chunk:].astype(LOW)

    in_got = swap(in_send, "seq", group)
    sent = feed_stage(1, in_send)
    rest_b.send("dp", 1, *sent)
    rest_a.send("seq", group, rest_b.sent)
    sent = feed_stage(2, rest_a.sent)
    rest = abreast(rest_a, rest_b)
    rest.send("dp", 2, *sent)
    feed = abreast(*feeds) if ways > 1 else feeds[0]
    for mask in dp_masks[2:]:
        feed.send("dp", mask, rest.sent)
        rest.send("dp", mask, feed.sent)

    def everyone(piece):
        gots = [piece] + [swap(piece, "seq", e) for e in range(1, group)]
        return by_owner(gots, member)

    here = lambda a: lax.dynamic_slice_in_dim(a.reshape(-1), lax.axis_index("dp") * (a.size // n_dp), a.size // n_dp)
    feed_piece, rest_piece = feed.finish(rest.sent), rest.finish()
    if fine:
        sources = [(0, 0), (0, 1), (1, 0), (1, 1)]

        def from_all(piece):
            piece = piece.reshape(piece.shape[-2:])
            got = swap(piece, "seq", group)
            return [piece, got, swap(piece, "seq", 1), swap(got, "seq", 1)]

        grad_w_outer, grad_w_inner, grad_w_attn_out, totals = finish_feed(
            plan, from_all(feed_piece), sources, first, width, share, wide)
        grad_w_qkv, sums_qv = finish_rest(plan, from_all(rest_piece), sources, first, pairs, share, dim)
    else:
        feed_pieces = everyone(feed.spread(feed_piece))
        sizes = [unit * width, share * (wide // group // rows), share * dim // group // rows, 16 * dim // rows]
        ends_of = [sum(sizes[:i]) for i in range(5)]
        cut = lambda a, i: a.reshape(rows, -1)[:, ends_of[i]:ends_of[i + 1]]
        grad_w_outer = jnp.concatenate([cut(a, 0).reshape(rows * unit, width) for a in feed_pieces]).T.astype(F32)
        grad_w_inner = jnp.concatenate(
            [cut(a, 1).reshape(rows, share, -1)[r] for a in feed_pieces for r in range(rows)], axis=1).astype(F32)
        grad_w_attn_out = jnp.concatenate([cut(a, 2).reshape(-1, dim) for a in feed_pieces], axis=0).astype(F32)
        totals = add_up([cut(a, 3) for a in feed_pieces]).reshape(16, dim)
        rest_pieces = [a.reshape(share, -1) for a in everyone(rest.spread(rest_piece))]
        grad_w_qkv = jnp.concatenate(
            [jnp.concatenate([a[:, (3 * j + i) * LANES:(3 * j + i + 1) * LANES] for j in range(pairs)], axis=1)[:, :cols]
             for i in range(3) for a in rest_pieces], axis=1).astype(F32)
        sums_qv = add_up([a[:, 3 * padded:] for a in rest_pieces])
    (grad_gain_ffn, grad_bias_ffn, grad_b_outer, grad_gain_attn, grad_bias_attn, grad_b_attn_out) = [here(totals[i]) for i in range(6)]
    grad_b_inner = here(totals[8:8 + wide // dim])
    grad_b_query, grad_b_value = sums_qv[0, :share], sums_qv[1, :share]

    def in_place(own, got):
        return jnp.where(side == 0, jnp.stack([own, got]), jnp.stack([got, own]))

    out = in_place(after(out_own, rest_b.sent), out_got[:chunk].astype(F32))
    grad_in = in_place(after(in_own, rest.sent), in_got.astype(F32))
    sums = in_place(after(out_send, rest_b.sent)[chunk:chunk + slots], out_got[chunk:chunk + slots])
    sums = add_up([sums] + [swap(sums, "seq", e) for e in range(1, group)])
    pooled = sums / jnp.maximum(passage_lengths.astype(F32), 1.0)[:, :, None]

    return (out, pooled, grad_in, grad_w_qkv, grad_b_query, grad_b_value, grad_w_attn_out,
            grad_b_attn_out, grad_gain_attn, grad_bias_attn, grad_w_inner, grad_b_inner,
            grad_w_outer, grad_b_outer, grad_gain_ffn, grad_bias_ffn)


def solution(mesh):
    tokens, rows, all_of = P("dp", "seq", None), P("dp", None), P()
    vector, cube = P("dp"), P("dp", None, None)
    return jax.shard_map(
        body,
        mesh=mesh,
        in_specs=(tokens, rows) + (all_of,) * 13 + (tokens,),
        out_specs=(tokens, cube, tokens, rows, vector, vector, rows, vector, vector, vector, rows,
                   vector, rows, vector, vector, vector),
        check_vma=False,
    )
```

```python
import functools
import math

import jax
import jax.numpy as jnp
from jax import lax
from jax.experimental import pallas as pl
from jax.experimental.pallas import tpu as pltpu
from jax.sharding import PartitionSpec as P

LOW = jnp.bfloat16
F32 = jnp.float32
HEADS = 12
HEAD_DIM = 64
LANES = 128
MIB = 1024 * 1024
MASKED = -1e30
EPS = 1e-12
COST = 1000
SLOTS = 8
HALF_ROOT = math.sqrt(0.5)
PHI_SCALE = 1.0 / math.sqrt(2.0 * math.pi)


def dot(left, right):
    return jnp.dot(left, right, preferred_element_type=F32)


def dot_nt(left, right):
    return lax.dot_general(left, right, (((1,), (1,)), ((), ())), preferred_element_type=F32)


def dot_tn(left, right):
    return lax.dot_general(left, right, (((0,), (0,)), ((), ())), preferred_element_type=F32)


def head_lanes(shape, head):
    lane = lax.rem(lax.broadcasted_iota(jnp.int32, shape, 1), LANES)
    return (lane >= HEAD_DIM) if head else (lane < HEAD_DIM)


def spread(column, width):
    return jnp.concatenate([column] * (width // LANES), axis=1)


def segments(plan, shape, axis, start=0):
    place = lax.broadcasted_iota(jnp.int32, shape, axis) + start
    return sum((place >= plan[j]).astype(jnp.int32) for j in range(SLOTS))


def whole(array, buffers=1):
    return pl.BlockSpec(array.shape, lambda *_: (0,) * array.ndim, pipeline_mode=pl.Buffered(buffers))


def kernel_call(body, name, grid, ins, in_specs, outs, scratch, flops, moved, exps=0, prefetch=(), limit=24):
    spec = pltpu.PrefetchScalarGridSpec(
        num_scalar_prefetch=len(prefetch),
        grid=grid,
        in_specs=in_specs,
        out_specs=[
            pl.BlockSpec(memory_space=pltpu.HBM) if b == "hbm" else pl.BlockSpec(b, m) if b else pl.BlockSpec(s, lambda *_, n=len(s): (0,) * n, pipeline_mode=pl.Buffered(1))
            for s, _, b, m in outs
        ],
        scratch_shapes=scratch,
    )
    return pl.pallas_call(
        body,
        grid_spec=spec,
        out_shape=[jax.ShapeDtypeStruct(s, t) for s, t, _, _ in outs],
        compiler_params=pltpu.CompilerParams(vmem_limit_bytes=limit * MIB),
        cost_estimate=pl.CostEstimate(flops=int(flops) // COST, bytes_accessed=int(moved) // COST, transcendentals=int(exps) // COST),
        name=name,
    )(*prefetch, *ins)


def key_spans(count):
    return list(range(1, count + 1)) if count <= 4 else [n for n in (1, 2, 4, 8, 16) if n <= count]


def turn(block):
    return block.T.astype(LOW)


def in_place_of(ref, chunk):
    return pl.ds(pl.multiple_of(ref * chunk, chunk), chunk)


def attend_kernel(plan, *refs, block, count, near, pairs):
    chunks, refs = refs[:count], refs[count:]
    (wq_ref, wk_ref, wv_ref, vec_ref, om_ref, os_ref, lse_ref, q_out, k_out, v_out,
     q, k, v, qt, km, vm, segk_ref, segq_ref, sem) = refs
    width = pairs * LANES
    segk_ref[...] = segments(plan, segk_ref.shape, 0)
    segq_ref[...] = segments(plan, segq_ref.shape, 1)
    lse_ref[...] = jnp.zeros(lse_ref.shape, F32)
    w = jnp.concatenate([wq_ref[...], wk_ref[...], wv_ref[...]], axis=1)
    bias_q, bias_v = vec_ref[6:7, :], vec_ref[7:8, :]
    for i in range(count):
        at = in_place_of(plan[SLOTS + i], block)
        made = dot(chunks[i][...], w)
        q_low = (made[:, :width] + bias_q).astype(LOW).astype(F32) * HEAD_DIM ** (-0.5)
        k_low = made[:, width:2 * width].astype(LOW)
        v_low = (made[:, 2 * width:] + bias_v).astype(LOW)
        q[at, :] = q_low.astype(LOW)
        k[at, :] = k_low
        v[at, :] = v_low
        qt[:, at] = turn(q_low)
        for h in range(2):
            lanes = head_lanes((block, width), h)
            km[h, at, :] = jnp.where(lanes, k_low, jnp.zeros((), LOW))
            vm[h, at, :] = jnp.where(lanes, v_low, jnp.zeros((), LOW))
    copies = [pltpu.make_async_copy(a, b, sem.at[i]) for i, (a, b) in enumerate([(q, q_out), (k, k_out), (v, v_out)])]
    for copy in copies:
        copy.start()

    def one_block(j, o_ref, row):
        cols = in_place_of(plan[SLOTS + j], block)
        for span in key_spans(count):
            @pl.when(plan[SLOTS + 2 * count + j] == span)
            def _():
                rows = pl.ds(pl.multiple_of(plan[SLOTS + count + j] * block, block), span * block)
                same = spread(segk_ref[rows, :], block) == segq_ref[0:1, cols]
                made, totals = [], []
                for i in range(pairs):
                    pair = slice(i * LANES, (i + 1) * LANES)
                    for h in range(2):
                        s = jnp.where(same, dot(km[h, rows, pair], qt[pair, cols]), MASKED)
                        top = jnp.max(s, axis=0, keepdims=True)
                        p = jnp.exp(s - top)
                        total = jnp.sum(p, axis=0, keepdims=True)
                        made.append(dot_tn(p.astype(LOW), vm[h, rows, pair]))
                        totals.append(total)
                        lse_ref[2 * i + h:2 * i + h + 1, cols] = top + jnp.log(total)
                totals += [jnp.ones((1, block), F32)] * (-len(totals) % 8)
                scale = (1.0 / jnp.concatenate(totals, axis=0)).T
                for i in range(pairs):
                    o = made[2 * i] * scale[:, 2 * i:2 * i + 1] + made[2 * i + 1] * scale[:, 2 * i + 1:2 * i + 2]
                    o_ref[in_place_of(row, block), i * LANES:(i + 1) * LANES] = o.astype(LOW)

    def near_block(j, carry):
        one_block(j, om_ref, j)
        return carry

    def far_block(j, carry):
        one_block(j, os_ref, j - near)
        return carry

    lax.fori_loop(0, near, near_block, 0)
    lax.fori_loop(near, count, far_block, 0)
    for copy in copies:
        copy.wait()


def hbm(shape):
    return (shape, LOW, "hbm", None)


def attend(plan, chunks, weights, vec, pairs, near):
    block = chunks[0].shape[0]
    count = len(chunks)
    tokens = block * count
    width = pairs * LANES
    arrays, maps = weights
    low = lambda *s: pltpu.VMEM(s, LOW)
    return kernel_call(
        functools.partial(attend_kernel, block=block, count=count, near=near, pairs=pairs),
        "attend", (1,),
        (*chunks, *arrays, vec),
        [whole(c) for c in chunks]
        + [pl.BlockSpec((arrays[0].shape[0], width), m, pipeline_mode=pl.Buffered(1)) for m in maps[:3]]
        + [pl.BlockSpec((vec.shape[0], width), maps[3], pipeline_mode=pl.Buffered(1))],
        [
            ((near * block, width), LOW, None, None),
            ((tokens - near * block, width), LOW, None, None),
            ((8, tokens), F32, None, None),
            hbm((tokens, width)), hbm((tokens, width)), hbm((tokens, width)),
        ],
        [low(tokens, width), low(tokens, width), low(tokens, width), low(width, tokens), low(2, tokens, width),
         low(2, tokens, width), pltpu.VMEM((tokens, LANES), jnp.int32),
         pltpu.VMEM((8, tokens), jnp.int32), pltpu.SemaphoreType.DMA((3,))],
        4 * tokens * tokens * width, 20 * tokens * width, 2 * tokens * tokens * pairs, (plan,), 60)


def attend_back_kernel(plan, *refs, block, count, near, pairs, owned, first, base):
    chunks, refs = refs[:count], refs[count:]
    (q_in, k_in, v_in, dm_in, do_in, om_in, oo_in, lse_ref, gm_ref, go_ref, gw_ref, small_ref,
     hidden, q, k, v, given, o, qt, dt, km, vm, qm, dom, cen, dq, dk, dv, joined, segk_ref, segq_ref, sem) = refs
    tokens, width = q.shape
    head, tail = pl.ds(0, near * block), pl.ds(near * block, tokens - near * block)
    order = [(dm_in, given.at[head]), (om_in, o.at[head]), (do_in, given.at[tail]), (oo_in, o.at[tail]),
             (q_in, q), (k_in, k), (v_in, v)]
    order += [(c, hidden.at[pl.ds(i * block, block)]) for i, c in enumerate(chunks)]
    lanes_in = pl.ds(base * LANES, width)
    order = [(a.at[:, lanes_in], b) if i < 7 else (a, b) for i, (a, b) in enumerate(order)]
    copies = [pltpu.make_async_copy(a, b, sem.at[i]) for i, (a, b) in enumerate(order)]
    for copy in copies:
        copy.start()
    segk_ref[...] = segments(plan, segk_ref.shape, 0)
    segq_ref[...] = segments(plan, segq_ref.shape, 1)
    dk[...] = jnp.zeros(dk.shape, F32)
    dv[...] = jnp.zeros(dv.shape, F32)
    zero = jnp.zeros((), LOW)
    lanes = [head_lanes((block, width), h) for h in range(2)]
    for copy in copies[:4]:
        copy.wait()
    for i in range(count):
        at = in_place_of(plan[SLOTS + i], block)
        rows = given[i * block:(i + 1) * block, :]
        dt[:, at] = turn(rows.astype(F32))
        both = (rows.astype(F32) * o[i * block:(i + 1) * block, :].astype(F32)).T
        for n in range(2 * pairs):
            cen[n:n + 1, at] = jnp.sum(both[n * HEAD_DIM:(n + 1) * HEAD_DIM, :], axis=0, keepdims=True)
        for h in range(2):
            dom[h, at, :] = jnp.where(lanes[h], rows, zero)
    for copy in copies[4:7]:
        copy.wait()
    for i in range(count):
        fixed = slice(i * block, (i + 1) * block)
        qt[:, fixed] = turn(q[fixed, :].astype(F32))
        for h in range(2):
            km[h, fixed, :] = jnp.where(lanes[h], k[fixed, :], zero)
            vm[h, fixed, :] = jnp.where(lanes[h], v[fixed, :], zero)
            qm[h, fixed, :] = jnp.where(lanes[h], q[fixed, :], zero)

    def one_block(j, carry):
        cols = in_place_of(j, block)
        for span in key_spans(count):
            @pl.when(plan[SLOTS + 4 * count + j] == span)
            def _():
                rows = pl.ds(pl.multiple_of(plan[SLOTS + 3 * count + j] * block, block), span * block)
                same = spread(segk_ref[rows, :], block) == segq_ref[0:1, cols]
                for p in range(pairs):
                    pair = slice(p * LANES, (p + 1) * LANES)
                    dk_add, dv_add, dq_add = 0.0, 0.0, 0.0
                    for h in range(2):
                        n = 2 * p + h
                        s = jnp.where(same, dot(km[h, rows, pair], qt[pair, cols]), MASKED)
                        e = jnp.exp(s - lse_ref[2 * base + n:2 * base + n + 1, cols])
                        ds = (e * (dot(vm[h, rows, pair], dt[pair, cols]) - cen[n:n + 1, cols])).astype(LOW)
                        dv_add += dot(e.astype(LOW), dom[h, cols, pair])
                        dk_add += dot(ds, qm[h, cols, pair])
                        dq_add += dot_tn(ds, km[h, rows, pair])
                    dv[rows, pair] += dv_add
                    dk[rows, pair] += dk_add
                    dq[cols, pair] = dq_add * HEAD_DIM ** (-0.5)
        return carry

    lax.fori_loop(0, count, one_block, 0)
    small_ref[...] = jnp.zeros(small_ref.shape, F32)
    for i in range(count):
        at = in_place_of(plan[SLOTS + i], block)
        parts = [a[at, :].astype(LOW) for a in (dq, dk, dv)]
        small_ref[0:1, :] += jnp.sum(parts[0].astype(F32), axis=0, keepdims=True)
        small_ref[1:2, :] += jnp.sum(parts[2].astype(F32), axis=0, keepdims=True)
        columns = jnp.concatenate(
            [a[:, p * LANES:(p + 1) * LANES] for p in range(pairs) for a in parts], axis=1)
        joined[i * block:(i + 1) * block, :] = columns
        if i < near:
            gm_ref[i * block:(i + 1) * block, :] = columns
        else:
            go_ref[(i - near) * block:(i - near + 1) * block, :] = columns
    for copy in copies[7:]:
        copy.wait()
    made = dot_tn(hidden[...], joined[...]).astype(LOW)
    if owned:
        gw_ref[:, :3 * width] = made
        gw_ref[:, 3 * width:] = jnp.zeros((gw_ref.shape[0], LANES), LOW)
        whole_cols, begin = owned[1], base * LANES
        for t in range(whole_cols // owned[0]):
            low, high = max(t * owned[0], begin), min((t + 1) * owned[0], begin + width)
            if low < high:
                piece = jnp.pad(small_ref[0:2, low - begin:high - begin],
                                ((0, 14), (low - t * owned[0], LANES - (high - t * owned[0]))))
                at = pl.multiple_of((plan[first] * (whole_cols // owned[0]) + t) * owned[0], 16)
                gw_ref[pl.ds(at, 16), 3 * width:] = piece.astype(LOW)
    else:
        gw_ref[...] = made


def attend_back(plan, chunks, q, k, v, d_mine, d_others, o_mine, o_others, lse, pairs, near, owned, first, base):
    block = chunks[0].shape[0]
    count = len(chunks)
    tokens = block * count
    width = pairs * LANES
    dim = chunks[0].shape[1]
    low = lambda *s: pltpu.VMEM(s, LOW)
    wide = lambda *s: pltpu.VMEM(s, F32)
    anywhere = pl.BlockSpec(memory_space=pl.ANY)
    return kernel_call(
        functools.partial(attend_back_kernel, block=block, count=count, near=near, pairs=pairs, owned=owned, first=first, base=base),
        "attend_back", (1,),
        (*chunks, q, k, v, d_mine, d_others, o_mine, o_others, lse),
        [anywhere] * (count + 7) + [whole(lse)],
        [
            ((d_mine.shape[0], 3 * width), LOW, None, None),
            ((d_others.shape[0], 3 * width), LOW, None, None),
            ((dim, 3 * width + (LANES if owned else 0)), LOW, None, None),
            ((8, width), F32, None, None),
        ],
        [low(tokens, dim), low(tokens, width), low(tokens, width), low(tokens, width), low(tokens, width), low(tokens, width),
         low(width, tokens), low(width, tokens), low(2, tokens, width), low(2, tokens, width),
         low(2, tokens, width), low(2, tokens, width), wide(8, tokens),
         wide(tokens, width), wide(tokens, width), wide(tokens, width), low(tokens, 3 * width),
         pltpu.VMEM((tokens, LANES), jnp.int32), pltpu.VMEM((8, tokens), jnp.int32), pltpu.SemaphoreType.DMA((count + 7,))],
        10 * tokens * tokens * width, 30 * tokens * width, 2 * tokens * tokens * pairs, (plan,), 60)


def input_kernel(plan, *refs, group, runs, pairs, first):
    n = group * len(runs)
    d_ins, (w_in, dh_in, own_ref, sent_ref), held, (w_held, total, sem) = refs[:n], refs[n:n + 4], refs[n + 4:2 * n + 4], refs[2 * n + 4:]
    dim = w_in.shape[0]
    w_copies, copies = [], []
    for e in range(group):
        base = pl.multiple_of(plan[first + e] * pairs * LANES, LANES)
        for i in range(3):
            w_copies.append(pltpu.make_async_copy(
                w_in.at[:, pl.ds(base + i * dim, pairs * LANES)], w_held.at[3 * e + i], sem.at[3 * e + i]))
    for i in range(n):
        copies.append(pltpu.make_async_copy(d_ins[i], held[i], sem.at[3 * group + i]))
    last = pltpu.make_async_copy(dh_in, total, sem.at[3 * group + n])
    per = len(runs)
    for e in range(group):
        for copy in w_copies[3 * e:3 * e + 3] + copies[per * e:per * e + per]:
            copy.start()
    last.start()
    made = 0.0
    for e in range(group):
        for copy in w_copies[3 * e:3 * e + 3] + copies[per * e:per * e + per]:
            copy.wait()
        d = jnp.concatenate([held[per * e + r][...] for r in range(per)], axis=1)
        w = jnp.concatenate(
            [w_held[3 * e + i, :, j * LANES:(j + 1) * LANES] for j in range(pairs) for i in range(3)], axis=1)
        made += dot_nt(d, w)
    last.wait()
    made += total[...]
    chunk = own_ref.shape[0]
    own_ref[...] = made[:chunk]
    sent_ref[...] = made[chunk:].astype(LOW)


def input_grads(plan, d_parts, runs, w, dh, pairs, chunk, first):
    tokens, dim = dh.shape
    group = len(d_parts)
    ins = (*[d for parts in d_parts for d in parts], w, dh)
    return kernel_call(
        functools.partial(input_kernel, group=group, runs=runs, pairs=pairs, first=first), "input_grads", (1,), ins,
        [pl.BlockSpec(memory_space=pltpu.HBM)] * len(ins),
        [((chunk, dim), F32, None, None), ((tokens - chunk, dim), LOW, None, None)],
        [pltpu.VMEM(d.shape, LOW) for parts in d_parts for d in parts]
        + [pltpu.VMEM((3 * group, dim, pairs * LANES), LOW), pltpu.VMEM((tokens, dim), F32),
           pltpu.SemaphoreType.DMA((len(ins) - 2 + 3 * group + 1,))],
        6 * tokens * dim * dim, 6 * dim * dim + 10 * tokens * dim, 0, (plan,), 60)


def row_mean(values):
    return jnp.mean(values, axis=-1, keepdims=True)


def normal(values):
    centre = values - row_mean(values)
    scale = lax.rsqrt(row_mean(centre * centre) + EPS)
    return centre * scale, scale


def normal_back(hat, scale, grads):
    return scale * (grads - row_mean(grads) - hat * row_mean(grads * hat))


def head_rows(ref, owner, cols):
    return ref[pl.ds(pl.multiple_of(owner * cols, 16), cols), :]


def token_kernel(plan, *refs, group, cols, chunk, first_bias, first, count, fine):
    x_refs, o_refs, refs = refs[:2], refs[2:2 + group], refs[2 + group:]
    wa_ref, vec_ref, wi_ref, wo_ref, go_ref, gg_ref, own_ref, sent_ref, dh_ref = refs[:9]
    do_refs, refs = refs[9:9 + group], refs[9 + group:]
    if fine:
        dest, refs = [refs[3 * e:3 * e + 3] for e in range(group)], refs[3 * group:]
    else:
        (outer_ref, inner_ref, attn_ref, vector_ref), refs = refs[:4], refs[4:]
    yl, acc, g, slope, hat1, scale1, dz, attn, vectors = refs
    step = pl.program_id(0)
    tokens, dim = acc.shape
    total = lambda values: jnp.sum(values, axis=0, keepdims=True)

    def put(refs, d, r, rows, first_col, values):
        third, end = refs[0].shape[3], first_col + values.shape[1]
        for i, ref in enumerate(refs):
            low, high = max(first_col, i * third), min(end, (i + 1) * third)
            if low < high:
                ref[d, r, rows, low - i * third:high - i * third] = values[:, low - first_col:high - first_col]

    @pl.when(step == 0)
    def _():
        x = jnp.concatenate([r[...] for r in x_refs], axis=0)
        h1 = x.astype(F32) + vec_ref[0:1, :]
        for e in range(group):
            h1 += dot(o_refs[e][:, :cols], head_rows(wa_ref, plan[first + e], cols))
        hat, scale = normal(h1)
        y1 = hat * vec_ref[1:2, :] + vec_ref[2:3, :]
        hat1[...] = hat
        scale1[...] = jnp.broadcast_to(scale, scale1.shape)
        yl[...] = y1.astype(LOW)
        acc[...] = y1 + vec_ref[3:4, :]
        vectors[...] = jnp.zeros(vectors.shape, F32)

    @pl.when(step < count)
    def _():
        u = dot(yl[...], wi_ref[...]) + vec_ref[pl.ds(first_bias + step, 1), :]
        cdf = 0.5 * (1.0 + lax.erf(u * HALF_ROOT))
        low = (u * cdf).astype(LOW)
        g[step] = low
        slope[step] = (cdf + u * (PHI_SCALE * jnp.exp(-0.5 * u * u))).astype(LOW)
        acc[...] += dot(low, wo_ref[...])

    @pl.when(step == count - 1)
    def _():
        hat, scale = normal(acc[...])
        gain = vec_ref[4:5, :]
        out = hat * gain + vec_ref[5:6, :]
        high = out.astype(LOW)
        own_ref[...] = out[:chunk]
        slots = sent_ref.shape[0] - (tokens - chunk)
        place = lax.broadcasted_iota(jnp.int32, (slots, tokens), 0)
        segs = jnp.concatenate(
            [segments(plan, (slots, chunk), 1, plan[SLOTS + i] * chunk) for i in range(tokens // chunk)], axis=1)
        onehot = (place == segs).astype(LOW)
        rest = (out - high.astype(F32)).astype(LOW)
        sent_ref[:tokens - chunk, :] = high[chunk:]
        sent_ref[tokens - chunk:, :] = (dot(onehot, high) + dot(onehot, rest)).astype(LOW)
        dy = jnp.concatenate([go_ref[0], gg_ref[...]], axis=0).astype(F32)
        dh = normal_back(hat, scale, dy * gain)
        low = dh.astype(LOW)
        dz[...] = low
        acc[...] = dh
        vectors[0:1, :] = total(dy * hat)
        vectors[1:2, :] = total(dy)
        vectors[2:3, :] = total(low.astype(F32))

    @pl.when(step >= count)
    def _():
        b = plan[first + group + 1 + step - count]
        du = (dot_nt(dz[...], wo_ref[...]) * slope[b].astype(F32)).astype(LOW)
        vectors[pl.ds(8 + b, 1), :] = total(du.astype(F32))
        inner = dot_tn(yl[...], du).astype(LOW)
        if fine:
            per, unit, width = count // group, dest[0][0].shape[2] - 32, dest[0][0].shape[3] * 3 // 2
            share = unit // 2
            for e in range(group):
                member_cols = pl.ds(pl.multiple_of(plan[first + e] * (dim // group), LANES), dim // group)
                outer = dot_tn(dz[:, member_cols], g[b]).astype(LOW)
                for i in range(dim // width):
                    for r in range(per):
                        put(dest[e], b * (dim // width) + i, r, slice(0, unit), 0,
                            outer[r * unit:(r + 1) * unit, i * width:(i + 1) * width])

                @pl.when((step - count) // per == group - 1 - e)
                def _():
                    r = lax.rem(step - count, per)
                    for d in range(dest[e][0].shape[0]):
                        for half in range(2):
                            put(dest[e], d, r, slice(half * share, (half + 1) * share), width,
                                inner[d * share:(d + 1) * share, half * width:(half + 1) * width])
        else:
            outer_ref[b] = dot_tn(dz[...], g[b]).astype(LOW)
            inner_ref[b] = inner
        acc[...] += dot_nt(du, wi_ref[...])

    @pl.when(step == pl.num_programs(0) - 1)
    def _():
        hat = hat1[...]
        dy = acc[...]
        dh = normal_back(hat, scale1[:, 0:1], dy * vec_ref[1:2, :])
        dh_ref[...] = dh
        da = dh.astype(LOW)
        for e in range(group):
            made = dot_nt(da, head_rows(wa_ref, plan[first + e], cols)).astype(LOW)
            if do_refs[e].shape[1] > cols:
                do_refs[e][...] = jnp.zeros(do_refs[e].shape, LOW)
            do_refs[e][:, :cols] = made
            attn[pl.ds(pl.multiple_of(plan[first + e] * cols, 8), cols), :] = dot_tn(o_refs[e][:, :cols], da)
        vectors[3:4, :] = total(dy * hat)
        vectors[4:5, :] = total(dy)
        vectors[5:6, :] = total(da.astype(F32))
        if fine:
            n_dp, sides, unit = dest[0][0].shape[0], dest[0][0].shape[1], dest[0][0].shape[2] - 32
            for e in range(group):
                for d in range(n_dp):
                    for r in range(sides):
                        at = d * (dim // n_dp) + plan[first + e] * (24 * sides) + r * 24
                        tail = vectors[8 * r:8 * r + 8, :] if e == 0 else jnp.zeros((8, dim), F32)
                        both = jnp.concatenate([attn[pl.ds(pl.multiple_of(at, 8), 24), :], tail], axis=0)
                        put(dest[e], d, r, slice(unit, unit + 32), 0, both.astype(LOW))
        else:
            attn_ref[...] = attn[...].astype(LOW)
            vector_ref[...] = vectors[...]


def token_work(plan, x_parts, o_parts, wa, vec, wi, wo, grad_out, grad_got, cols, padded, first_bias, first, n_dp, fine):
    chunk, dim = x_parts[0].shape
    tokens = 2 * chunk
    wide = wi.shape[1]
    block = dim
    count = wide // block
    group = len(o_parts)
    ins = (*x_parts, *o_parts, wa, vec, wi, wo, grad_out, grad_got)
    specs = [whole(a) for a in ins]
    which = lambda i, n: jnp.where(i < count, i, n[first + group + 1 + jnp.maximum(i - count, 0)])
    specs[-4] = pl.BlockSpec((dim, block), lambda i, n: (0, which(i, n)))
    specs[-3] = pl.BlockSpec((block, dim), lambda i, n: (which(i, n), 0))
    specs[-2] = pl.BlockSpec((1, chunk, dim), lambda i, n: (n[first + group], 0, 0))
    outs = [
        ((chunk, dim), F32, None, None),
        ((tokens - chunk + 16, dim), LOW, None, None),
        ((tokens, dim), F32, None, None),
    ] + [((tokens, padded), LOW, None, None)] * group
    if fine:
        outs += [((n_dp, 2, dim // group // 2 + 32, 2 * (wide // n_dp) // 3), LOW, None, None)] * (3 * group)
    else:
        outs += [((count, dim, block), LOW, None, None)] * 2 + [((dim, dim), LOW, None, None), ((16, dim), F32, None, None)]
    own = lambda *s: pltpu.VMEM(s, F32)
    low = lambda *s: pltpu.VMEM(s, LOW)
    return kernel_call(
        functools.partial(token_kernel, group=group, cols=cols, chunk=chunk, first_bias=first_bias, first=first, count=count, fine=fine),
        "token_work", (2 * count,), ins, specs, outs,
        [low(tokens, dim), own(tokens, dim), low(count, tokens, block), low(count, tokens, block), own(tokens, dim),
         own(tokens, LANES), low(tokens, dim), own(dim, dim), own(16, dim)],
        12 * tokens * dim * wide, 8 * dim * wide, 2 * tokens * wide, (plan,), 60)


def swap(values, name, mask):
    size = lax.axis_size(name)
    return lax.ppermute(values, name, [(i, i ^ mask) for i in range(size)])


def after(value, *first):
    return lax.optimization_barrier((value,) + first)[0]


def add_up(parts):
    return sum(p.astype(F32) for p in parts)


def split_bits(size):
    return (2,) * (size.bit_length() - 1)


class Cut:
    def __init__(self, array, kept=()):
        self.array, self.kept = array, dict(kept)

    def pick(self, axis, index):
        return Cut(self.array, {**self.kept, axis: index})

    def value(self):
        shape = [1 if d in self.kept else n for d, n in enumerate(self.array.shape)]
        return lax.dynamic_slice(self.array, [self.kept.get(d, 0) for d in range(len(shape))], shape)


class Halving:
    def __init__(self, parts, bits):
        self.parts = [[Cut(a) for a in (p if isinstance(p, list) else [p])] for p in parts]
        self.bits = bits
        self.sides = []

    def send(self, name, mask, *first):
        axis = self.bits[name, mask]
        bit = (lax.axis_index(name) // mask) % 2
        self.sent = self.join(self.parts, first, axis, 1 - bit)
        self.got = swap(self.sent, name, mask)
        self.parts = [[c.pick(axis, bit) for c in p] for p in self.parts] + [[Cut(self.got)]]
        if name == "seq":
            self.sides.append((mask, axis))

    def join(self, parts, first=(), axis=None, index=None):
        parts = [[c if axis is None else c.pick(axis, index) for c in p] for p in parts]
        if first:
            parts[0][0] = Cut(after(parts[0][0].array, *first), parts[0][0].kept)
        fine = max(parts, key=len)
        widths = [c.array.shape[-1] for c in fine]
        edges = [sum(widths[:i]) for i in range(len(widths) + 1)]

        def cut(p, i):
            at = 0
            for c in p:
                width = c.array.shape[-1]
                if at <= edges[i] and edges[i + 1] <= at + width:
                    value = c.value()
                    return value if width == widths[i] else value[..., edges[i] - at:edges[i + 1] - at]
                at += width
            raise ValueError(widths)

        sums = [add_up([cut(p, i) for p in parts]).astype(LOW) for i in range(len(widths))]
        return sums[0] if len(sums) == 1 else jnp.concatenate(sums, axis=-1)

    def finish(self, *first):
        return self.join(self.parts, first)

    def spread(self, piece):
        for mask, axis in reversed(self.sides):
            got = swap(piece, "seq", mask)
            bit = (lax.axis_index("seq") // mask) % 2
            piece = jnp.concatenate([jnp.where(bit == 0, piece, got), jnp.where(bit == 0, got, piece)], axis=axis)
        return piece


def abreast(*chains):
    both = Halving([[c.finish() for c in chains]], chains[0].bits)
    both.sides = list(chains[0].sides)
    return both


def join_kernel(plan, *refs, moves, shapes, merged, n_outs):
    n = sum(len(m) for m in moves)
    ins, outs, held, sem = refs[:n], refs[n:n + n_outs], refs[n + n_outs:-1], refs[-1]
    copies = []
    for i, (ref, (index, cols)) in enumerate(zip(ins, [p for m in moves for p in m])):
        at = tuple(
            slice(None) if k is None else pl.ds(0, 1) if k == 0 else pl.ds(lax.rem(plan[k[0]] + k[1], 2), 1) for k in index)
        copies.append(pltpu.make_async_copy(ref.at[at + (slice(None), cols)], held[i], sem.at[i]))
    for copy in copies:
        copy.start()
    at = 0
    for i, parts in enumerate(moves):
        for copy in copies[at:at + len(parts)]:
            copy.wait()
        total = sum(r[...].astype(F32) for r in held[at:at + len(parts)]).astype(LOW)
        at += len(parts)
        if merged:
            width = total.shape[-1]
            outs[0][..., i * width:(i + 1) * width] = total
        else:
            outs[i][...] = total


def join_all(plan, chains, dims, merged=False, first=()):
    ins, specs, outs, moves, scratch = [], [], [], [], []
    if first:
        plan = after(plan, *first)
    for c, (chain, dim) in enumerate(zip(chains, dims)):
        parts = [p[0] for p in chain.parts]
        kept = dict(parts[0].kept)
        if dim is not None:
            kept[dim[0]] = dim[1]
        shape = parts[0].array.shape
        size = tuple(1 if d in kept else n for d, n in enumerate(shape[:-2])) + shape[-2:]
        move = []
        for p, part in enumerate(parts):
            array = part.array
            index = tuple(0 if array.shape[d] == 1 else kept.get(d) for d in range(array.ndim - 2))
            same = array.shape[-1] == shape[-1]
            move.append((index, slice(None) if same else pl.ds(c * shape[-1], shape[-1])))
            ins.append(array)
            specs.append(pl.BlockSpec(memory_space=pltpu.HBM if array.size * 2 > 600000 else pl.ANY))
            scratch.append(pltpu.VMEM(size, LOW))
        moves.append(move)
        outs.append(size)
    if merged:
        outs = [outs[0][:-1] + (sum(o[-1] for o in outs),)]
    return pl.pallas_call(
        functools.partial(join_kernel, moves=moves, shapes=None, merged=merged, n_outs=len(outs)),
        grid_spec=pltpu.PrefetchScalarGridSpec(
            num_scalar_prefetch=1, grid=(1,), in_specs=specs,
            out_specs=[pl.BlockSpec(o, lambda *_, n=len(o): (0,) * n, pipeline_mode=pl.Buffered(1)) for o in outs],
            scratch_shapes=scratch + [pltpu.SemaphoreType.DMA((len(ins),))]),
        out_shape=[jax.ShapeDtypeStruct(o, LOW) for o in outs],
        compiler_params=pltpu.CompilerParams(vmem_limit_bytes=(60 if len(chains) == 3 else 28) * MIB),
        cost_estimate=pl.CostEstimate(flops=1, bytes_accessed=1, transcendentals=0),
        name="join",
    )(plan, *ins)


def exchange(plan, places, chains, moves, *first):
    axes = [c.bits[m] for c, m in zip(chains, moves)]
    sents = join_all(plan, chains, [(axis, (places[m], 1)) for axis, m in zip(axes, moves)], first=first)
    for chain, (name, mask), axis, sent in zip(chains, moves, axes, sents):
        got = swap(sent, name, mask)
        chain.parts = [[c.pick(axis, (places[name, mask], 0)) for c in p] for p in chain.parts] + [[Cut(got)]]
    return sents


def exchange_merged(plan, places, chains, move, *first):
    axis = chains[0].bits[move]
    sent = join_all(plan, chains, [(axis, (places[move], 1))] * len(chains), merged=True, first=first)[0]
    got = swap(sent, *move)
    for chain in chains:
        chain.parts = [[c.pick(axis, (places[move], 0)) for c in p] for p in chain.parts] + [[Cut(got)]]
    return sent


def finish_feed_kernel(plan, *refs, first, sources):
    pieces, refs = refs[:len(sources)], refs[len(sources):]
    outer_ref, inner_ref, attn_ref, *line_refs, vec_ref, turned = refs
    width, dim = outer_ref.shape
    share = attn_ref.shape[0]
    unit = pieces[0].shape[0] - 32
    vec_ref[...] = jnp.zeros(vec_ref.shape, F32)
    for (e, d), ref in zip(sources, pieces):
        member, side = plan[first + e], lax.rem(plan[first + 2] + d, 2)
        owner = member * 2 + side
        turned[pl.ds(pl.multiple_of(owner * unit, 8), unit), :] = ref[:unit, :width].astype(F32)
        for half in range(2):
            inner_ref[:, pl.ds(pl.multiple_of(owner * 2 * width + half * width, LANES), width)] = (
                ref[half * share:(half + 1) * share, width:].astype(F32))
        attn_ref[pl.ds(pl.multiple_of(owner * 24, 8), 24), :] = ref[unit:unit + 24, :].astype(F32)
        vec_ref[pl.ds(pl.multiple_of(side * 8, 8), 8), :] += ref[unit:, :].astype(F32)[24:, :]
    outer_ref[...] = turned[...].T
    dp = plan[first + 3 + 4 + 4]
    here = pltpu.roll(vec_ref[...], lax.rem(dim - dp * share, dim), 1)
    for i, ref in enumerate(line_refs[:6]):
        ref[...] = here[i, :share]
    per = dim // width
    line_refs[6][...] = vec_ref[pl.ds(8 + dp // per, 1), pl.ds(pl.multiple_of(lax.rem(dp, per) * width, LANES), width)][0]


def finish_feed(plan, pieces, sources, first, width, share, wide):
    dim = pieces[0].shape[1]
    return kernel_call(
        functools.partial(finish_feed_kernel, first=first, sources=sources), "finish_feed", (1,), tuple(pieces),
        [whole(a) for a in pieces],
        [((width, dim), F32, None, None), ((share, wide), F32, None, None), ((share, dim), F32, None, None)]
        + [((share,), F32, None, None)] * 6 + [((width,), F32, None, None)],
        [pltpu.VMEM((16, dim), F32), pltpu.VMEM((dim, width), F32)], 0, 10 * dim * width, 0, (plan,), 12)


def finish_rest_kernel(plan, *refs, first, sources, pairs, runs):
    n = len(sources)
    groups, (out_ref, bq_ref, bv_ref, vec_ref) = [refs[i * n:(i + 1) * n] for i in range(len(runs))], refs[len(runs) * n:]
    share = bq_ref.shape[0]
    part = groups[0][0].shape[0]
    dim = out_ref.shape[1] // 3
    vec_ref[...] = jnp.zeros(vec_ref.shape, F32)
    for pieces, (begin, size) in zip(groups, runs):
        for (e, d), ref in zip(sources, pieces):
            member, side = plan[first + e], lax.rem(plan[first + 2] + d, 2)
            rows = pl.ds(pl.multiple_of(side * part, 8), part)
            for i in range(3):
                for j in range(size):
                    at = pl.multiple_of(i * dim + (member * pairs + begin + j) * LANES, LANES)
                    out_ref[rows, pl.ds(at, LANES)] = ref[:, (3 * j + i) * LANES:(3 * j + i + 1) * LANES].astype(F32)
            vec_ref[rows, :] += ref[:, 3 * size * LANES:].astype(F32)
    bq_ref[...] = vec_ref[0, :share]
    bv_ref[...] = vec_ref[1, :share]


def finish_rest(plan, groups, runs, sources, first, pairs, share, dim):
    pieces = [p for g in groups for p in g]
    return kernel_call(
        functools.partial(finish_rest_kernel, first=first, sources=sources, pairs=pairs, runs=runs), "finish_rest", (1,),
        tuple(pieces), [whole(a) for a in pieces],
        [((share, 3 * dim), F32, None, None), ((share,), F32, None, None), ((share,), F32, None, None)],
        [pltpu.VMEM((share, LANES), F32)], 0, 10 * share * dim, 0, (plan,), 12)


def by_owner(parts, member):
    stack = jnp.stack(parts)
    return [lax.dynamic_index_in_dim(stack, member ^ m, 0, keepdims=False) for m in range(len(parts))]


def body(hidden_in, passage_lengths, w_qkv, b_query, b_value, w_attn_out, b_attn_out, gain_attn,
         bias_attn, w_inner, b_inner, w_outer, b_outer, gain_ffn, bias_ffn, grad_out):
    rows, chunk, dim = hidden_in.shape
    n_dp, n_seq = lax.axis_size("dp"), lax.axis_size("seq")
    wide = w_inner.shape[1]
    slots = passage_lengths.shape[1]
    assert slots == SLOTS
    group = n_seq // rows
    seq = lax.axis_index("seq")
    side, member = seq // group, seq % group
    tokens = group * rows * chunk
    cols = HEADS // group * HEAD_DIM
    pairs = -(-cols // LANES)
    padded = pairs * LANES
    aligned = cols % LANES == 0
    count = rows * group
    share = dim // n_dp
    row_at = lambda a, d: lax.dynamic_index_in_dim(a, side ^ d, 0, keepdims=False)

    send = row_at(hidden_in, 1)
    got = swap(send, "seq", group)
    own = row_at(hidden_in, 0)
    chunks = [own, got]
    for e in range(1, group):
        chunks += [swap(own, "seq", e), swap(got, "seq", e)]
    cot_send = after(row_at(grad_out, 1), got)
    cot_got = swap(cot_send, "seq", group)

    start = jnp.stack([(side ^ d) * group + (member ^ e) for e in range(group) for d in range(rows)]).astype(jnp.int32)
    ends = jnp.cumsum(row_at(passage_lengths, 0), dtype=jnp.int32)
    segment = lambda p: jnp.sum((p[..., None] >= ends).astype(jnp.int32), axis=-1, dtype=jnp.int32)
    index = jnp.arange(count, dtype=jnp.int32)
    low_seg, high_seg = segment(index * chunk), segment(index * chunk + (chunk - 1))
    meets = (jnp.maximum(low_seg[:, None], low_seg[None, :]) <= jnp.minimum(high_seg[:, None], high_seg[None, :]))
    first_key = jnp.min(jnp.where(meets, index[None, :], count), axis=1)
    spans = jnp.max(jnp.where(meets, index[None, :], -1), axis=1) + 1 - first_key
    rounded = functools.reduce(lambda r, n: jnp.where(spans <= n, n, r), reversed(key_spans(count)), count)
    first_key = jnp.minimum(first_key, count - rounded)
    reorder = lambda a: jnp.sum(jnp.where(start[:, None] == index[None, :], a[None, :], 0), axis=1)
    per = wide // dim // group
    turns = [(member ^ e) * per + r for e in reversed(range(group)) for r in range(per)]
    moves = [("dp", 1 << b) for b in range(len(split_bits(n_dp)))] + [("seq", group)]
    members = jnp.stack([member ^ e for e in range(group)] + [side] + turns
                        + [(lax.axis_index(name) // mask) % 2 for name, mask in moves] + [lax.axis_index("dp")])
    plan = jnp.concatenate([ends, start, reorder(first_key), reorder(rounded), first_key, rounded, members]).astype(jnp.int32)
    first = SLOTS + 5 * count
    places = {m: first + group + 1 + len(turns) + i for i, m in enumerate(moves)}
    first_bias = 8
    vec = jnp.concatenate(
        [b_attn_out, gain_attn, bias_attn, b_outer, gain_ffn, bias_ffn, b_query, b_value, b_inner]
    ).astype(F32).reshape(-1, dim)
    if aligned:
        weights = [w_qkv] * 3, [lambda j, n, i=i: (0, i * group + n[first]) for i in range(3)] + [lambda j, n: (0, n[first])]
        vec_heads = vec
    else:
        widen = lambda a: jnp.pad(a, ((0, 0), (0, padded - cols)))
        weights_of = lambda m: [widen(lax.dynamic_slice_in_dim(w_qkv, m * cols + i * dim, cols, 1)) for i in range(3)]
        vec_heads = widen(lax.dynamic_slice_in_dim(vec, member * cols, cols, 1))
        weights = weights_of(member), [lambda j, n: (0, 0)] * 4

    o_mine, o_send, lse, q, k, v = attend(
        plan, chunks, weights, vec_heads, pairs, rows)
    apart = lambda a: [a] if group == 2 else [a[i * rows * chunk:(i + 1) * rows * chunk] for i in range(group - 1)]
    together = lambda a: a[0] if len(a) == 1 else jnp.concatenate(a, axis=0)
    o_parts = [o_mine] + [swap(a, "seq", e) for e, a in enumerate(apart(o_send), 1)]
    fine = aligned and (wide // n_dp) % LANES == 0 and share % 16 == 0 and per == rows and share == 24 * rows * group
    out_own, out_send, dh1, *made = token_work(
        plan, chunks[:rows], o_parts, w_attn_out, vec, w_inner, w_outer, grad_out, cot_got, cols, padded,
        first_bias, first, n_dp, fine)
    do_parts, made = made[:group], made[group:]
    do_gots = [swap(do_parts[e], "seq", e) for e in range(1, group)]
    out_got = swap(out_send, "seq", group)

    dp_masks = [1 << b for b in range(len(split_bits(n_dp)))]
    bit_shape = split_bits(n_dp) + split_bits(rows)
    bits = {("dp", m): len(dp_masks) - 1 - i for i, m in enumerate(dp_masks)}
    bits["seq", group] = len(dp_masks)

    unit, width = dim // group // rows, wide // n_dp
    if fine:
        feed_parts = made
    else:
        raw_outer, raw_inner, raw_attn, raw_vectors = made
        flat = lambda a: a.reshape(group, n_dp, rows, -1)
        feed_all = jnp.concatenate([
            flat(raw_outer.transpose(1, 0, 2).reshape(group, rows, unit, n_dp, width).transpose(0, 3, 1, 2, 4)),
            flat(raw_inner.transpose(1, 0, 2).reshape(n_dp, share, group, rows, -1).transpose(2, 0, 3, 1, 4)),
            flat(raw_attn.reshape(n_dp, group, rows, -1, dim).transpose(1, 0, 2, 3, 4))], axis=3)
        vectors = jnp.broadcast_to(raw_vectors.reshape(1, rows, -1), (n_dp, rows, 16 * dim // rows)).astype(LOW)
        feed_parts = [
            jnp.concatenate([lax.dynamic_index_in_dim(feed_all, member ^ e, 0, keepdims=False),
                             vectors if e == 0 else jnp.zeros_like(vectors)], axis=2).reshape(n_dp, rows, -1, LANES)
            for e in range(group)]
    ways = 3 if fine else 1
    shaped = lambda a: a.reshape(bit_shape + a.shape[2:])
    by_way = [[feed_parts[e * ways + i] for e in range(group)] for i in range(ways)]
    feeds = [Halving([shaped(p[0])] + [shaped(swap(after(p[e], *do_gots), "seq", e)) for e in range(1, group)], bits) for p in by_way]
    stages = [("dp", 1), ("seq", group), ("dp", 2)]

    def feed_stage(n, *before):
        moves = [stages[(n + i) % 3] for i in range(ways)]
        if fine:
            return exchange(plan, places, feeds, moves, *before)
        for f, move in zip(feeds, moves):
            f.send(*move, *before)
        return [f.sent for f in feeds]

    runs = [(0, pairs - 1), (pairs - 1, 1)]
    part = share // rows
    packed_grads = lambda a: a.reshape(bit_shape + (part, a.shape[-1]))
    owned = (share, padded) if fine else None
    back = lambda do, run: attend_back(
        plan, chunks, q, k, v, do_parts[0], do, o_mine, o_send, lse, run[1], rows, owned, first, run[0])
    do_in = together(do_gots)
    d_mine_a, d_other_a, grad_qkv_a, small_a = back(do_in, runs[0])
    sent = feed_stage(0, grad_qkv_a, out_got)
    d_gots_a = [swap(a, "seq", e) for e, a in enumerate(apart(d_other_a), 1)]
    d_mine_b, d_other_b, grad_qkv_b, small_b = back(after(do_in, *sent), runs[1])
    d_gots_b = [swap(a, "seq", e) for e, a in enumerate(apart(d_other_b), 1)]

    if fine:
        rests = [Halving([packed_grads(grad_qkv_a)], bits), Halving([packed_grads(grad_qkv_b)], bits)]
    else:
        heads = lax.dynamic_update_slice_in_dim(
            jnp.zeros((2, dim), F32), jnp.concatenate([small_a, small_b], axis=1)[:2, :cols], member * cols, 1)
        vectors = heads.reshape(2, n_dp, -1).transpose(1, 0, 2)
        vectors = jnp.pad(vectors, ((0, 0), (0, rows * part - 2), (0, LANES - share))).astype(LOW).reshape(n_dp, rows, part, LANES)
        rests = [Halving([[packed_grads(grad_qkv_a), packed_grads(grad_qkv_b), vectors.reshape(bit_shape + vectors.shape[2:])]], bits)]
    rest_moves = [[("dp", 1), ("dp", 2)], [("seq", group), ("dp", 1)], [("dp", 2), ("seq", group)]]

    def rest_stage(n, *before):
        moves = rest_moves[n] if n < 3 else [dp_stages[n - 1]] * 2
        if fine:
            return exchange(plan, places, rests, moves, *before)
        rests[0].send(*moves[0], *before)
        return [rests[0].sent]

    dp_stages = [("dp", m) for m in dp_masks]
    rest_sent = rest_stage(0, *sent)

    sent = feed_stage(1, *rest_sent)

    runs_of = [[d_mine_a, d_mine_b]] + [[a, b] for a, b in zip(d_gots_a, d_gots_b)]
    if aligned:
        in_own, in_send = input_grads(plan, runs_of, runs, w_qkv, after(dh1, *sent), pairs, chunk, first)
    else:
        grad_hidden = dh1
        for e, parts in enumerate(runs_of):
            w = weights_of(member ^ e)
            d = jnp.concatenate(parts, axis=1)
            for j in range(pairs):
                w_pair = jnp.concatenate([a[:, j * LANES:(j + 1) * LANES] for a in w], axis=1)
                grad_hidden = grad_hidden + dot_nt(d[:, j * 3 * LANES:(j + 1) * 3 * LANES], w_pair)
        in_own, in_send = grad_hidden[:chunk], grad_hidden[chunk:].astype(LOW)

    rest_sent = rest_stage(1, in_send)
    sent = feed_stage(2, *rest_sent)
    rest_sent = rest_stage(2, *sent)
    if fine:
        last = ("dp", dp_masks[-1])
        sent = exchange_merged(plan, places, feeds, last, *rest_sent)
        in_got = swap(after(in_send, sent), "seq", group)
        rest_stage(3, sent)
        late = [r.parts[-1][0].array for r in rests]
        feed_piece = join_all(plan, feeds, [None] * ways, merged=True, first=late)[0]
        rest_pieces = join_all(plan, rests, [None] * 2, first=(feed_piece,))
        late = rest_pieces
    else:
        feed = feeds[0]
        in_got = swap(in_send, "seq", group)
        for i, mask in enumerate(dp_masks[2:]):
            feed.send("dp", mask, *rest_sent)
            rest_sent = rest_stage(3 + i, feed.sent)
        late = rest_sent
        feed_piece, rest_piece = feed.finish(*late), rests[0].finish()

    def everyone(piece):
        gots = [piece] + [swap(piece, "seq", e) for e in range(1, group)]
        return by_owner(gots, member)

    here = lambda a: lax.dynamic_slice_in_dim(a.reshape(-1), lax.axis_index("dp") * (a.size // n_dp), a.size // n_dp)
    if fine:
        sources = [(0, 0), (0, 1), (1, 0), (1, 1)]

        def from_all(piece):
            piece = piece.reshape(piece.shape[-2:])
            got = swap(piece, "seq", group)
            return [piece, got, swap(piece, "seq", 1), swap(got, "seq", 1)]

        (grad_w_outer, grad_w_inner, grad_w_attn_out, grad_gain_ffn, grad_bias_ffn, grad_b_outer, grad_gain_attn,
         grad_bias_attn, grad_b_attn_out, grad_b_inner) = finish_feed(
            plan, from_all(feed_piece), sources, first, width, share, wide)
        grad_w_qkv, grad_b_query, grad_b_value = finish_rest(
            plan, [from_all(a) for a in rest_pieces], runs, sources, first, pairs, share, dim)
    else:
        feed_pieces = everyone(feed.spread(feed_piece))
        sizes = [unit * width, share * (wide // group // rows), share * dim // group // rows, 16 * dim // rows]
        ends_of = [sum(sizes[:i]) for i in range(5)]
        cut = lambda a, i: a.reshape(rows, -1)[:, ends_of[i]:ends_of[i + 1]]
        grad_w_outer = jnp.concatenate([cut(a, 0).reshape(rows * unit, width) for a in feed_pieces]).T.astype(F32)
        grad_w_inner = jnp.concatenate(
            [cut(a, 1).reshape(rows, share, -1)[r] for a in feed_pieces for r in range(rows)], axis=1).astype(F32)
        grad_w_attn_out = jnp.concatenate([cut(a, 2).reshape(-1, dim) for a in feed_pieces], axis=0).astype(F32)
        totals = add_up([cut(a, 3) for a in feed_pieces]).reshape(16, dim)
        rest_pieces = [a.reshape(share, -1) for a in everyone(rests[0].spread(rest_piece))]
        grad_w_qkv = jnp.concatenate(
            [jnp.concatenate([a[:, (3 * j + i) * LANES:(3 * j + i + 1) * LANES] for j in range(pairs)], axis=1)[:, :cols]
             for i in range(3) for a in rest_pieces], axis=1).astype(F32)
        sums_qv = add_up([a[:, 3 * padded:] for a in rest_pieces])
        (grad_gain_ffn, grad_bias_ffn, grad_b_outer, grad_gain_attn, grad_bias_attn, grad_b_attn_out) = [
            here(totals[i]) for i in range(6)]
        grad_b_inner = here(totals[8:8 + wide // dim])
        grad_b_query, grad_b_value = sums_qv[0, :share], sums_qv[1, :share]

    def in_place(own, got):
        return jnp.where(side == 0, jnp.stack([own, got]), jnp.stack([got, own]))

    out = in_place(after(out_own, *rest_sent), out_got[:chunk].astype(F32))
    grad_in = in_place(after(in_own, *late), in_got.astype(F32))
    sums = in_place(after(out_send, *rest_sent)[chunk:chunk + slots], out_got[chunk:chunk + slots])
    sums = add_up([sums] + [swap(sums, "seq", e) for e in range(1, group)])
    pooled = sums / jnp.maximum(passage_lengths.astype(F32), 1.0)[:, :, None]

    return (out, pooled, grad_in, grad_w_qkv, grad_b_query, grad_b_value, grad_w_attn_out,
            grad_b_attn_out, grad_gain_attn, grad_bias_attn, grad_w_inner, grad_b_inner,
            grad_w_outer, grad_b_outer, grad_gain_ffn, grad_bias_ffn)


def solution(mesh):
    tokens, rows, all_of = P("dp", "seq", None), P("dp", None), P()
    vector, cube = P("dp"), P("dp", None, None)
    return jax.shard_map(
        body,
        mesh=mesh,
        in_specs=(tokens, rows) + (all_of,) * 13 + (tokens,),
        out_specs=(tokens, cube, tokens, rows, vector, vector, rows, vector, vector, vector, rows,
                   vector, rows, vector, vector, vector),
        check_vma=False,
    )
```

```python
import functools
import math

import jax
import jax.numpy as jnp
from jax import lax
from jax.experimental import pallas as pl
from jax.experimental.pallas import tpu as pltpu
from jax.sharding import PartitionSpec as P

LOW = jnp.bfloat16
F32 = jnp.float32
HEADS = 12
HEAD_DIM = 64
LANES = 128
MIB = 1024 * 1024
MASKED = -1e30
EPS = 1e-12
COST = 1000
SLOTS = 8
HALF_ROOT = math.sqrt(0.5)
PHI_SCALE = 1.0 / math.sqrt(2.0 * math.pi)


def dot(left, right):
    return jnp.dot(left, right, preferred_element_type=F32)


def dot_nt(left, right):
    return lax.dot_general(left, right, (((1,), (1,)), ((), ())), preferred_element_type=F32)


def dot_tn(left, right):
    return lax.dot_general(left, right, (((0,), (0,)), ((), ())), preferred_element_type=F32)


def head_lanes(shape, head):
    lane = lax.rem(lax.broadcasted_iota(jnp.int32, shape, 1), LANES)
    return (lane >= HEAD_DIM) if head else (lane < HEAD_DIM)


def spread(column, width):
    return jnp.concatenate([column] * (width // LANES), axis=1)


def segments(plan, shape, axis, start=0):
    place = lax.broadcasted_iota(jnp.int32, shape, axis) + start
    return sum((place >= plan[j]).astype(jnp.int32) for j in range(SLOTS))


def whole(array, buffers=1):
    return pl.BlockSpec(array.shape, lambda *_: (0,) * array.ndim, pipeline_mode=pl.Buffered(buffers))


def kernel_call(body, name, grid, ins, in_specs, outs, scratch, flops, moved, exps=0, prefetch=(), limit=24):
    spec = pltpu.PrefetchScalarGridSpec(
        num_scalar_prefetch=len(prefetch),
        grid=grid,
        in_specs=in_specs,
        out_specs=[
            pl.BlockSpec(memory_space=pltpu.HBM) if b == "hbm" else pl.BlockSpec(b, m) if b else pl.BlockSpec(s, lambda *_, n=len(s): (0,) * n, pipeline_mode=pl.Buffered(1))
            for s, _, b, m in outs
        ],
        scratch_shapes=scratch,
    )
    return pl.pallas_call(
        body,
        grid_spec=spec,
        out_shape=[jax.ShapeDtypeStruct(s, t) for s, t, _, _ in outs],
        compiler_params=pltpu.CompilerParams(vmem_limit_bytes=limit * MIB),
        cost_estimate=pl.CostEstimate(flops=int(flops) // COST, bytes_accessed=int(moved) // COST, transcendentals=int(exps) // COST),
        name=name,
    )(*prefetch, *ins)


def key_spans(count):
    return list(range(1, count + 1)) if count <= 4 else [n for n in (1, 2, 4, 8, 16) if n <= count]


def turn(block):
    return block.T.astype(LOW)


def in_place_of(ref, chunk):
    return pl.ds(pl.multiple_of(ref * chunk, chunk), chunk)


def attend_kernel(plan, *refs, block, count, near, pairs):
    chunks, refs = refs[:count], refs[count:]
    (wq_ref, wk_ref, wv_ref, vec_ref, om_ref, os_ref, lse_ref, q_out, k_out, v_out,
     q, k, v, qt, km, vm, segk_ref, segq_ref, sem) = refs
    width = pairs * LANES
    segk_ref[...] = segments(plan, segk_ref.shape, 0)
    segq_ref[...] = segments(plan, segq_ref.shape, 1)
    lse_ref[...] = jnp.zeros(lse_ref.shape, F32)
    w = jnp.concatenate([wq_ref[...], wk_ref[...], wv_ref[...]], axis=1)
    bias_q, bias_v = vec_ref[6:7, :], vec_ref[7:8, :]
    for i in range(count):
        at = in_place_of(plan[SLOTS + i], block)
        made = dot(chunks[i][...], w)
        q_low = (made[:, :width] + bias_q).astype(LOW).astype(F32) * HEAD_DIM ** (-0.5)
        k_low = made[:, width:2 * width].astype(LOW)
        v_low = (made[:, 2 * width:] + bias_v).astype(LOW)
        q[at, :] = q_low.astype(LOW)
        k[at, :] = k_low
        v[at, :] = v_low
        qt[:, at] = turn(q_low)
        for h in range(2):
            lanes = head_lanes((block, width), h)
            km[h, at, :] = jnp.where(lanes, k_low, jnp.zeros((), LOW))
            vm[h, at, :] = jnp.where(lanes, v_low, jnp.zeros((), LOW))
    copies = [pltpu.make_async_copy(a, b, sem.at[i]) for i, (a, b) in enumerate([(q, q_out), (k, k_out), (v, v_out)])]
    for copy in copies:
        copy.start()

    def one_block(j, o_ref, row):
        cols = in_place_of(plan[SLOTS + j], block)
        for span in key_spans(count):
            @pl.when(plan[SLOTS + 2 * count + j] == span)
            def _():
                rows = pl.ds(pl.multiple_of(plan[SLOTS + count + j] * block, block), span * block)
                same = spread(segk_ref[rows, :], block) == segq_ref[0:1, cols]
                made, totals = [], []
                for i in range(pairs):
                    pair = slice(i * LANES, (i + 1) * LANES)
                    for h in range(2):
                        s = jnp.where(same, dot(km[h, rows, pair], qt[pair, cols]), MASKED)
                        top = jnp.max(s, axis=0, keepdims=True)
                        p = jnp.exp(s - top)
                        total = jnp.sum(p, axis=0, keepdims=True)
                        made.append(dot_tn(p.astype(LOW), vm[h, rows, pair]))
                        totals.append(total)
                        lse_ref[2 * i + h:2 * i + h + 1, cols] = top + jnp.log(total)
                totals += [jnp.ones((1, block), F32)] * (-len(totals) % 8)
                scale = (1.0 / jnp.concatenate(totals, axis=0)).T
                for i in range(pairs):
                    o = made[2 * i] * scale[:, 2 * i:2 * i + 1] + made[2 * i + 1] * scale[:, 2 * i + 1:2 * i + 2]
                    o_ref[in_place_of(row, block), i * LANES:(i + 1) * LANES] = o.astype(LOW)

    def near_block(j, carry):
        one_block(j, om_ref, j)
        return carry

    def far_block(j, carry):
        one_block(j, os_ref, j - near)
        return carry

    lax.fori_loop(0, near, near_block, 0)
    lax.fori_loop(near, count, far_block, 0)
    for copy in copies:
        copy.wait()


def hbm(shape):
    return (shape, LOW, "hbm", None)


def attend(plan, chunks, weights, vec, pairs, near):
    block = chunks[0].shape[0]
    count = len(chunks)
    tokens = block * count
    width = pairs * LANES
    arrays, maps = weights
    low = lambda *s: pltpu.VMEM(s, LOW)
    return kernel_call(
        functools.partial(attend_kernel, block=block, count=count, near=near, pairs=pairs),
        "attend", (1,),
        (*chunks, *arrays, vec),
        [whole(c) for c in chunks]
        + [pl.BlockSpec((arrays[0].shape[0], width), m, pipeline_mode=pl.Buffered(1)) for m in maps[:3]]
        + [pl.BlockSpec((vec.shape[0], width), maps[3], pipeline_mode=pl.Buffered(1))],
        [
            ((near * block, width), LOW, None, None),
            ((tokens - near * block, width), LOW, None, None),
            ((8, tokens), F32, None, None),
            hbm((tokens, width)), hbm((tokens, width)), hbm((tokens, width)),
        ],
        [low(tokens, width), low(tokens, width), low(tokens, width), low(width, tokens), low(2, tokens, width),
         low(2, tokens, width), pltpu.VMEM((tokens, LANES), jnp.int32),
         pltpu.VMEM((8, tokens), jnp.int32), pltpu.SemaphoreType.DMA((3,))],
        4 * tokens * tokens * width, 20 * tokens * width, 2 * tokens * tokens * pairs, (plan,), 60)


def attend_back_kernel(plan, *refs, block, count, near, pairs, owned, first):
    chunks, refs = refs[:count], refs[count:]
    (q_in, k_in, v_in, dm_in, do_in, om_in, oo_in, lse_ref, gm_ref, go_ref, small_ref), refs = refs[:11], refs[11:]
    gw_refs, refs = refs[:2 if owned else 1], refs[2 if owned else 1:]
    (hidden, q, k, v, given, o, qt, dt, km, vm, qm, dom, cen, dq, dk, dv, joined, segk_ref, segq_ref, sem) = refs
    tokens, width = q.shape
    head, tail = pl.ds(0, near * block), pl.ds(near * block, tokens - near * block)
    order = [(dm_in, given.at[head]), (om_in, o.at[head]), (do_in, given.at[tail]), (oo_in, o.at[tail]),
             (q_in, q), (k_in, k), (v_in, v)]
    order += [(c, hidden.at[pl.ds(i * block, block)]) for i, c in enumerate(chunks)]
    copies = [pltpu.make_async_copy(a, b, sem.at[i]) for i, (a, b) in enumerate(order)]
    for copy in copies:
        copy.start()
    segk_ref[...] = segments(plan, segk_ref.shape, 0)
    segq_ref[...] = segments(plan, segq_ref.shape, 1)
    dk[...] = jnp.zeros(dk.shape, F32)
    dv[...] = jnp.zeros(dv.shape, F32)
    zero = jnp.zeros((), LOW)
    lanes = [head_lanes((block, width), h) for h in range(2)]
    for copy in copies[:4]:
        copy.wait()
    for i in range(count):
        at = in_place_of(plan[SLOTS + i], block)
        rows = given[i * block:(i + 1) * block, :]
        dt[:, at] = turn(rows.astype(F32))
        both = (rows.astype(F32) * o[i * block:(i + 1) * block, :].astype(F32)).T
        for n in range(2 * pairs):
            cen[n:n + 1, at] = jnp.sum(both[n * HEAD_DIM:(n + 1) * HEAD_DIM, :], axis=0, keepdims=True)
        for h in range(2):
            dom[h, at, :] = jnp.where(lanes[h], rows, zero)
    for copy in copies[4:7]:
        copy.wait()
    for i in range(count):
        fixed = slice(i * block, (i + 1) * block)
        qt[:, fixed] = turn(q[fixed, :].astype(F32))
        for h in range(2):
            km[h, fixed, :] = jnp.where(lanes[h], k[fixed, :], zero)
            vm[h, fixed, :] = jnp.where(lanes[h], v[fixed, :], zero)
            qm[h, fixed, :] = jnp.where(lanes[h], q[fixed, :], zero)

    def one_block(j, carry):
        cols = in_place_of(j, block)
        for span in key_spans(count):
            @pl.when(plan[SLOTS + 4 * count + j] == span)
            def _():
                rows = pl.ds(pl.multiple_of(plan[SLOTS + 3 * count + j] * block, block), span * block)
                same = spread(segk_ref[rows, :], block) == segq_ref[0:1, cols]
                for p in range(pairs):
                    pair = slice(p * LANES, (p + 1) * LANES)
                    dk_add, dv_add, dq_add = 0.0, 0.0, 0.0
                    for h in range(2):
                        n = 2 * p + h
                        s = jnp.where(same, dot(km[h, rows, pair], qt[pair, cols]), MASKED)
                        e = jnp.exp(s - lse_ref[n:n + 1, cols])
                        ds = (e * (dot(vm[h, rows, pair], dt[pair, cols]) - cen[n:n + 1, cols])).astype(LOW)
                        dv_add += dot(e.astype(LOW), dom[h, cols, pair])
                        dk_add += dot(ds, qm[h, cols, pair])
                        dq_add += dot_tn(ds, km[h, rows, pair])
                    dv[rows, pair] += dv_add
                    dk[rows, pair] += dk_add
                    dq[cols, pair] = dq_add * HEAD_DIM ** (-0.5)
        return carry

    lax.fori_loop(0, count, one_block, 0)
    small_ref[...] = jnp.zeros(small_ref.shape, F32)
    for i in range(count):
        at = in_place_of(plan[SLOTS + i], block)
        parts = [a[at, :].astype(LOW) for a in (dq, dk, dv)]
        small_ref[0:1, :] += jnp.sum(parts[0].astype(F32), axis=0, keepdims=True)
        small_ref[1:2, :] += jnp.sum(parts[2].astype(F32), axis=0, keepdims=True)
        columns = jnp.concatenate(
            [a[:, p * LANES:(p + 1) * LANES] for p in range(pairs) for a in parts], axis=1)
        joined[i * block:(i + 1) * block, :] = columns
    leaving = [pltpu.make_async_copy(joined.at[head], gm_ref, sem.at[count + 7]),
               pltpu.make_async_copy(joined.at[tail], go_ref, sem.at[count + 8])]
    for copy in leaving:
        copy.start()
    for copy in copies[7:]:
        copy.wait()
    made = dot_tn(hidden[...], joined[...]).astype(LOW)
    for copy in leaving:
        copy.wait()
    if owned:
        half = gw_refs[0].shape[1]
        gw_refs[0][...] = made[:, :half]
        gw_refs[1][:, :3 * width - half] = made[:, half:]
        gw_refs[1][:, 3 * width - half:] = jnp.zeros((made.shape[0], LANES), LOW)
        for t in range(width // owned):
            piece = jnp.pad(small_ref[0:2, t * owned:(t + 1) * owned], ((0, 14), (0, LANES - owned)))
            at = pl.multiple_of((plan[first] * (width // owned) + t) * owned, 16)
            gw_refs[1][pl.ds(at, 16), 3 * width - half:] = piece.astype(LOW)
    else:
        gw_refs[0][...] = made


def attend_back(plan, chunks, q, k, v, d_mine, d_others, o_mine, o_others, lse, pairs, near, owned, first):
    block = chunks[0].shape[0]
    count = len(chunks)
    tokens = block * count
    width = pairs * LANES
    dim = chunks[0].shape[1]
    low = lambda *s: pltpu.VMEM(s, LOW)
    wide = lambda *s: pltpu.VMEM(s, F32)
    anywhere = pl.BlockSpec(memory_space=pl.ANY)
    return kernel_call(
        functools.partial(attend_back_kernel, block=block, count=count, near=near, pairs=pairs, owned=owned, first=first),
        "attend_back", (1,),
        (*chunks, q, k, v, d_mine, d_others, o_mine, o_others, lse),
        [anywhere] * (count + 7) + [whole(lse)],
        [
            hbm((d_mine.shape[0], 3 * width)), hbm((d_others.shape[0], 3 * width)),
            ((8, width), F32, None, None),
        ] + [((dim, n), LOW, None, None) for n in ([(3 * width + LANES) // 2] * 2 if owned else [3 * width])],
        [low(tokens, dim), low(tokens, width), low(tokens, width), low(tokens, width), low(tokens, width), low(tokens, width),
         low(width, tokens), low(width, tokens), low(2, tokens, width), low(2, tokens, width),
         low(2, tokens, width), low(2, tokens, width), wide(8, tokens),
         wide(tokens, width), wide(tokens, width), wide(tokens, width), low(tokens, 3 * width),
         pltpu.VMEM((tokens, LANES), jnp.int32), pltpu.VMEM((8, tokens), jnp.int32), pltpu.SemaphoreType.DMA((count + 9,))],
        10 * tokens * tokens * width, 30 * tokens * width, 2 * tokens * tokens * pairs, (plan,), 60)


def input_kernel(plan, *refs, group, runs, pairs, first):
    n = group * len(runs)
    d_ins, (w_in, dh_in, own_ref, sent_ref), held, (w_held, total, sem) = refs[:n], refs[n:n + 4], refs[n + 4:2 * n + 4], refs[2 * n + 4:]
    dim = w_in.shape[0]
    w_copies, copies = [], []
    for e in range(group):
        base = pl.multiple_of(plan[first + e] * pairs * LANES, LANES)
        for i in range(3):
            w_copies.append(pltpu.make_async_copy(
                w_in.at[:, pl.ds(base + i * dim, pairs * LANES)], w_held.at[3 * e + i], sem.at[3 * e + i]))
    for i in range(n):
        copies.append(pltpu.make_async_copy(d_ins[i], held[i], sem.at[3 * group + i]))
    last = pltpu.make_async_copy(dh_in, total, sem.at[3 * group + n])
    per = len(runs)
    for e in range(group):
        for copy in w_copies[3 * e:3 * e + 3] + copies[per * e:per * e + per]:
            copy.start()
    last.start()
    made = 0.0
    for e in range(group):
        for copy in w_copies[3 * e:3 * e + 3] + copies[per * e:per * e + per]:
            copy.wait()
        d = jnp.concatenate([held[per * e + r][...] for r in range(per)], axis=1)
        w = jnp.concatenate(
            [w_held[3 * e + i, :, j * LANES:(j + 1) * LANES] for j in range(pairs) for i in range(3)], axis=1)
        made += dot_nt(d, w)
    last.wait()
    made += total[...]
    chunk = own_ref.shape[0]
    own_ref[...] = made[:chunk]
    sent_ref[...] = made[chunk:].astype(LOW)


def input_grads(plan, d_parts, runs, w, dh, pairs, chunk, first):
    tokens, dim = dh.shape
    group = len(d_parts)
    ins = (*[d for parts in d_parts for d in parts], w, dh)
    return kernel_call(
        functools.partial(input_kernel, group=group, runs=runs, pairs=pairs, first=first), "input_grads", (1,), ins,
        [pl.BlockSpec(memory_space=pltpu.HBM)] * len(ins),
        [((chunk, dim), F32, None, None), ((tokens - chunk, dim), LOW, None, None)],
        [pltpu.VMEM(d.shape, LOW) for parts in d_parts for d in parts]
        + [pltpu.VMEM((3 * group, dim, pairs * LANES), LOW), pltpu.VMEM((tokens, dim), F32),
           pltpu.SemaphoreType.DMA((len(ins) - 2 + 3 * group + 1,))],
        6 * tokens * dim * dim, 6 * dim * dim + 10 * tokens * dim, 0, (plan,), 60)


def row_mean(values):
    return jnp.mean(values, axis=-1, keepdims=True)


def normal(values):
    centre = values - row_mean(values)
    scale = lax.rsqrt(row_mean(centre * centre) + EPS)
    return centre * scale, scale


def normal_back(hat, scale, grads):
    return scale * (grads - row_mean(grads) - hat * row_mean(grads * hat))


def head_rows(ref, owner, cols):
    return ref[pl.ds(pl.multiple_of(owner * cols, 16), cols), :]


def token_kernel(plan, *refs, group, cols, chunk, first_bias, first, count, fine):
    x_refs, o_refs, refs = refs[:2], refs[2:2 + group], refs[2 + group:]
    wa_ref, vec_ref, wi_ref, wo_ref, go_ref, gg_ref, own_ref, sent_ref, dh_ref = refs[:9]
    do_refs, refs = refs[9:9 + group], refs[9 + group:]
    if fine:
        dest_out, refs = refs[:3 * group], refs[3 * group:]
        held, sem, refs = refs[-1 - 3 * group:-1], refs[-1], refs[:-1 - 3 * group]
        dest = [held[3 * e:3 * e + 3] for e in range(group)]
    else:
        (outer_ref, inner_ref, attn_ref, vector_ref), refs = refs[:4], refs[4:]
    yl, acc, g, slope, hat1, scale1, dz, attn, vectors = refs
    step = pl.program_id(0)
    tokens, dim = acc.shape
    total = lambda values: jnp.sum(values, axis=0, keepdims=True)

    def put(refs, d, r, rows, first_col, values):
        third, end = refs[0].shape[3], first_col + values.shape[1]
        for i, ref in enumerate(refs):
            low, high = max(first_col, i * third), min(end, (i + 1) * third)
            if low < high:
                ref[d, r, rows, low - i * third:high - i * third] = values[:, low - first_col:high - first_col]

    @pl.when(step == 0)
    def _():
        x = jnp.concatenate([r[...] for r in x_refs], axis=0)
        h1 = x.astype(F32) + vec_ref[0:1, :]
        for e in range(group):
            h1 += dot(o_refs[e][:, :cols], head_rows(wa_ref, plan[first + e], cols))
        hat, scale = normal(h1)
        y1 = hat * vec_ref[1:2, :] + vec_ref[2:3, :]
        hat1[...] = hat
        scale1[...] = jnp.broadcast_to(scale, scale1.shape)
        yl[...] = y1.astype(LOW)
        acc[...] = y1 + vec_ref[3:4, :]
        vectors[...] = jnp.zeros(vectors.shape, F32)

    @pl.when(step < count)
    def _():
        u = dot(yl[...], wi_ref[...]) + vec_ref[pl.ds(first_bias + step, 1), :]
        cdf = 0.5 * (1.0 + lax.erf(u * HALF_ROOT))
        low = (u * cdf).astype(LOW)
        g[step] = low
        slope[step] = (cdf + u * (PHI_SCALE * jnp.exp(-0.5 * u * u))).astype(LOW)
        acc[...] += dot(low, wo_ref[...])

    @pl.when(step == count - 1)
    def _():
        hat, scale = normal(acc[...])
        gain = vec_ref[4:5, :]
        out = hat * gain + vec_ref[5:6, :]
        high = out.astype(LOW)
        own_ref[...] = out[:chunk]
        slots = sent_ref.shape[0] - (tokens - chunk)
        place = lax.broadcasted_iota(jnp.int32, (slots, tokens), 0)
        segs = jnp.concatenate(
            [segments(plan, (slots, chunk), 1, plan[SLOTS + i] * chunk) for i in range(tokens // chunk)], axis=1)
        onehot = (place == segs).astype(LOW)
        rest = (out - high.astype(F32)).astype(LOW)
        sent_ref[:tokens - chunk, :] = high[chunk:]
        sent_ref[tokens - chunk:, :] = (dot(onehot, high) + dot(onehot, rest)).astype(LOW)
        dy = jnp.concatenate([go_ref[0], gg_ref[...]], axis=0).astype(F32)
        dh = normal_back(hat, scale, dy * gain)
        low = dh.astype(LOW)
        dz[...] = low
        acc[...] = dh
        vectors[0:1, :] = total(dy * hat)
        vectors[1:2, :] = total(dy)
        vectors[2:3, :] = total(low.astype(F32))

    @pl.when(step >= count)
    def _():
        b = plan[first + group + 1 + step - count]
        du = (dot_nt(dz[...], wo_ref[...]) * slope[b].astype(F32)).astype(LOW)
        vectors[pl.ds(8 + b, 1), :] = total(du.astype(F32))
        inner = dot_tn(yl[...], du).astype(LOW)
        if fine:
            per, unit, width = count // group, dest[0][0].shape[2] - 32, dest[0][0].shape[3] * 3 // 2
            share = unit // 2
            for e in range(group):
                member_cols = pl.ds(pl.multiple_of(plan[first + e] * (dim // group), LANES), dim // group)
                outer = dot_tn(dz[:, member_cols], g[b]).astype(LOW)
                for i in range(dim // width):
                    for r in range(per):
                        put(dest[e], b * (dim // width) + i, r, slice(0, unit), 0,
                            outer[r * unit:(r + 1) * unit, i * width:(i + 1) * width])

                @pl.when((step - count) // per == group - 1 - e)
                def _():
                    r = lax.rem(step - count, per)
                    for d in range(dest[e][0].shape[0]):
                        for half in range(2):
                            put(dest[e], d, r, slice(half * share, (half + 1) * share), width,
                                inner[d * share:(d + 1) * share, half * width:(half + 1) * width])
        else:
            outer_ref[b] = dot_tn(dz[...], g[b]).astype(LOW)
            inner_ref[b] = inner
        acc[...] += dot_nt(du, wi_ref[...])

    def leave(rows, start):
        return [pltpu.make_async_copy(a.at[:, :, rows], b.at[:, :, rows], sem.at[start + i])
                for i, (a, b) in enumerate(zip(held, dest_out))]

    @pl.when(step == pl.num_programs(0) - 1)
    def _():
        if fine:
            unit = held[0].shape[2] - 32
            copies = leave(pl.ds(0, unit), 0)
            for copy in copies:
                copy.start()
        hat = hat1[...]
        dy = acc[...]
        dh = normal_back(hat, scale1[:, 0:1], dy * vec_ref[1:2, :])
        dh_ref[...] = dh
        da = dh.astype(LOW)
        for e in range(group):
            made = dot_nt(da, head_rows(wa_ref, plan[first + e], cols)).astype(LOW)
            if do_refs[e].shape[1] > cols:
                do_refs[e][...] = jnp.zeros(do_refs[e].shape, LOW)
            do_refs[e][:, :cols] = made
            attn[pl.ds(pl.multiple_of(plan[first + e] * cols, 8), cols), :] = dot_tn(o_refs[e][:, :cols], da)
        vectors[3:4, :] = total(dy * hat)
        vectors[4:5, :] = total(dy)
        vectors[5:6, :] = total(da.astype(F32))
        if fine:
            n_dp, sides, unit = dest[0][0].shape[0], dest[0][0].shape[1], dest[0][0].shape[2] - 32
            for e in range(group):
                for d in range(n_dp):
                    for r in range(sides):
                        at = d * (dim // n_dp) + plan[first + e] * (24 * sides) + r * 24
                        tail = vectors[8 * r:8 * r + 8, :] if e == 0 else jnp.zeros((8, dim), F32)
                        both = jnp.concatenate([attn[pl.ds(pl.multiple_of(at, 8), 24), :], tail], axis=0)
                        put(dest[e], d, r, slice(unit, unit + 32), 0, both.astype(LOW))
            copies += leave(pl.ds(unit, 32), 3 * group)
            for copy in copies[3 * group:]:
                copy.start()
            for copy in copies:
                copy.wait()
        else:
            attn_ref[...] = attn[...].astype(LOW)
            vector_ref[...] = vectors[...]


def token_work(plan, x_parts, o_parts, wa, vec, wi, wo, grad_out, grad_got, cols, padded, first_bias, first, n_dp, fine):
    chunk, dim = x_parts[0].shape
    tokens = 2 * chunk
    wide = wi.shape[1]
    block = dim
    count = wide // block
    group = len(o_parts)
    ins = (*x_parts, *o_parts, wa, vec, wi, wo, grad_out, grad_got)
    specs = [whole(a) for a in ins]
    which = lambda i, n: jnp.where(i < count, i, n[first + group + 1 + jnp.maximum(i - count, 0)])
    specs[-4] = pl.BlockSpec((dim, block), lambda i, n: (0, which(i, n)))
    specs[-3] = pl.BlockSpec((block, dim), lambda i, n: (which(i, n), 0))
    specs[-2] = pl.BlockSpec((1, chunk, dim), lambda i, n: (n[first + group], 0, 0))
    outs = [
        ((chunk, dim), F32, None, None),
        ((tokens - chunk + 16, dim), LOW, None, None),
        ((tokens, dim), F32, None, None),
    ] + [((tokens, padded), LOW, None, None)] * group
    if fine:
        made = (n_dp, 2, dim // group // 2 + 32, 2 * (wide // n_dp) // 3)
        outs += [hbm(made)] * (3 * group)
    else:
        outs += [((count, dim, block), LOW, None, None)] * 2 + [((dim, dim), LOW, None, None), ((16, dim), F32, None, None)]
    own = lambda *s: pltpu.VMEM(s, F32)
    low = lambda *s: pltpu.VMEM(s, LOW)
    return kernel_call(
        functools.partial(token_kernel, group=group, cols=cols, chunk=chunk, first_bias=first_bias, first=first, count=count, fine=fine),
        "token_work", (2 * count,), ins, specs, outs,
        [low(tokens, dim), own(tokens, dim), low(count, tokens, block), low(count, tokens, block), own(tokens, dim),
         own(tokens, LANES), low(tokens, dim), own(dim, dim), own(16, dim)]
        + ([low(*made)] * (3 * group) + [pltpu.SemaphoreType.DMA((6 * group,))] if fine else []),
        12 * tokens * dim * wide, 8 * dim * wide, 2 * tokens * wide, (plan,), 60)


def swap(values, name, mask):
    size = lax.axis_size(name)
    return lax.ppermute(values, name, [(i, i ^ mask) for i in range(size)])


def after(value, *first):
    return lax.optimization_barrier((value,) + first)[0]


def add_up(parts):
    return sum(p.astype(F32) for p in parts)


def split_bits(size):
    return (2,) * (size.bit_length() - 1)


class Cut:
    def __init__(self, array, kept=()):
        self.array, self.kept = array, dict(kept)

    def pick(self, axis, index):
        return Cut(self.array, {**self.kept, axis: index})

    def value(self):
        shape = [1 if d in self.kept else n for d, n in enumerate(self.array.shape)]
        return lax.dynamic_slice(self.array, [self.kept.get(d, 0) for d in range(len(shape))], shape)


class Halving:
    def __init__(self, parts, bits):
        self.parts = [[Cut(a) for a in (p if isinstance(p, list) else [p])] for p in parts]
        self.bits = bits
        self.sides = []

    def send(self, name, mask, *first):
        axis = self.bits[name, mask]
        bit = (lax.axis_index(name) // mask) % 2
        self.sent = self.join(self.parts, first, axis, 1 - bit)
        self.got = swap(self.sent, name, mask)
        self.parts = [[c.pick(axis, bit) for c in p] for p in self.parts] + [[Cut(self.got)]]
        if name == "seq":
            self.sides.append((mask, axis))

    def join(self, parts, first=(), axis=None, index=None):
        parts = [[c if axis is None else c.pick(axis, index) for c in p] for p in parts]
        if first:
            parts[0][0] = Cut(after(parts[0][0].array, *first), parts[0][0].kept)
        fine = max(parts, key=len)
        widths = [c.array.shape[-1] for c in fine]
        edges = [sum(widths[:i]) for i in range(len(widths) + 1)]

        def cut(p, i):
            at = 0
            for c in p:
                width = c.array.shape[-1]
                if at <= edges[i] and edges[i + 1] <= at + width:
                    value = c.value()
                    return value if width == widths[i] else value[..., edges[i] - at:edges[i + 1] - at]
                at += width
            raise ValueError(widths)

        sums = [add_up([cut(p, i) for p in parts]).astype(LOW) for i in range(len(widths))]
        return sums[0] if len(sums) == 1 else jnp.concatenate(sums, axis=-1)

    def finish(self, *first):
        return self.join(self.parts, first)

    def spread(self, piece):
        for mask, axis in reversed(self.sides):
            got = swap(piece, "seq", mask)
            bit = (lax.axis_index("seq") // mask) % 2
            piece = jnp.concatenate([jnp.where(bit == 0, piece, got), jnp.where(bit == 0, got, piece)], axis=axis)
        return piece


def abreast(*chains):
    both = Halving([[c.finish() for c in chains]], chains[0].bits)
    both.sides = list(chains[0].sides)
    return both


def join_kernel(plan, *refs, moves, merged, n_outs):
    n = sum(len(m) for m in moves)
    ins, refs = refs[:n], refs[n:]
    outs, held, sem = refs[:n_outs], refs[n_outs:n_outs + n], refs[-1]
    copies = []
    for i, (ref, (index, cols)) in enumerate(zip(ins, [p for m in moves for p in m])):
        at = tuple(
            slice(None) if k is None else pl.ds(0, 1) if k == 0 else pl.ds(lax.rem(plan[k[0]] + k[1], 2), 1) for k in index)
        copies.append(pltpu.make_async_copy(ref.at[at + (slice(None), cols)], held[i], sem.at[i]))
    for copy in copies:
        copy.start()
    at, col = 0, 0
    for i, parts in enumerate(moves):
        for copy in copies[at:at + len(parts)]:
            copy.wait()
        total = sum(r[...].astype(F32) for r in held[at:at + len(parts)]).astype(LOW)
        at += len(parts)
        if merged:
            outs[0][..., col:col + total.shape[-1]] = total
            col += total.shape[-1]
        else:
            outs[i][...] = total


def join_all(plan, chains, dims, merged=False, first=()):
    ins, outs, moves, scratch = [], [], [], []
    if first:
        plan = after(plan, *first)
    for chain, dim in zip(chains, dims):
        parts = [p[0] for p in chain.parts]
        kept = dict(parts[0].kept)
        if dim is not None:
            kept[dim[0]] = dim[1]
        shape = parts[0].array.shape
        size = tuple(1 if d in kept else n for d, n in enumerate(shape[:-2])) + shape[-2:]
        move = []
        for part in parts:
            array = part.array
            index = tuple(0 if array.shape[d] == 1 else kept.get(d) for d in range(array.ndim - 2))
            same = array.shape[-1] == shape[-1]
            move.append((index, slice(None) if same else pl.ds(len(moves) * shape[-1], shape[-1])))
            ins.append(array)
            scratch.append(pltpu.VMEM(size, LOW))
        moves.append(move)
        outs.append(size)
    if merged:
        outs = [outs[0][:-1] + (sum(o[-1] for o in outs),)]
    big = len(chains) > 2
    return pl.pallas_call(
        functools.partial(join_kernel, moves=moves, merged=merged, n_outs=len(outs)),
        grid_spec=pltpu.PrefetchScalarGridSpec(
            num_scalar_prefetch=1, grid=(1,), in_specs=[pl.BlockSpec(memory_space=pl.ANY)] * len(ins),
            out_specs=[pl.BlockSpec(o, lambda *_, n=len(o): (0,) * n, pipeline_mode=pl.Buffered(1)) for o in outs],
            scratch_shapes=scratch + [pltpu.SemaphoreType.DMA((len(ins),))]),
        out_shape=[jax.ShapeDtypeStruct(o, LOW) for o in outs],
        compiler_params=pltpu.CompilerParams(vmem_limit_bytes=(60 if big else 28) * MIB),
        cost_estimate=pl.CostEstimate(flops=1, bytes_accessed=1, transcendentals=0),
        name="join",
    )(plan, *ins)


def exchange(plan, places, chains, moves, *first):
    axes = [c.bits[m] for c, m in zip(chains, moves)]
    sents = join_all(plan, chains, [(axis, (places[m], 1)) for axis, m in zip(axes, moves)], first=first)
    for chain, (name, mask), axis, sent in zip(chains, moves, axes, sents):
        got = swap(sent, name, mask)
        chain.parts = [[c.pick(axis, (places[name, mask], 0)) for c in p] for p in chain.parts] + [[Cut(got)]]
    return sents


def exchange_merged(plan, places, chains, move, *first):
    axis = chains[0].bits[move]
    sent = join_all(plan, chains, [(axis, (places[move], 1))] * len(chains), merged=True, first=first)[0]
    got = swap(sent, *move)
    for chain in chains:
        chain.parts = [[c.pick(axis, (places[move], 0)) for c in p] for p in chain.parts] + [[Cut(got)]]
    return sent


def finish_kernel(plan, *refs, first, sources, pairs, unit):
    n = len(sources)
    pieces, rests, refs = refs[:n], refs[n:2 * n], refs[2 * n:]
    outer_ref, inner_ref, attn_ref, qkv_ref, bq_ref, bv_ref, *line_refs, vec_ref, turned, vec_qv = refs
    width, dim = outer_ref.shape
    share = attn_ref.shape[0]
    top, part = unit + 32, share // 2
    vec_ref[...] = jnp.zeros(vec_ref.shape, F32)
    vec_qv[...] = jnp.zeros(vec_qv.shape, F32)
    for (e, d), ref, rest in zip(sources, pieces, rests):
        member, side = plan[first + e], lax.rem(plan[first + 2] + d, 2)
        owner = member * 2 + side
        turned[pl.ds(pl.multiple_of(owner * unit, 8), unit), :] = ref[:unit, :width].astype(F32)
        for half in range(2):
            inner_ref[:, pl.ds(pl.multiple_of(owner * 2 * width + half * width, LANES), width)] = (
                ref[half * share:(half + 1) * share, width:].astype(F32))
        attn_ref[pl.ds(pl.multiple_of(owner * 24, 8), 24), :] = ref[unit:unit + 24, :].astype(F32)
        vec_ref[pl.ds(pl.multiple_of(side * 8, 8), 8), :] += ref[unit:top, :].astype(F32)[24:, :]
        rows = pl.ds(pl.multiple_of(side * part, 8), part)
        for block in range(3 * pairs + 1):
            values = rest[:, block * LANES:(block + 1) * LANES].astype(F32)
            if block == 3 * pairs:
                vec_qv[rows, :] += values
            else:
                j, i = divmod(block, 3)
                to = pl.multiple_of(i * dim + (member * pairs + j) * LANES, LANES)
                qkv_ref[rows, pl.ds(to, LANES)] = values
    outer_ref[...] = turned[...].T
    dp = plan[first + 3 + 4 + 4]
    here = pltpu.roll(vec_ref[...], lax.rem(dim - dp * share, dim), 1)
    for i, ref in enumerate(line_refs[:6]):
        ref[...] = here[i, :share]
    per = dim // width
    line_refs[6][...] = vec_ref[pl.ds(8 + dp // per, 1), pl.ds(pl.multiple_of(lax.rem(dp, per) * width, LANES), width)][0]
    bq_ref[...] = vec_qv[0, :share]
    bv_ref[...] = vec_qv[1, :share]


def finish(plan, pieces, rests, sources, first, pairs, unit, width, share, wide):
    dim = pieces[0].shape[1]
    return kernel_call(
        functools.partial(finish_kernel, first=first, sources=sources, pairs=pairs, unit=unit),
        "finish", (1,), (*pieces, *rests), [whole(a) for a in (*pieces, *rests)],
        [((width, dim), F32, None, None), ((share, wide), F32, None, None), ((share, dim), F32, None, None),
         ((share, 3 * dim), F32, None, None)]
        + [((share,), F32, None, None)] * 8 + [((width,), F32, None, None)],
        [pltpu.VMEM((16, dim), F32), pltpu.VMEM((dim, width), F32), pltpu.VMEM((share, LANES), F32)],
        0, 10 * dim * width, 0, (plan,), 16)


def by_owner(parts, member):
    stack = jnp.stack(parts)
    return [lax.dynamic_index_in_dim(stack, member ^ m, 0, keepdims=False) for m in range(len(parts))]


def body(hidden_in, passage_lengths, w_qkv, b_query, b_value, w_attn_out, b_attn_out, gain_attn,
         bias_attn, w_inner, b_inner, w_outer, b_outer, gain_ffn, bias_ffn, grad_out):
    rows, chunk, dim = hidden_in.shape
    n_dp, n_seq = lax.axis_size("dp"), lax.axis_size("seq")
    wide = w_inner.shape[1]
    slots = passage_lengths.shape[1]
    assert slots == SLOTS
    group = n_seq // rows
    seq = lax.axis_index("seq")
    side, member = seq // group, seq % group
    tokens = group * rows * chunk
    cols = HEADS // group * HEAD_DIM
    pairs = -(-cols // LANES)
    padded = pairs * LANES
    aligned = cols % LANES == 0
    count = rows * group
    share = dim // n_dp
    row_at = lambda a, d: lax.dynamic_index_in_dim(a, side ^ d, 0, keepdims=False)

    send = row_at(hidden_in, 1)
    got = swap(send, "seq", group)
    own = row_at(hidden_in, 0)
    cot_send = after(row_at(grad_out, 1), got)
    cot_got = swap(cot_send, "seq", group)

    start = jnp.stack([(side ^ d) * group + (member ^ e) for e in range(group) for d in range(rows)]).astype(jnp.int32)
    ends = jnp.cumsum(row_at(passage_lengths, 0), dtype=jnp.int32)
    segment = lambda p: jnp.sum((p[..., None] >= ends).astype(jnp.int32), axis=-1, dtype=jnp.int32)
    index = jnp.arange(count, dtype=jnp.int32)
    low_seg, high_seg = segment(index * chunk), segment(index * chunk + (chunk - 1))
    meets = (jnp.maximum(low_seg[:, None], low_seg[None, :]) <= jnp.minimum(high_seg[:, None], high_seg[None, :]))
    first_key = jnp.min(jnp.where(meets, index[None, :], count), axis=1)
    spans = jnp.max(jnp.where(meets, index[None, :], -1), axis=1) + 1 - first_key
    rounded = functools.reduce(lambda r, n: jnp.where(spans <= n, n, r), reversed(key_spans(count)), count)
    first_key = jnp.minimum(first_key, count - rounded)
    reorder = lambda a: jnp.sum(jnp.where(start[:, None] == index[None, :], a[None, :], 0), axis=1)
    per = wide // dim // group
    turns = [(member ^ e) * per + r for e in reversed(range(group)) for r in range(per)]
    moves = [("dp", 1 << b) for b in range(len(split_bits(n_dp)))] + [("seq", group)]
    members = jnp.stack([member ^ e for e in range(group)] + [side] + turns
                        + [(lax.axis_index(name) // mask) % 2 for name, mask in moves] + [lax.axis_index("dp")])
    plan = jnp.concatenate([ends, start, reorder(first_key), reorder(rounded), first_key, rounded, members]).astype(jnp.int32)
    first = SLOTS + 5 * count
    places = {m: first + group + 1 + len(turns) + i for i, m in enumerate(moves)}
    first_bias = 8
    vec = jnp.concatenate(
        [b_attn_out, gain_attn, bias_attn, b_outer, gain_ffn, bias_ffn, b_query, b_value, b_inner]
    ).astype(F32).reshape(-1, dim)
    if aligned:
        weights = [w_qkv] * 3, [lambda j, n, i=i: (0, i * group + n[first]) for i in range(3)] + [lambda j, n: (0, n[first])]
        vec_heads = vec
    else:
        widen = lambda a: jnp.pad(a, ((0, 0), (0, padded - cols)))
        weights_of = lambda m: [widen(lax.dynamic_slice_in_dim(w_qkv, m * cols + i * dim, cols, 1)) for i in range(3)]
        vec_heads = widen(lax.dynamic_slice_in_dim(vec, member * cols, cols, 1))
        weights = weights_of(member), [lambda j, n: (0, 0)] * 4

    chunks = [own, got]
    for e in range(1, group):
        chunks += [swap(own, "seq", e), swap(after(got, plan, vec), "seq", e)]

    o_mine, o_send, lse, q, k, v = attend(
        plan, chunks, weights, vec_heads, pairs, rows)
    apart = lambda a: [a] if group == 2 else [a[i * rows * chunk:(i + 1) * rows * chunk] for i in range(group - 1)]
    together = lambda a: a[0] if len(a) == 1 else jnp.concatenate(a, axis=0)
    o_parts = [o_mine] + [swap(a, "seq", e) for e, a in enumerate(apart(o_send), 1)]
    fine = aligned and (wide // n_dp) % LANES == 0 and share % 16 == 0 and per == rows and share == 24 * rows * group
    out_own, out_send, dh1, *made = token_work(
        plan, chunks[:rows], o_parts, w_attn_out, vec, w_inner, w_outer, grad_out, cot_got, cols, padded,
        first_bias, first, n_dp, fine)
    do_parts, made = made[:group], made[group:]
    do_gots = [swap(do_parts[e], "seq", e) for e in range(1, group)]
    out_got = swap(out_send, "seq", group)

    dp_masks = [1 << b for b in range(len(split_bits(n_dp)))]
    bit_shape = split_bits(n_dp) + split_bits(rows)
    bits = {("dp", m): len(dp_masks) - 1 - i for i, m in enumerate(dp_masks)}
    bits["seq", group] = len(dp_masks)

    unit, width = dim // group // rows, wide // n_dp
    if fine:
        feed_parts = made
    else:
        raw_outer, raw_inner, raw_attn, raw_vectors = made
        flat = lambda a: a.reshape(group, n_dp, rows, -1)
        feed_all = jnp.concatenate([
            flat(raw_outer.transpose(1, 0, 2).reshape(group, rows, unit, n_dp, width).transpose(0, 3, 1, 2, 4)),
            flat(raw_inner.transpose(1, 0, 2).reshape(n_dp, share, group, rows, -1).transpose(2, 0, 3, 1, 4)),
            flat(raw_attn.reshape(n_dp, group, rows, -1, dim).transpose(1, 0, 2, 3, 4))], axis=3)
        vectors = jnp.broadcast_to(raw_vectors.reshape(1, rows, -1), (n_dp, rows, 16 * dim // rows)).astype(LOW)
        feed_parts = [
            jnp.concatenate([lax.dynamic_index_in_dim(feed_all, member ^ e, 0, keepdims=False),
                             vectors if e == 0 else jnp.zeros_like(vectors)], axis=2).reshape(n_dp, rows, -1, LANES)
            for e in range(group)]
    ways = 3 if fine else 1
    shaped = lambda a: a.reshape(bit_shape + a.shape[2:])
    by_way = [[feed_parts[e * ways + i] for e in range(group)] for i in range(ways)]
    feeds = [Halving([shaped(p[0])] + [shaped(swap(after(p[e], *do_gots), "seq", e)) for e in range(1, group)], bits) for p in by_way]
    stages = [("dp", 1), ("seq", group), ("dp", 2)]

    def feed_stage(n, *before):
        moves = [stages[(n + i) % 3] for i in range(ways)]
        if fine:
            return exchange(plan, places, feeds, moves, *before)
        for f, move in zip(feeds, moves):
            f.send(*move, *before)
        return [f.sent for f in feeds]

    if fine:
        sent = []
        for f, move in zip(feeds, stages):
            sent = exchange(plan, places, [f], [move], *sent, *([out_got] if f is feeds[-1] else []))
    else:
        sent = feed_stage(0)

    runs = [(0, pairs)]
    part = share // rows
    packed_grads = lambda a: a.reshape(bit_shape + (part, a.shape[-1]))
    d_mine, d_other, small_qkv, *grad_qkv = attend_back(
        plan, chunks, q, k, v, do_parts[0], after(together(do_gots), *sent), o_mine, o_send, lse, pairs, rows,
        share if fine else 0, first)
    if fine:
        rests = [Halving([packed_grads(a)], bits) for a in grad_qkv]
    else:
        heads = lax.dynamic_update_slice_in_dim(jnp.zeros((2, dim), F32), small_qkv[:2, :cols], member * cols, 1)
        vectors = heads.reshape(2, n_dp, -1).transpose(1, 0, 2)
        vectors = jnp.pad(vectors, ((0, 0), (0, rows * part - 2), (0, LANES - share))).astype(LOW).reshape(n_dp, rows, part, LANES)
        rests = [Halving([[packed_grads(grad_qkv[0]), vectors.reshape(bit_shape + vectors.shape[2:])]], bits)]
    rest_moves = [[("dp", 2), ("dp", 1)], [("seq", group), ("dp", 2)], [("dp", 1), ("seq", group)]]
    dp_stages = [("dp", m) for m in dp_masks]

    def rest_stage(n, *before):
        moves = rest_moves[n] if n < 3 else [dp_stages[n - 1]] * 2
        if fine:
            return exchange(plan, places, rests, moves, *before)
        rests[0].send(*moves[0], *before)
        return [rests[0].sent]

    sent = feed_stage(1, d_mine)
    d_gots = [swap(after(a, *sent), "seq", e) for e, a in enumerate(apart(d_other), 1)]
    rest_sent = rest_stage(0, *sent)
    out_first = rest_sent

    runs_of = [[a] for a in [d_mine] + d_gots]
    if aligned:
        in_own, in_send = input_grads(plan, runs_of, runs, w_qkv, after(dh1, *rest_sent), pairs, chunk, first)
    else:
        grad_hidden = dh1
        for e, parts in enumerate(runs_of):
            w = weights_of(member ^ e)
            d = jnp.concatenate(parts, axis=1)
            for j in range(pairs):
                w_pair = jnp.concatenate([a[:, j * LANES:(j + 1) * LANES] for a in w], axis=1)
                grad_hidden = grad_hidden + dot_nt(d[:, j * 3 * LANES:(j + 1) * 3 * LANES], w_pair)
        in_own, in_send = grad_hidden[:chunk], grad_hidden[chunk:].astype(LOW)

    def in_place(own, got):
        return jnp.where(side == 0, jnp.stack([own, got]), jnp.stack([got, own]))

    sent = feed_stage(2, in_send)
    early = [feeds[0].parts[-1][0].array] if fine else sent
    if fine:
        last = ("dp", dp_masks[-1])
        rest_sent = rest_stage(1, *early)
        sent = exchange_merged(plan, places, feeds, last, *rest_sent)
        early = [sent]
        in_got = swap(after(in_send, sent), "seq", group)
        rest_stage(2, sent)
        late = [exchange_merged(plan, places, rests, last)]
    else:
        rest_sent = rest_stage(1, *sent)
        feed = feeds[0]
        in_got = swap(in_send, "seq", group)
        rest_sent = rest_stage(2, *rest_sent)
        for i, mask in enumerate(dp_masks[2:]):
            feed.send("dp", mask, *rest_sent)
            rest_sent = rest_stage(3 + i, feed.sent)
        late = rest_sent
        feed_piece, rest_piece = feed.finish(*late), rests[0].finish()
    out = in_place(after(out_own, *early), out_got[:chunk].astype(F32))
    sums = in_place(after(out_send, *early)[chunk:chunk + slots], out_got[chunk:chunk + slots])
    sums = add_up([sums] + [swap(sums, "seq", e) for e in range(1, group)])
    pooled = sums / jnp.maximum(passage_lengths.astype(F32), 1.0)[:, :, None]
    grad_in = in_place(after(in_own, *early), in_got.astype(F32))

    def everyone(piece):
        gots = [piece] + [swap(piece, "seq", e) for e in range(1, group)]
        return by_owner(gots, member)

    here = lambda a: lax.dynamic_slice_in_dim(a.reshape(-1), lax.axis_index("dp") * (a.size // n_dp), a.size // n_dp)
    if fine:
        sources = [(0, 0), (0, 1), (1, 0), (1, 1)]

        def from_all(piece):
            piece = piece.reshape(piece.shape[-2:])
            got = swap(piece, "seq", group)
            return [piece, got, swap(piece, "seq", 1), swap(got, "seq", 1)]

        feed_piece = join_all(plan, feeds, [None] * ways, merged=True, first=late + [grad_in, pooled, out])[0]
        pieces_of = [from_all(feed_piece)]
        rest_piece = join_all(plan, rests, [None] * 2, merged=True, first=[pieces_of[0][1]])[0]
        pieces_of.append(from_all(rest_piece))
        (grad_w_outer, grad_w_inner, grad_w_attn_out, grad_w_qkv, grad_b_query, grad_b_value, grad_gain_ffn,
         grad_bias_ffn, grad_b_outer, grad_gain_attn, grad_bias_attn, grad_b_attn_out, grad_b_inner) = finish(
            plan, pieces_of[0], pieces_of[1], sources, first, pairs, unit, width, share, wide)
    else:
        feed_pieces = everyone(feed.spread(feed_piece))
        sizes = [unit * width, share * (wide // group // rows), share * dim // group // rows, 16 * dim // rows]
        ends_of = [sum(sizes[:i]) for i in range(5)]
        cut = lambda a, i: a.reshape(rows, -1)[:, ends_of[i]:ends_of[i + 1]]
        grad_w_outer = jnp.concatenate([cut(a, 0).reshape(rows * unit, width) for a in feed_pieces]).T.astype(F32)
        grad_w_inner = jnp.concatenate(
            [cut(a, 1).reshape(rows, share, -1)[r] for a in feed_pieces for r in range(rows)], axis=1).astype(F32)
        grad_w_attn_out = jnp.concatenate([cut(a, 2).reshape(-1, dim) for a in feed_pieces], axis=0).astype(F32)
        totals = add_up([cut(a, 3) for a in feed_pieces]).reshape(16, dim)
        rest_pieces = [a.reshape(share, -1) for a in everyone(rests[0].spread(rest_piece))]
        grad_w_qkv = jnp.concatenate(
            [jnp.concatenate([a[:, (3 * j + i) * LANES:(3 * j + i + 1) * LANES] for j in range(pairs)], axis=1)[:, :cols]
             for i in range(3) for a in rest_pieces], axis=1).astype(F32)
        sums_qv = add_up([a[:, 3 * padded:] for a in rest_pieces])
        (grad_gain_ffn, grad_bias_ffn, grad_b_outer, grad_gain_attn, grad_bias_attn, grad_b_attn_out) = [
            here(totals[i]) for i in range(6)]
        grad_b_inner = here(totals[8:8 + wide // dim])
        grad_b_query, grad_b_value = sums_qv[0, :share], sums_qv[1, :share]

    return (out, pooled, grad_in, grad_w_qkv, grad_b_query, grad_b_value, grad_w_attn_out,
            grad_b_attn_out, grad_gain_attn, grad_bias_attn, grad_w_inner, grad_b_inner,
            grad_w_outer, grad_b_outer, grad_gain_ffn, grad_bias_ffn)


def solution(mesh):
    tokens, rows, all_of = P("dp", "seq", None), P("dp", None), P()
    vector, cube = P("dp"), P("dp", None, None)
    return jax.shard_map(
        body,
        mesh=mesh,
        in_specs=(tokens, rows) + (all_of,) * 13 + (tokens,),
        out_specs=(tokens, cube, tokens, rows, vector, vector, rows, vector, vector, vector, rows,
                   vector, rows, vector, vector, vector),
        check_vma=False,
    )
```

```python
import functools
import math

import jax
import jax.numpy as jnp
from jax import lax
from jax.experimental import pallas as pl
from jax.experimental.pallas import tpu as pltpu
from jax.sharding import PartitionSpec as P

LOW = jnp.bfloat16
F32 = jnp.float32
HEADS = 12
HEAD_DIM = 64
LANES = 128
MIB = 1024 * 1024
MASKED = -1e30
EPS = 1e-12
COST = 1000
SLOTS = 8
HALF_ROOT = math.sqrt(0.5)
PHI_SCALE = 1.0 / math.sqrt(2.0 * math.pi)


def dot(left, right):
    return jnp.dot(left, right, preferred_element_type=F32)


def dot_nt(left, right):
    return lax.dot_general(left, right, (((1,), (1,)), ((), ())), preferred_element_type=F32)


def dot_tn(left, right):
    return lax.dot_general(left, right, (((0,), (0,)), ((), ())), preferred_element_type=F32)


def head_lanes(shape, head):
    lane = lax.rem(lax.broadcasted_iota(jnp.int32, shape, 1), LANES)
    return (lane >= HEAD_DIM) if head else (lane < HEAD_DIM)


def spread(column, width):
    return jnp.concatenate([column] * (width // LANES), axis=1)


def segments(plan, shape, axis, start=0):
    place = lax.broadcasted_iota(jnp.int32, shape, axis) + start
    return sum((place >= plan[j]).astype(jnp.int32) for j in range(SLOTS))


def whole(array, buffers=1):
    return pl.BlockSpec(array.shape, lambda *_: (0,) * array.ndim, pipeline_mode=pl.Buffered(buffers))


def kernel_call(body, name, grid, ins, in_specs, outs, scratch, flops, moved, exps=0, prefetch=(), limit=24):
    spec = pltpu.PrefetchScalarGridSpec(
        num_scalar_prefetch=len(prefetch),
        grid=grid,
        in_specs=in_specs,
        out_specs=[
            pl.BlockSpec(memory_space=pltpu.HBM) if b == "hbm" else pl.BlockSpec(b, m) if b else pl.BlockSpec(s, lambda *_, n=len(s): (0,) * n, pipeline_mode=pl.Buffered(1))
            for s, _, b, m in outs
        ],
        scratch_shapes=scratch,
    )
    return pl.pallas_call(
        body,
        grid_spec=spec,
        out_shape=[jax.ShapeDtypeStruct(s, t) for s, t, _, _ in outs],
        compiler_params=pltpu.CompilerParams(vmem_limit_bytes=limit * MIB),
        cost_estimate=pl.CostEstimate(flops=int(flops) // COST, bytes_accessed=int(moved) // COST, transcendentals=int(exps) // COST),
        name=name,
    )(*prefetch, *ins)


def key_spans(count):
    return list(range(2, 2 * count + 1)) if count <= 4 else [n for n in (2, 4, 8, 16, 32) if n <= 2 * count]


def turn(block):
    return block.T.astype(LOW)


def in_place_of(ref, chunk):
    return pl.ds(pl.multiple_of(ref * chunk, chunk), chunk)


def attend_kernel(plan, *refs, block, count, near, pairs):
    chunks, refs = refs[:count], refs[count:]
    (wq_ref, wk_ref, wv_ref, vec_ref, om_ref, os_ref, lse_ref, q_out, k_out, v_out,
     q, k, v, o, qt, km, vm, segk_ref, segq_ref, sem) = refs
    width = pairs * LANES
    segk_ref[...] = segments(plan, segk_ref.shape, 0)
    segq_ref[...] = segments(plan, segq_ref.shape, 1)
    lse_ref[...] = jnp.zeros(lse_ref.shape, F32)
    w = jnp.concatenate([wq_ref[...], wk_ref[...], wv_ref[...]], axis=1)
    bias_q, bias_v = vec_ref[6:7, :], vec_ref[7:8, :]
    for i in range(count):
        at = in_place_of(plan[SLOTS + i], block)
        made = dot(chunks[i][...], w)
        q_low = (made[:, :width] + bias_q).astype(LOW).astype(F32) * HEAD_DIM ** (-0.5)
        k_low = made[:, width:2 * width].astype(LOW)
        v_low = (made[:, 2 * width:] + bias_v).astype(LOW)
        q[at, :] = q_low.astype(LOW)
        k[at, :] = k_low
        v[at, :] = v_low
        qt[:, at] = turn(q_low)
        for h in range(2):
            lanes = head_lanes((block, width), h)
            km[h, at, :] = jnp.where(lanes, k_low, jnp.zeros((), LOW))
            vm[h, at, :] = jnp.where(lanes, v_low, jnp.zeros((), LOW))
    copies = [pltpu.make_async_copy(a, b, sem.at[i]) for i, (a, b) in enumerate([(q, q_out), (k, k_out), (v, v_out)])]
    for copy in copies:
        copy.start()

    def one_block(j, carry):
        cols = in_place_of(plan[SLOTS + j], block)
        for span in key_spans(count):
            @pl.when(plan[SLOTS + 2 * count + j] == span)
            def _():
                rows = pl.ds(pl.multiple_of(plan[SLOTS + count + j] * (block // 2), block // 2), span * (block // 2))
                same = spread(segk_ref[rows, :], block) == segq_ref[0:1, cols]
                made, totals = [], []
                for i in range(pairs):
                    pair = slice(i * LANES, (i + 1) * LANES)
                    for h in range(2):
                        s = jnp.where(same, dot(km[h, rows, pair], qt[pair, cols]), MASKED)
                        top = jnp.max(s, axis=0, keepdims=True)
                        p = jnp.exp(s - top)
                        total = jnp.sum(p, axis=0, keepdims=True)
                        made.append(dot_tn(p.astype(LOW), vm[h, rows, pair]))
                        totals.append(total)
                        lse_ref[2 * i + h:2 * i + h + 1, cols] = top + jnp.log(total)
                totals += [jnp.ones((1, block), F32)] * (-len(totals) % 8)
                scale = (1.0 / jnp.concatenate(totals, axis=0)).T
                for i in range(pairs):
                    both = made[2 * i] * scale[:, 2 * i:2 * i + 1] + made[2 * i + 1] * scale[:, 2 * i + 1:2 * i + 2]
                    o[in_place_of(j, block), i * LANES:(i + 1) * LANES] = both.astype(LOW)
        return carry

    lax.fori_loop(0, count, one_block, 0)
    copies += [pltpu.make_async_copy(o.at[pl.ds(0, near * block)], om_ref, sem.at[3]),
               pltpu.make_async_copy(o.at[pl.ds(near * block, (count - near) * block)], os_ref, sem.at[4])]
    for copy in copies[3:]:
        copy.start()
    for copy in copies:
        copy.wait()


def hbm(shape):
    return (shape, LOW, "hbm", None)


def attend(plan, chunks, weights, vec, pairs, near):
    block = chunks[0].shape[0]
    count = len(chunks)
    tokens = block * count
    width = pairs * LANES
    arrays, maps = weights
    low = lambda *s: pltpu.VMEM(s, LOW)
    return kernel_call(
        functools.partial(attend_kernel, block=block, count=count, near=near, pairs=pairs),
        "attend", (1,),
        (*chunks, *arrays, vec),
        [whole(c) for c in chunks]
        + [pl.BlockSpec((arrays[0].shape[0], width), m, pipeline_mode=pl.Buffered(1)) for m in maps[:3]]
        + [pl.BlockSpec((vec.shape[0], width), maps[3], pipeline_mode=pl.Buffered(1))],
        [
            hbm((near * block, width)), hbm((tokens - near * block, width)),
            ((8, tokens), F32, None, None),
            hbm((tokens, width)), hbm((tokens, width)), hbm((tokens, width)),
        ],
        [low(tokens, width), low(tokens, width), low(tokens, width), low(tokens, width), low(width, tokens), low(2, tokens, width),
         low(2, tokens, width), pltpu.VMEM((tokens, LANES), jnp.int32),
         pltpu.VMEM((8, tokens), jnp.int32), pltpu.SemaphoreType.DMA((5,))],
        4 * tokens * tokens * width, 20 * tokens * width, 2 * tokens * tokens * pairs, (plan,), 60)


def attend_back_kernel(plan, *refs, block, count, near, pairs, owned, first):
    chunks, refs = refs[:count], refs[count:]
    (q_in, k_in, v_in, dm_in, do_in, lse_ref, gm_ref, go_ref, small_ref), refs = refs[:9], refs[9:]
    gw_refs, refs = refs[:2 if owned else 1], refs[2 if owned else 1:]
    (hidden, q, k, v, given, qt, dt, km, vm, qm, dom, dq, dk, dv, joined, segk_ref, segq_ref, sem) = refs
    tokens, width = q.shape
    head, tail = pl.ds(0, near * block), pl.ds(near * block, tokens - near * block)
    order = [(dm_in, given.at[head]), (do_in, given.at[tail]), (q_in, q), (k_in, k), (v_in, v)]
    order += [(c, hidden.at[pl.ds(i * block, block)]) for i, c in enumerate(chunks)]
    copies = [pltpu.make_async_copy(a, b, sem.at[i]) for i, (a, b) in enumerate(order)]
    for copy in copies:
        copy.start()
    segk_ref[...] = segments(plan, segk_ref.shape, 0)
    segq_ref[...] = segments(plan, segq_ref.shape, 1)
    dk[...] = jnp.zeros(dk.shape, F32)
    dv[...] = jnp.zeros(dv.shape, F32)
    zero = jnp.zeros((), LOW)
    lanes = [head_lanes((block, width), h) for h in range(2)]
    for copy in copies[:2]:
        copy.wait()
    for i in range(count):
        at = in_place_of(plan[SLOTS + i], block)
        rows = given[i * block:(i + 1) * block, :]
        dt[:, at] = turn(rows.astype(F32))
        for h in range(2):
            dom[h, at, :] = jnp.where(lanes[h], rows, zero)
    for copy in copies[2:5]:
        copy.wait()
    for i in range(count):
        fixed = slice(i * block, (i + 1) * block)
        qt[:, fixed] = turn(q[fixed, :].astype(F32))
        for h in range(2):
            km[h, fixed, :] = jnp.where(lanes[h], k[fixed, :], zero)
            vm[h, fixed, :] = jnp.where(lanes[h], v[fixed, :], zero)
            qm[h, fixed, :] = jnp.where(lanes[h], q[fixed, :], zero)

    def one_block(j, carry):
        cols = in_place_of(j, block)
        for span in key_spans(count):
            @pl.when(plan[SLOTS + 4 * count + j] == span)
            def _():
                rows = pl.ds(pl.multiple_of(plan[SLOTS + 3 * count + j] * (block // 2), block // 2), span * (block // 2))
                same = spread(segk_ref[rows, :], block) == segq_ref[0:1, cols]
                for p in range(pairs):
                    pair = slice(p * LANES, (p + 1) * LANES)
                    dk_add, dv_add, dq_add = 0.0, 0.0, 0.0
                    for h in range(2):
                        n = 2 * p + h
                        s = jnp.where(same, dot(km[h, rows, pair], qt[pair, cols]), MASKED)
                        e = jnp.exp(s - lse_ref[n:n + 1, cols])
                        weighed = e * dot(vm[h, rows, pair], dt[pair, cols])
                        ds = (weighed - e * jnp.sum(weighed, axis=0, keepdims=True)).astype(LOW)
                        dv_add += dot(e.astype(LOW), dom[h, cols, pair])
                        dk_add += dot(ds, qm[h, cols, pair])
                        dq_add += dot_tn(ds, km[h, rows, pair])
                    dv[rows, pair] += dv_add
                    dk[rows, pair] += dk_add
                    dq[cols, pair] = dq_add * HEAD_DIM ** (-0.5)
        return carry

    lax.fori_loop(0, count, one_block, 0)
    small_ref[...] = jnp.zeros(small_ref.shape, F32)
    for i in range(count):
        at = in_place_of(plan[SLOTS + i], block)
        parts = [a[at, :].astype(LOW) for a in (dq, dk, dv)]
        small_ref[0:1, :] += jnp.sum(parts[0].astype(F32), axis=0, keepdims=True)
        small_ref[1:2, :] += jnp.sum(parts[2].astype(F32), axis=0, keepdims=True)
        columns = jnp.concatenate(
            [a[:, p * LANES:(p + 1) * LANES] for p in range(pairs) for a in parts], axis=1)
        joined[i * block:(i + 1) * block, :] = columns
    leaving = [pltpu.make_async_copy(joined.at[head], gm_ref, sem.at[count + 5]),
               pltpu.make_async_copy(joined.at[tail], go_ref, sem.at[count + 6])]
    for copy in leaving:
        copy.start()
    for copy in copies[5:]:
        copy.wait()
    made = dot_tn(hidden[...], joined[...]).astype(LOW)
    for copy in leaving:
        copy.wait()
    if owned:
        half = gw_refs[0].shape[1]
        gw_refs[0][...] = made[:, :half]
        gw_refs[1][:, :3 * width - half] = made[:, half:]
        gw_refs[1][:, 3 * width - half:] = jnp.zeros((made.shape[0], LANES), LOW)
        for t in range(width // owned):
            piece = jnp.pad(small_ref[0:2, t * owned:(t + 1) * owned], ((0, 14), (0, LANES - owned)))
            at = pl.multiple_of((plan[first] * (width // owned) + t) * owned, 16)
            gw_refs[1][pl.ds(at, 16), 3 * width - half:] = piece.astype(LOW)
    else:
        gw_refs[0][...] = made


def attend_back(plan, chunks, q, k, v, d_mine, d_others, lse, pairs, near, owned, first):
    block = chunks[0].shape[0]
    count = len(chunks)
    tokens = block * count
    width = pairs * LANES
    dim = chunks[0].shape[1]
    low = lambda *s: pltpu.VMEM(s, LOW)
    wide = lambda *s: pltpu.VMEM(s, F32)
    anywhere = pl.BlockSpec(memory_space=pl.ANY)
    return kernel_call(
        functools.partial(attend_back_kernel, block=block, count=count, near=near, pairs=pairs, owned=owned, first=first),
        "attend_back", (1,),
        (*chunks, q, k, v, d_mine, d_others, lse),
        [anywhere] * (count + 5) + [whole(lse)],
        [
            hbm((d_mine.shape[0], 3 * width)), hbm((d_others.shape[0], 3 * width)),
            ((8, width), F32, None, None),
        ] + [((dim, n), LOW, None, None) for n in ([(3 * width + LANES) // 2] * 2 if owned else [3 * width])],
        [low(tokens, dim), low(tokens, width), low(tokens, width), low(tokens, width), low(tokens, width),
         low(width, tokens), low(width, tokens), low(2, tokens, width), low(2, tokens, width),
         low(2, tokens, width), low(2, tokens, width),
         wide(tokens, width), wide(tokens, width), wide(tokens, width), low(tokens, 3 * width),
         pltpu.VMEM((tokens, LANES), jnp.int32), pltpu.VMEM((8, tokens), jnp.int32), pltpu.SemaphoreType.DMA((count + 7,))],
        10 * tokens * tokens * width, 30 * tokens * width, 2 * tokens * tokens * pairs, (plan,), 60)


def input_kernel(plan, *refs, group, runs, pairs, first):
    n = group * len(runs)
    d_ins, (w_in, dh_in, own_ref, sent_ref), held, (w_held, total, sem) = refs[:n], refs[n:n + 4], refs[n + 4:2 * n + 4], refs[2 * n + 4:]
    dim = w_in.shape[0]
    w_copies, copies = [], []
    for e in range(group):
        base = pl.multiple_of(plan[first + e] * pairs * LANES, LANES)
        for i in range(3):
            w_copies.append(pltpu.make_async_copy(
                w_in.at[:, pl.ds(base + i * dim, pairs * LANES)], w_held.at[3 * e + i], sem.at[3 * e + i]))
    for i in range(n):
        copies.append(pltpu.make_async_copy(d_ins[i], held[i], sem.at[3 * group + i]))
    last = pltpu.make_async_copy(dh_in, total, sem.at[3 * group + n])
    per = len(runs)
    for e in range(group):
        for copy in w_copies[3 * e:3 * e + 3] + copies[per * e:per * e + per]:
            copy.start()
    last.start()
    made = 0.0
    for e in range(group):
        for copy in w_copies[3 * e:3 * e + 3] + copies[per * e:per * e + per]:
            copy.wait()
        d = jnp.concatenate([held[per * e + r][...] for r in range(per)], axis=1)
        w = jnp.concatenate(
            [w_held[3 * e + i, :, j * LANES:(j + 1) * LANES] for j in range(pairs) for i in range(3)], axis=1)
        made += dot_nt(d, w)
    last.wait()
    made += total[...]
    chunk = own_ref.shape[0]
    own_ref[...] = made[:chunk]
    sent_ref[...] = made[chunk:].astype(LOW)


def input_grads(plan, d_parts, runs, w, dh, pairs, chunk, first):
    tokens, dim = dh.shape
    group = len(d_parts)
    ins = (*[d for parts in d_parts for d in parts], w, dh)
    return kernel_call(
        functools.partial(input_kernel, group=group, runs=runs, pairs=pairs, first=first), "input_grads", (1,), ins,
        [pl.BlockSpec(memory_space=pltpu.HBM)] * len(ins),
        [((chunk, dim), F32, None, None), ((tokens - chunk, dim), LOW, None, None)],
        [pltpu.VMEM(d.shape, LOW) for parts in d_parts for d in parts]
        + [pltpu.VMEM((3 * group, dim, pairs * LANES), LOW), pltpu.VMEM((tokens, dim), F32),
           pltpu.SemaphoreType.DMA((len(ins) - 2 + 3 * group + 1,))],
        6 * tokens * dim * dim, 6 * dim * dim + 10 * tokens * dim, 0, (plan,), 60)


def row_mean(values):
    return jnp.mean(values, axis=-1, keepdims=True)


def normal(values):
    centre = values - row_mean(values)
    scale = lax.rsqrt(row_mean(centre * centre) + EPS)
    return centre * scale, scale


def normal_back(hat, scale, grads):
    return scale * (grads - row_mean(grads) - hat * row_mean(grads * hat))


def head_rows(ref, owner, cols):
    return ref[pl.ds(pl.multiple_of(owner * cols, 16), cols), :]


def token_kernel(plan, *refs, group, cols, chunk, first_bias, first, count, fine):
    x_refs, o_refs, refs = refs[:2], refs[2:2 + group], refs[2 + group:]
    wa_ref, vec_ref, wi_ref, wo_ref, go_ref, gg_ref, own_ref, sent_ref, dh_ref = refs[:9]
    do_refs, refs = refs[9:9 + group], refs[9 + group:]
    if fine:
        dest_out, refs = refs[:3 * group], refs[3 * group:]
        held, sem, refs = refs[-1 - 3 * group:-1], refs[-1], refs[:-1 - 3 * group]
        dest = [held[3 * e:3 * e + 3] for e in range(group)]
    else:
        (outer_ref, inner_ref, attn_ref, vector_ref), refs = refs[:4], refs[4:]
    yl, acc, g, slope, hat1, scale1, dz, attn, vectors = refs
    step = pl.program_id(0)
    tokens, dim = acc.shape
    total = lambda values: jnp.sum(values, axis=0, keepdims=True)

    def put(refs, d, r, rows, first_col, values):
        third, end = refs[0].shape[3], first_col + values.shape[1]
        for i, ref in enumerate(refs):
            low, high = max(first_col, i * third), min(end, (i + 1) * third)
            if low < high:
                ref[d, r, rows, low - i * third:high - i * third] = values[:, low - first_col:high - first_col]

    @pl.when(step == 0)
    def _():
        x = jnp.concatenate([r[...] for r in x_refs], axis=0)
        h1 = x.astype(F32) + vec_ref[0:1, :]
        for e in range(group):
            h1 += dot(o_refs[e][:, :cols], head_rows(wa_ref, plan[first + e], cols))
        hat, scale = normal(h1)
        y1 = hat * vec_ref[1:2, :] + vec_ref[2:3, :]
        hat1[...] = hat
        scale1[...] = jnp.broadcast_to(scale, scale1.shape)
        yl[...] = y1.astype(LOW)
        acc[...] = y1 + vec_ref[3:4, :]
        vectors[...] = jnp.zeros(vectors.shape, F32)

    @pl.when(step < count)
    def _():
        u = dot(yl[...], wi_ref[...]) + vec_ref[pl.ds(first_bias + step, 1), :]
        cdf = 0.5 * (1.0 + lax.erf(u * HALF_ROOT))
        low = (u * cdf).astype(LOW)
        g[step] = low
        slope[step] = (cdf + u * (PHI_SCALE * jnp.exp(-0.5 * u * u))).astype(LOW)
        acc[...] += dot(low, wo_ref[...])

    @pl.when(step == count - 1)
    def _():
        hat, scale = normal(acc[...])
        gain = vec_ref[4:5, :]
        out = hat * gain + vec_ref[5:6, :]
        high = out.astype(LOW)
        own_ref[...] = out[:chunk]
        slots = sent_ref.shape[0] - (tokens - chunk)
        place = lax.broadcasted_iota(jnp.int32, (slots, tokens), 0)
        segs = jnp.concatenate(
            [segments(plan, (slots, chunk), 1, plan[SLOTS + i] * chunk) for i in range(tokens // chunk)], axis=1)
        onehot = (place == segs).astype(LOW)
        rest = (out - high.astype(F32)).astype(LOW)
        sent_ref[:tokens - chunk, :] = high[chunk:]
        sent_ref[tokens - chunk:, :] = (dot(onehot, high) + dot(onehot, rest)).astype(LOW)
        dy = jnp.concatenate([go_ref[0], gg_ref[...]], axis=0).astype(F32)
        dh = normal_back(hat, scale, dy * gain)
        low = dh.astype(LOW)
        dz[...] = low
        acc[...] = dh
        vectors[0:1, :] = total(dy * hat)
        vectors[1:2, :] = total(dy)
        vectors[2:3, :] = total(low.astype(F32))

    @pl.when(step >= count)
    def _():
        b = plan[first + group + 1 + step - count]
        du = (dot_nt(dz[...], wo_ref[...]) * slope[b].astype(F32)).astype(LOW)
        vectors[pl.ds(8 + b, 1), :] = total(du.astype(F32))
        inner = dot_tn(yl[...], du).astype(LOW)
        if fine:
            per, unit, width = count // group, dest[0][0].shape[2] - 32, dest[0][0].shape[3] * 3 // 2
            share = unit // 2
            for e in range(group):
                member_cols = pl.ds(pl.multiple_of(plan[first + e] * (dim // group), LANES), dim // group)
                outer = dot_tn(dz[:, member_cols], g[b]).astype(LOW)
                for i in range(dim // width):
                    for r in range(per):
                        put(dest[e], b * (dim // width) + i, r, slice(0, unit), 0,
                            outer[r * unit:(r + 1) * unit, i * width:(i + 1) * width])

                @pl.when((step - count) // per == group - 1 - e)
                def _():
                    r = lax.rem(step - count, per)
                    for d in range(dest[e][0].shape[0]):
                        for half in range(2):
                            put(dest[e], d, r, slice(half * share, (half + 1) * share), width,
                                inner[d * share:(d + 1) * share, half * width:(half + 1) * width])
        else:
            outer_ref[b] = dot_tn(dz[...], g[b]).astype(LOW)
            inner_ref[b] = inner
        acc[...] += dot_nt(du, wi_ref[...])

    def leave(rows, start):
        return [pltpu.make_async_copy(a.at[:, :, rows], b.at[:, :, rows], sem.at[start + i])
                for i, (a, b) in enumerate(zip(held, dest_out))]

    @pl.when(step == pl.num_programs(0) - 1)
    def _():
        if fine:
            unit = held[0].shape[2] - 32
            copies = leave(pl.ds(0, unit), 0)
            for copy in copies:
                copy.start()
        hat = hat1[...]
        dy = acc[...]
        dh = normal_back(hat, scale1[:, 0:1], dy * vec_ref[1:2, :])
        dh_ref[...] = dh
        da = dh.astype(LOW)
        for e in range(group):
            made = dot_nt(da, head_rows(wa_ref, plan[first + e], cols)).astype(LOW)
            if do_refs[e].shape[1] > cols:
                do_refs[e][...] = jnp.zeros(do_refs[e].shape, LOW)
            do_refs[e][:, :cols] = made
            attn[pl.ds(pl.multiple_of(plan[first + e] * cols, 8), cols), :] = dot_tn(o_refs[e][:, :cols], da)
        vectors[3:4, :] = total(dy * hat)
        vectors[4:5, :] = total(dy)
        vectors[5:6, :] = total(da.astype(F32))
        if fine:
            n_dp, sides, unit = dest[0][0].shape[0], dest[0][0].shape[1], dest[0][0].shape[2] - 32
            for e in range(group):
                for d in range(n_dp):
                    for r in range(sides):
                        at = d * (dim // n_dp) + plan[first + e] * (24 * sides) + r * 24
                        tail = vectors[8 * r:8 * r + 8, :] if e == 0 else jnp.zeros((8, dim), F32)
                        both = jnp.concatenate([attn[pl.ds(pl.multiple_of(at, 8), 24), :], tail], axis=0)
                        put(dest[e], d, r, slice(unit, unit + 32), 0, both.astype(LOW))
            copies += leave(pl.ds(unit, 32), 3 * group)
            for copy in copies[3 * group:]:
                copy.start()
            for copy in copies:
                copy.wait()
        else:
            attn_ref[...] = attn[...].astype(LOW)
            vector_ref[...] = vectors[...]


def token_work(plan, x_parts, o_parts, wa, vec, wi, wo, grad_out, grad_got, cols, padded, first_bias, first, n_dp, fine):
    chunk, dim = x_parts[0].shape
    tokens = 2 * chunk
    wide = wi.shape[1]
    block = dim
    count = wide // block
    group = len(o_parts)
    ins = (*x_parts, *o_parts, wa, vec, wi, wo, grad_out, grad_got)
    specs = [whole(a) for a in ins]
    which = lambda i, n: jnp.where(i < count, i, n[first + group + 1 + jnp.maximum(i - count, 0)])
    specs[-4] = pl.BlockSpec((dim, block), lambda i, n: (0, which(i, n)))
    specs[-3] = pl.BlockSpec((block, dim), lambda i, n: (which(i, n), 0))
    specs[-2] = pl.BlockSpec((1, chunk, dim), lambda i, n: (n[first + group], 0, 0))
    outs = [
        ((chunk, dim), F32, None, None),
        ((tokens - chunk + 16, dim), LOW, None, None),
        ((tokens, dim), F32, None, None),
    ] + [((tokens, padded), LOW, None, None)] * group
    if fine:
        made = (n_dp, 2, dim // group // 2 + 32, 2 * (wide // n_dp) // 3)
        outs += [hbm(made)] * (3 * group)
    else:
        outs += [((count, dim, block), LOW, None, None)] * 2 + [((dim, dim), LOW, None, None), ((16, dim), F32, None, None)]
    own = lambda *s: pltpu.VMEM(s, F32)
    low = lambda *s: pltpu.VMEM(s, LOW)
    return kernel_call(
        functools.partial(token_kernel, group=group, cols=cols, chunk=chunk, first_bias=first_bias, first=first, count=count, fine=fine),
        "token_work", (2 * count,), ins, specs, outs,
        [low(tokens, dim), own(tokens, dim), low(count, tokens, block), low(count, tokens, block), own(tokens, dim),
         own(tokens, LANES), low(tokens, dim), own(dim, dim), own(16, dim)]
        + ([low(*made)] * (3 * group) + [pltpu.SemaphoreType.DMA((6 * group,))] if fine else []),
        12 * tokens * dim * wide, 8 * dim * wide, 2 * tokens * wide, (plan,), 60)


def swap(values, name, mask):
    size = lax.axis_size(name)
    return lax.ppermute(values, name, [(i, i ^ mask) for i in range(size)])


def after(value, *first):
    return lax.optimization_barrier((value,) + first)[0]


def add_up(parts):
    return sum(p.astype(F32) for p in parts)


def split_bits(size):
    return (2,) * (size.bit_length() - 1)


class Cut:
    def __init__(self, array, kept=()):
        self.array, self.kept = array, dict(kept)

    def pick(self, axis, index):
        return Cut(self.array, {**self.kept, axis: index})

    def value(self):
        shape = [1 if d in self.kept else n for d, n in enumerate(self.array.shape)]
        return lax.dynamic_slice(self.array, [self.kept.get(d, 0) for d in range(len(shape))], shape)


class Halving:
    def __init__(self, parts, bits):
        self.parts = [[Cut(a) for a in (p if isinstance(p, list) else [p])] for p in parts]
        self.bits = bits
        self.sides = []

    def send(self, name, mask, *first):
        axis = self.bits[name, mask]
        bit = (lax.axis_index(name) // mask) % 2
        self.sent = self.join(self.parts, first, axis, 1 - bit)
        self.got = swap(self.sent, name, mask)
        self.parts = [[c.pick(axis, bit) for c in p] for p in self.parts] + [[Cut(self.got)]]
        if name == "seq":
            self.sides.append((mask, axis))

    def join(self, parts, first=(), axis=None, index=None):
        parts = [[c if axis is None else c.pick(axis, index) for c in p] for p in parts]
        if first:
            parts[0][0] = Cut(after(parts[0][0].array, *first), parts[0][0].kept)
        fine = max(parts, key=len)
        widths = [c.array.shape[-1] for c in fine]
        edges = [sum(widths[:i]) for i in range(len(widths) + 1)]

        def cut(p, i):
            at = 0
            for c in p:
                width = c.array.shape[-1]
                if at <= edges[i] and edges[i + 1] <= at + width:
                    value = c.value()
                    return value if width == widths[i] else value[..., edges[i] - at:edges[i + 1] - at]
                at += width
            raise ValueError(widths)

        sums = [add_up([cut(p, i) for p in parts]).astype(LOW) for i in range(len(widths))]
        return sums[0] if len(sums) == 1 else jnp.concatenate(sums, axis=-1)

    def finish(self, *first):
        return self.join(self.parts, first)

    def spread(self, piece):
        for mask, axis in reversed(self.sides):
            got = swap(piece, "seq", mask)
            bit = (lax.axis_index("seq") // mask) % 2
            piece = jnp.concatenate([jnp.where(bit == 0, piece, got), jnp.where(bit == 0, got, piece)], axis=axis)
        return piece


def abreast(*chains):
    both = Halving([[c.finish() for c in chains]], chains[0].bits)
    both.sides = list(chains[0].sides)
    return both


def join_kernel(plan, *refs, moves, merged, n_outs):
    n = sum(len(m) for m in moves)
    ins, refs = refs[:n], refs[n:]
    outs, held, sem = refs[:n_outs], refs[n_outs:n_outs + n], refs[-1]
    copies = []
    for i, (ref, (index, cols)) in enumerate(zip(ins, [p for m in moves for p in m])):
        at = tuple(
            slice(None) if k is None else pl.ds(0, 1) if k == 0 else pl.ds(lax.rem(plan[k[0]] + k[1], 2), 1) for k in index)
        copies.append(pltpu.make_async_copy(ref.at[at + (slice(None), cols)], held[i], sem.at[i]))
    for copy in copies:
        copy.start()
    at, col = 0, 0
    for i, parts in enumerate(moves):
        for copy in copies[at:at + len(parts)]:
            copy.wait()
        total = sum(r[...].astype(F32) for r in held[at:at + len(parts)]).astype(LOW)
        at += len(parts)
        if merged:
            outs[0][..., col:col + total.shape[-1]] = total
            col += total.shape[-1]
        else:
            outs[i][...] = total


def join_all(plan, chains, dims, merged=False, first=()):
    ins, outs, moves, scratch = [], [], [], []
    if first:
        plan = after(plan, *first)
    for chain, dim in zip(chains, dims):
        parts = [p[0] for p in chain.parts]
        kept = dict(parts[0].kept)
        if dim is not None:
            kept[dim[0]] = dim[1]
        shape = parts[0].array.shape
        size = tuple(1 if d in kept else n for d, n in enumerate(shape[:-2])) + shape[-2:]
        move = []
        for part in parts:
            array = part.array
            index = tuple(0 if array.shape[d] == 1 else kept.get(d) for d in range(array.ndim - 2))
            same = array.shape[-1] == shape[-1]
            move.append((index, slice(None) if same else pl.ds(len(moves) * shape[-1], shape[-1])))
            ins.append(array)
            scratch.append(pltpu.VMEM(size, LOW))
        moves.append(move)
        outs.append(size)
    if merged:
        outs = [outs[0][:-1] + (sum(o[-1] for o in outs),)]
    big = len(chains) > 2
    return pl.pallas_call(
        functools.partial(join_kernel, moves=moves, merged=merged, n_outs=len(outs)),
        grid_spec=pltpu.PrefetchScalarGridSpec(
            num_scalar_prefetch=1, grid=(1,), in_specs=[pl.BlockSpec(memory_space=pl.ANY)] * len(ins),
            out_specs=[pl.BlockSpec(o, lambda *_, n=len(o): (0,) * n, pipeline_mode=pl.Buffered(1)) for o in outs],
            scratch_shapes=scratch + [pltpu.SemaphoreType.DMA((len(ins),))]),
        out_shape=[jax.ShapeDtypeStruct(o, LOW) for o in outs],
        compiler_params=pltpu.CompilerParams(vmem_limit_bytes=(60 if big else 28) * MIB),
        cost_estimate=pl.CostEstimate(flops=1, bytes_accessed=1, transcendentals=0),
        name="join",
    )(plan, *ins)


def exchange(plan, places, chains, moves, *first):
    axes = [c.bits[m] for c, m in zip(chains, moves)]
    sents = join_all(plan, chains, [(axis, (places[m], 1)) for axis, m in zip(axes, moves)], first=first)
    for chain, (name, mask), axis, sent in zip(chains, moves, axes, sents):
        got = swap(sent, name, mask)
        chain.parts = [[c.pick(axis, (places[name, mask], 0)) for c in p] for p in chain.parts] + [[Cut(got)]]
    return sents


def exchange_merged(plan, places, chains, move, *first):
    axis = chains[0].bits[move]
    sent = join_all(plan, chains, [(axis, (places[move], 1))] * len(chains), merged=True, first=first)[0]
    got = swap(sent, *move)
    for chain in chains:
        chain.parts = [[c.pick(axis, (places[move], 0)) for c in p] for p in chain.parts] + [[Cut(got)]]
    return sent


def finish_kernel(plan, *refs, first, sources, pairs, unit):
    n = len(sources)
    pieces, rests, refs = refs[:n], refs[n:2 * n], refs[2 * n:]
    outer_ref, inner_ref, attn_ref, qkv_ref, bq_ref, bv_ref, *line_refs, vec_ref, turned, vec_qv = refs
    width, dim = outer_ref.shape
    share = attn_ref.shape[0]
    top, part = unit + 32, share // 2
    vec_ref[...] = jnp.zeros(vec_ref.shape, F32)
    vec_qv[...] = jnp.zeros(vec_qv.shape, F32)
    for (e, d), ref, rest in zip(sources, pieces, rests):
        member, side = plan[first + e], lax.rem(plan[first + 2] + d, 2)
        owner = member * 2 + side
        turned[pl.ds(pl.multiple_of(owner * unit, 8), unit), :] = ref[:unit, :width].astype(F32)
        for half in range(2):
            inner_ref[:, pl.ds(pl.multiple_of(owner * 2 * width + half * width, LANES), width)] = (
                ref[half * share:(half + 1) * share, width:].astype(F32))
        attn_ref[pl.ds(pl.multiple_of(owner * 24, 8), 24), :] = ref[unit:unit + 24, :].astype(F32)
        vec_ref[pl.ds(pl.multiple_of(side * 8, 8), 8), :] += ref[unit:top, :].astype(F32)[24:, :]
        rows = pl.ds(pl.multiple_of(side * part, 8), part)
        for block in range(3 * pairs + 1):
            values = rest[:, block * LANES:(block + 1) * LANES].astype(F32)
            if block == 3 * pairs:
                vec_qv[rows, :] += values
            else:
                j, i = divmod(block, 3)
                to = pl.multiple_of(i * dim + (member * pairs + j) * LANES, LANES)
                qkv_ref[rows, pl.ds(to, LANES)] = values
    outer_ref[...] = turned[...].T
    dp = plan[first + 3 + 4 + 4]
    here = pltpu.roll(vec_ref[...], lax.rem(dim - dp * share, dim), 1)
    for i, ref in enumerate(line_refs[:6]):
        ref[...] = here[i, :share]
    per = dim // width
    line_refs[6][...] = vec_ref[pl.ds(8 + dp // per, 1), pl.ds(pl.multiple_of(lax.rem(dp, per) * width, LANES), width)][0]
    bq_ref[...] = vec_qv[0, :share]
    bv_ref[...] = vec_qv[1, :share]


def finish(plan, pieces, rests, sources, first, pairs, unit, width, share, wide):
    dim = pieces[0].shape[1]
    return kernel_call(
        functools.partial(finish_kernel, first=first, sources=sources, pairs=pairs, unit=unit),
        "finish", (1,), (*pieces, *rests), [whole(a) for a in (*pieces, *rests)],
        [((width, dim), F32, None, None), ((share, wide), F32, None, None), ((share, dim), F32, None, None),
         ((share, 3 * dim), F32, None, None)]
        + [((share,), F32, None, None)] * 8 + [((width,), F32, None, None)],
        [pltpu.VMEM((16, dim), F32), pltpu.VMEM((dim, width), F32), pltpu.VMEM((share, LANES), F32)],
        0, 10 * dim * width, 0, (plan,), 16)


def by_owner(parts, member):
    stack = jnp.stack(parts)
    return [lax.dynamic_index_in_dim(stack, member ^ m, 0, keepdims=False) for m in range(len(parts))]


def body(hidden_in, passage_lengths, w_qkv, b_query, b_value, w_attn_out, b_attn_out, gain_attn,
         bias_attn, w_inner, b_inner, w_outer, b_outer, gain_ffn, bias_ffn, grad_out):
    rows, chunk, dim = hidden_in.shape
    n_dp, n_seq = lax.axis_size("dp"), lax.axis_size("seq")
    wide = w_inner.shape[1]
    slots = passage_lengths.shape[1]
    assert slots == SLOTS
    group = n_seq // rows
    seq = lax.axis_index("seq")
    side, member = seq // group, seq % group
    tokens = group * rows * chunk
    cols = HEADS // group * HEAD_DIM
    pairs = -(-cols // LANES)
    padded = pairs * LANES
    aligned = cols % LANES == 0
    count = rows * group
    share = dim // n_dp
    row_at = lambda a, d: lax.dynamic_index_in_dim(a, side ^ d, 0, keepdims=False)

    send = row_at(hidden_in, 1)
    got = swap(send, "seq", group)
    own = row_at(hidden_in, 0)
    cot_send = after(row_at(grad_out, 1), got)
    cot_got = swap(cot_send, "seq", group)

    start = jnp.stack([(side ^ d) * group + (member ^ e) for e in range(group) for d in range(rows)]).astype(jnp.int32)
    ends = jnp.cumsum(row_at(passage_lengths, 0), dtype=jnp.int32)
    segment = lambda p: jnp.sum((p[..., None] >= ends).astype(jnp.int32), axis=-1, dtype=jnp.int32)
    index = jnp.arange(count, dtype=jnp.int32)
    half = chunk // 2
    units = jnp.arange(2 * count, dtype=jnp.int32)
    low_seg, high_seg = segment(index * chunk), segment(index * chunk + (chunk - 1))
    low_key, high_key = segment(units * half), segment(units * half + (half - 1))
    meets = jnp.maximum(low_seg[:, None], low_key[None, :]) <= jnp.minimum(high_seg[:, None], high_key[None, :])
    first_key = jnp.min(jnp.where(meets, units[None, :], 2 * count), axis=1)
    spans = jnp.max(jnp.where(meets, units[None, :], -1), axis=1) + 1 - first_key
    rounded = functools.reduce(lambda r, n: jnp.where(spans <= n, n, r), reversed(key_spans(count)), 2 * count)
    first_key = jnp.minimum(first_key, 2 * count - rounded)
    reorder = lambda a: jnp.sum(jnp.where(start[:, None] == index[None, :], a[None, :], 0), axis=1)
    per = wide // dim // group
    turns = [(member ^ e) * per + r for e in reversed(range(group)) for r in range(per)]
    moves = [("dp", 1 << b) for b in range(len(split_bits(n_dp)))] + [("seq", group)]
    members = jnp.stack([member ^ e for e in range(group)] + [side] + turns
                        + [(lax.axis_index(name) // mask) % 2 for name, mask in moves] + [lax.axis_index("dp")])
    plan = jnp.concatenate([ends, start, reorder(first_key), reorder(rounded), first_key, rounded, members]).astype(jnp.int32)
    first = SLOTS + 5 * count
    places = {m: first + group + 1 + len(turns) + i for i, m in enumerate(moves)}
    first_bias = 8
    vec = jnp.concatenate(
        [b_attn_out, gain_attn, bias_attn, b_outer, gain_ffn, bias_ffn, b_query, b_value, b_inner]
    ).astype(F32).reshape(-1, dim)
    if aligned:
        weights = [w_qkv] * 3, [lambda j, n, i=i: (0, i * group + n[first]) for i in range(3)] + [lambda j, n: (0, n[first])]
        vec_heads = vec
    else:
        widen = lambda a: jnp.pad(a, ((0, 0), (0, padded - cols)))
        weights_of = lambda m: [widen(lax.dynamic_slice_in_dim(w_qkv, m * cols + i * dim, cols, 1)) for i in range(3)]
        vec_heads = widen(lax.dynamic_slice_in_dim(vec, member * cols, cols, 1))
        weights = weights_of(member), [lambda j, n: (0, 0)] * 4

    chunks = [own, got]
    for e in range(1, group):
        chunks += [swap(own, "seq", e), swap(after(got, plan, vec), "seq", e)]

    o_mine, o_send, lse, q, k, v = attend(
        plan, chunks, weights, vec_heads, pairs, rows)
    apart = lambda a: [a] if group == 2 else [a[i * rows * chunk:(i + 1) * rows * chunk] for i in range(group - 1)]
    together = lambda a: a[0] if len(a) == 1 else jnp.concatenate(a, axis=0)
    o_parts = [o_mine] + [swap(a, "seq", e) for e, a in enumerate(apart(o_send), 1)]
    fine = aligned and (wide // n_dp) % LANES == 0 and share % 16 == 0 and per == rows and share == 24 * rows * group
    out_own, out_send, dh1, *made = token_work(
        plan, chunks[:rows], o_parts, w_attn_out, vec, w_inner, w_outer, grad_out, cot_got, cols, padded,
        first_bias, first, n_dp, fine)
    do_parts, made = made[:group], made[group:]
    do_gots = [swap(do_parts[e], "seq", e) for e in range(1, group)]
    out_got = swap(out_send, "seq", group)

    dp_masks = [1 << b for b in range(len(split_bits(n_dp)))]
    bit_shape = split_bits(n_dp) + split_bits(rows)
    bits = {("dp", m): len(dp_masks) - 1 - i for i, m in enumerate(dp_masks)}
    bits["seq", group] = len(dp_masks)

    unit, width = dim // group // rows, wide // n_dp
    if fine:
        feed_parts = made
    else:
        raw_outer, raw_inner, raw_attn, raw_vectors = made
        flat = lambda a: a.reshape(group, n_dp, rows, -1)
        feed_all = jnp.concatenate([
            flat(raw_outer.transpose(1, 0, 2).reshape(group, rows, unit, n_dp, width).transpose(0, 3, 1, 2, 4)),
            flat(raw_inner.transpose(1, 0, 2).reshape(n_dp, share, group, rows, -1).transpose(2, 0, 3, 1, 4)),
            flat(raw_attn.reshape(n_dp, group, rows, -1, dim).transpose(1, 0, 2, 3, 4))], axis=3)
        vectors = jnp.broadcast_to(raw_vectors.reshape(1, rows, -1), (n_dp, rows, 16 * dim // rows)).astype(LOW)
        feed_parts = [
            jnp.concatenate([lax.dynamic_index_in_dim(feed_all, member ^ e, 0, keepdims=False),
                             vectors if e == 0 else jnp.zeros_like(vectors)], axis=2).reshape(n_dp, rows, -1, LANES)
            for e in range(group)]
    ways = 3 if fine else 1
    shaped = lambda a: a.reshape(bit_shape + a.shape[2:])
    by_way = [[feed_parts[e * ways + i] for e in range(group)] for i in range(ways)]
    feeds = [Halving([shaped(p[0])] + [shaped(swap(p[e], "seq", e)) for e in range(1, group)], bits) for p in by_way]
    stages = [("dp", 1), ("seq", group), ("dp", 2)]

    def feed_stage(n, *before):
        moves = [stages[(n + i) % 3] for i in range(ways)]
        if fine:
            return exchange(plan, places, feeds, moves, *before)
        for f, move in zip(feeds, moves):
            f.send(*move, *before)
        return [f.sent for f in feeds]

    if fine:
        sent = []
        for f, move in zip(feeds, stages):
            sent = exchange(plan, places, [f], [move], *sent, *([out_got] + do_gots if f is feeds[-1] else []))
    else:
        sent = feed_stage(0)

    runs = [(0, pairs)]
    part = share // rows
    packed_grads = lambda a: a.reshape(bit_shape + (part, a.shape[-1]))
    d_mine, d_other, small_qkv, *grad_qkv = attend_back(
        plan, chunks, q, k, v, do_parts[0], after(together(do_gots), *sent), lse, pairs, rows,
        share if fine else 0, first)
    if fine:
        rests = [Halving([packed_grads(a)], bits) for a in grad_qkv]
    else:
        heads = lax.dynamic_update_slice_in_dim(jnp.zeros((2, dim), F32), small_qkv[:2, :cols], member * cols, 1)
        vectors = heads.reshape(2, n_dp, -1).transpose(1, 0, 2)
        vectors = jnp.pad(vectors, ((0, 0), (0, rows * part - 2), (0, LANES - share))).astype(LOW).reshape(n_dp, rows, part, LANES)
        rests = [Halving([[packed_grads(grad_qkv[0]), vectors.reshape(bit_shape + vectors.shape[2:])]], bits)]
    rest_moves = [[("dp", 2), ("dp", 1)], [("seq", group), ("dp", 2)], [("dp", 1), ("seq", group)]]
    dp_stages = [("dp", m) for m in dp_masks]

    def rest_stage(n, *before):
        moves = rest_moves[n] if n < 3 else [dp_stages[n - 1]] * 2
        if fine:
            return exchange(plan, places, rests, moves, *before)
        rests[0].send(*moves[0], *before)
        return [rests[0].sent]

    sent = feed_stage(1, d_mine)
    d_gots = [swap(after(a, *sent), "seq", e) for e, a in enumerate(apart(d_other), 1)]
    rest_sent = rest_stage(0, *sent)
    out_first = rest_sent

    runs_of = [[a] for a in [d_mine] + d_gots]
    if aligned:
        in_own, in_send = input_grads(plan, runs_of, runs, w_qkv, after(dh1, *rest_sent), pairs, chunk, first)
    else:
        grad_hidden = dh1
        for e, parts in enumerate(runs_of):
            w = weights_of(member ^ e)
            d = jnp.concatenate(parts, axis=1)
            for j in range(pairs):
                w_pair = jnp.concatenate([a[:, j * LANES:(j + 1) * LANES] for a in w], axis=1)
                grad_hidden = grad_hidden + dot_nt(d[:, j * 3 * LANES:(j + 1) * 3 * LANES], w_pair)
        in_own, in_send = grad_hidden[:chunk], grad_hidden[chunk:].astype(LOW)

    def in_place(own, got):
        return jnp.where(side == 0, jnp.stack([own, got]), jnp.stack([got, own]))

    sent = feed_stage(2, in_send)
    early = [feeds[0].parts[-1][0].array] if fine else sent
    if fine:
        last = ("dp", dp_masks[-1])
        rest_sent = rest_stage(1, *early)
        sent = exchange_merged(plan, places, feeds, last, *rest_sent)
        early = [sent]
        in_got = swap(after(in_send, sent), "seq", group)
        rest_stage(2, sent)
        late = [exchange_merged(plan, places, rests, last)]
    else:
        rest_sent = rest_stage(1, *sent)
        feed = feeds[0]
        in_got = swap(in_send, "seq", group)
        rest_sent = rest_stage(2, *rest_sent)
        for i, mask in enumerate(dp_masks[2:]):
            feed.send("dp", mask, *rest_sent)
            rest_sent = rest_stage(3 + i, feed.sent)
        late = rest_sent
        feed_piece, rest_piece = feed.finish(*late), rests[0].finish()
    out = in_place(after(out_own, *early), out_got[:chunk].astype(F32))
    sums = in_place(after(out_send, *early)[chunk:chunk + slots], out_got[chunk:chunk + slots])
    sums = add_up([sums] + [swap(sums, "seq", e) for e in range(1, group)])
    pooled = sums / jnp.maximum(passage_lengths.astype(F32), 1.0)[:, :, None]
    grad_in = in_place(after(in_own, *early), in_got.astype(F32))

    def everyone(piece):
        gots = [piece] + [swap(piece, "seq", e) for e in range(1, group)]
        return by_owner(gots, member)

    here = lambda a: lax.dynamic_slice_in_dim(a.reshape(-1), lax.axis_index("dp") * (a.size // n_dp), a.size // n_dp)
    if fine:
        sources = [(0, 0), (0, 1), (1, 0), (1, 1)]

        def from_all(piece):
            piece = piece.reshape(piece.shape[-2:])
            got = swap(piece, "seq", group)
            return [piece, got, swap(piece, "seq", 1), swap(got, "seq", 1)]

        feed_piece = join_all(plan, feeds, [None] * ways, merged=True, first=late + [grad_in, pooled, out])[0]
        pieces_of = [from_all(feed_piece)]
        rest_piece = join_all(plan, rests, [None] * 2, merged=True, first=[pieces_of[0][1]])[0]
        pieces_of.append(from_all(rest_piece))
        (grad_w_outer, grad_w_inner, grad_w_attn_out, grad_w_qkv, grad_b_query, grad_b_value, grad_gain_ffn,
         grad_bias_ffn, grad_b_outer, grad_gain_attn, grad_bias_attn, grad_b_attn_out, grad_b_inner) = finish(
            plan, pieces_of[0], pieces_of[1], sources, first, pairs, unit, width, share, wide)
    else:
        feed_pieces = everyone(feed.spread(feed_piece))
        sizes = [unit * width, share * (wide // group // rows), share * dim // group // rows, 16 * dim // rows]
        ends_of = [sum(sizes[:i]) for i in range(5)]
        cut = lambda a, i: a.reshape(rows, -1)[:, ends_of[i]:ends_of[i + 1]]
        grad_w_outer = jnp.concatenate([cut(a, 0).reshape(rows * unit, width) for a in feed_pieces]).T.astype(F32)
        grad_w_inner = jnp.concatenate(
            [cut(a, 1).reshape(rows, share, -1)[r] for a in feed_pieces for r in range(rows)], axis=1).astype(F32)
        grad_w_attn_out = jnp.concatenate([cut(a, 2).reshape(-1, dim) for a in feed_pieces], axis=0).astype(F32)
        totals = add_up([cut(a, 3) for a in feed_pieces]).reshape(16, dim)
        rest_pieces = [a.reshape(share, -1) for a in everyone(rests[0].spread(rest_piece))]
        grad_w_qkv = jnp.concatenate(
            [jnp.concatenate([a[:, (3 * j + i) * LANES:(3 * j + i + 1) * LANES] for j in range(pairs)], axis=1)[:, :cols]
             for i in range(3) for a in rest_pieces], axis=1).astype(F32)
        sums_qv = add_up([a[:, 3 * padded:] for a in rest_pieces])
        (grad_gain_ffn, grad_bias_ffn, grad_b_outer, grad_gain_attn, grad_bias_attn, grad_b_attn_out) = [
            here(totals[i]) for i in range(6)]
        grad_b_inner = here(totals[8:8 + wide // dim])
        grad_b_query, grad_b_value = sums_qv[0, :share], sums_qv[1, :share]

    return (out, pooled, grad_in, grad_w_qkv, grad_b_query, grad_b_value, grad_w_attn_out,
            grad_b_attn_out, grad_gain_attn, grad_bias_attn, grad_w_inner, grad_b_inner,
            grad_w_outer, grad_b_outer, grad_gain_ffn, grad_bias_ffn)


def solution(mesh):
    tokens, rows, all_of = P("dp", "seq", None), P("dp", None), P()
    vector, cube = P("dp"), P("dp", None, None)
    return jax.shard_map(
        body,
        mesh=mesh,
        in_specs=(tokens, rows) + (all_of,) * 13 + (tokens,),
        out_specs=(tokens, cube, tokens, rows, vector, vector, rows, vector, vector, vector, rows,
                   vector, rows, vector, vector, vector),
        check_vma=False,
    )
```

```python
import functools
import math

import jax
import jax.numpy as jnp
from jax import lax
from jax.experimental import pallas as pl
from jax.experimental.pallas import tpu as pltpu
from jax.sharding import PartitionSpec as P

LOW = jnp.bfloat16
F32 = jnp.float32
HEADS = 12
HEAD_DIM = 64
LANES = 128
MIB = 1024 * 1024
MASKED = -1e30
EPS = 1e-12
COST = 1000
SLOTS = 8
HALF_ROOT = math.sqrt(0.5)
PHI_SCALE = 1.0 / math.sqrt(2.0 * math.pi)


def dot(left, right):
    return jnp.dot(left, right, preferred_element_type=F32)


def dot_nt(left, right):
    return lax.dot_general(left, right, (((1,), (1,)), ((), ())), preferred_element_type=F32)


def dot_tn(left, right):
    return lax.dot_general(left, right, (((0,), (0,)), ((), ())), preferred_element_type=F32)


def head_lanes(shape, head):
    lane = lax.rem(lax.broadcasted_iota(jnp.int32, shape, 1), LANES)
    return (lane >= HEAD_DIM) if head else (lane < HEAD_DIM)


def spread(column, width):
    return jnp.concatenate([column] * (width // LANES), axis=1)


def segments(plan, shape, axis, start=0):
    place = lax.broadcasted_iota(jnp.int32, shape, axis) + start
    return sum((place >= plan[j]).astype(jnp.int32) for j in range(SLOTS))


def whole(array, buffers=1):
    return pl.BlockSpec(array.shape, lambda *_: (0,) * array.ndim, pipeline_mode=pl.Buffered(buffers))


def kernel_call(body, name, grid, ins, in_specs, outs, scratch, flops, moved, exps=0, prefetch=(), limit=24):
    spec = pltpu.PrefetchScalarGridSpec(
        num_scalar_prefetch=len(prefetch),
        grid=grid,
        in_specs=in_specs,
        out_specs=[
            pl.BlockSpec(memory_space=pltpu.HBM) if b == "hbm" else pl.BlockSpec(b, m) if b else pl.BlockSpec(s, lambda *_, n=len(s): (0,) * n, pipeline_mode=pl.Buffered(1))
            for s, _, b, m in outs
        ],
        scratch_shapes=scratch,
    )
    return pl.pallas_call(
        body,
        grid_spec=spec,
        out_shape=[jax.ShapeDtypeStruct(s, t) for s, t, _, _ in outs],
        compiler_params=pltpu.CompilerParams(vmem_limit_bytes=limit * MIB),
        cost_estimate=pl.CostEstimate(flops=int(flops) // COST, bytes_accessed=int(moved) // COST, transcendentals=int(exps) // COST),
        name=name,
    )(*prefetch, *ins)


def key_spans(count):
    return list(range(2, 2 * count + 1)) if count <= 4 else [n for n in (2, 4, 8, 16, 32) if n <= 2 * count]


def turn(block):
    return block.T.astype(LOW)


def in_place_of(ref, chunk):
    return pl.ds(pl.multiple_of(ref * chunk, chunk), chunk)


def attend_kernel(plan, *refs, block, count, near, pairs):
    chunks, refs = refs[:count], refs[count:]
    (wq_ref, wk_ref, wv_ref, vec_ref, om_ref, os_ref, lse_ref, q_out, k_out, v_out,
     q, k, v, o, qt, km, vm, segk_ref, segq_ref, sem) = refs
    width = pairs * LANES
    segk_ref[...] = segments(plan, segk_ref.shape, 0)
    segq_ref[...] = segments(plan, segq_ref.shape, 1)
    lse_ref[...] = jnp.zeros(lse_ref.shape, F32)
    w = jnp.concatenate([wq_ref[...], wk_ref[...], wv_ref[...]], axis=1)
    bias_q, bias_v = vec_ref[6:7, :], vec_ref[7:8, :]
    for i in range(count):
        at = in_place_of(plan[SLOTS + i], block)
        made = dot(chunks[i][...], w)
        q_low = (made[:, :width] + bias_q).astype(LOW).astype(F32) * HEAD_DIM ** (-0.5)
        k_low = made[:, width:2 * width].astype(LOW)
        v_low = (made[:, 2 * width:] + bias_v).astype(LOW)
        q[at, :] = q_low.astype(LOW)
        k[at, :] = k_low
        v[at, :] = v_low
        qt[:, at] = turn(q_low)
        for h in range(2):
            lanes = head_lanes((block, width), h)
            km[h, at, :] = jnp.where(lanes, k_low, jnp.zeros((), LOW))
            vm[h, at, :] = jnp.where(lanes, v_low, jnp.zeros((), LOW))
    copies = [pltpu.make_async_copy(a, b, sem.at[i]) for i, (a, b) in enumerate([(q, q_out), (k, k_out), (v, v_out)])]
    for copy in copies:
        copy.start()

    def one_block(j, carry):
        cols = in_place_of(plan[SLOTS + j], block)
        for span in key_spans(count):
            @pl.when(plan[SLOTS + 2 * count + j] == span)
            def _():
                rows = pl.ds(pl.multiple_of(plan[SLOTS + count + j] * (block // 2), block // 2), span * (block // 2))
                same = spread(segk_ref[rows, :], block) == segq_ref[0:1, cols]
                made, totals = [], []
                for i in range(pairs):
                    pair = slice(i * LANES, (i + 1) * LANES)
                    for h in range(2):
                        s = jnp.where(same, dot(km[h, rows, pair], qt[pair, cols]), MASKED)
                        top = jnp.max(s, axis=0, keepdims=True)
                        p = jnp.exp(s - top)
                        total = jnp.sum(p, axis=0, keepdims=True)
                        made.append(dot_tn(p.astype(LOW), vm[h, rows, pair]))
                        totals.append(total)
                        lse_ref[2 * i + h:2 * i + h + 1, cols] = top + jnp.log(total)
                totals += [jnp.ones((1, block), F32)] * (-len(totals) % 8)
                scale = (1.0 / jnp.concatenate(totals, axis=0)).T
                for i in range(pairs):
                    both = made[2 * i] * scale[:, 2 * i:2 * i + 1] + made[2 * i + 1] * scale[:, 2 * i + 1:2 * i + 2]
                    o[in_place_of(j, block), i * LANES:(i + 1) * LANES] = both.astype(LOW)
        return carry

    lax.fori_loop(0, count, one_block, 0)
    copies += [pltpu.make_async_copy(o.at[pl.ds(0, near * block)], om_ref, sem.at[3]),
               pltpu.make_async_copy(o.at[pl.ds(near * block, (count - near) * block)], os_ref, sem.at[4])]
    for copy in copies[3:]:
        copy.start()
    for copy in copies:
        copy.wait()


def hbm(shape):
    return (shape, LOW, "hbm", None)


def attend(plan, chunks, weights, vec, pairs, near):
    block = chunks[0].shape[0]
    count = len(chunks)
    tokens = block * count
    width = pairs * LANES
    arrays, maps = weights
    low = lambda *s: pltpu.VMEM(s, LOW)
    return kernel_call(
        functools.partial(attend_kernel, block=block, count=count, near=near, pairs=pairs),
        "attend", (1,),
        (*chunks, *arrays, vec),
        [whole(c) for c in chunks]
        + [pl.BlockSpec((arrays[0].shape[0], width), m, pipeline_mode=pl.Buffered(1)) for m in maps[:3]]
        + [pl.BlockSpec((vec.shape[0], width), maps[3], pipeline_mode=pl.Buffered(1))],
        [
            hbm((near * block, width)), hbm((tokens - near * block, width)),
            ((8, tokens), F32, None, None),
            hbm((tokens, width)), hbm((tokens, width)), hbm((tokens, width)),
        ],
        [low(tokens, width), low(tokens, width), low(tokens, width), low(tokens, width), low(width, tokens), low(2, tokens, width),
         low(2, tokens, width), pltpu.VMEM((tokens, LANES), jnp.int32),
         pltpu.VMEM((8, tokens), jnp.int32), pltpu.SemaphoreType.DMA((5,))],
        4 * tokens * tokens * width, 20 * tokens * width, 2 * tokens * tokens * pairs, (plan,), 50)


def attend_back_kernel(plan, *refs, block, count, near, pairs, owned, first):
    chunks, refs = refs[:count], refs[count:]
    (q_in, k_in, v_in, dm_in, do_in, lse_ref, gm_ref, go_ref, small_ref), refs = refs[:9], refs[9:]
    gw_refs, refs = refs[:2 if owned else 1], refs[2 if owned else 1:]
    (hidden, q, k, v, given, qt, dt, km, vm, qm, dom, dq, dk, dv, joined, segk_ref, segq_ref, sem) = refs
    tokens, width = q.shape
    head, tail = pl.ds(0, near * block), pl.ds(near * block, tokens - near * block)
    order = [(dm_in, given.at[head]), (do_in, given.at[tail]), (q_in, q), (k_in, k), (v_in, v)]
    order += [(c, hidden.at[pl.ds(i * block, block)]) for i, c in enumerate(chunks)]
    copies = [pltpu.make_async_copy(a, b, sem.at[i]) for i, (a, b) in enumerate(order)]
    for copy in copies:
        copy.start()
    segk_ref[...] = segments(plan, segk_ref.shape, 0)
    segq_ref[...] = segments(plan, segq_ref.shape, 1)
    dk[...] = jnp.zeros(dk.shape, F32)
    dv[...] = jnp.zeros(dv.shape, F32)
    zero = jnp.zeros((), LOW)
    lanes = [head_lanes((block, width), h) for h in range(2)]
    for copy in copies[:2]:
        copy.wait()
    for i in range(count):
        at = in_place_of(plan[SLOTS + i], block)
        rows = given[i * block:(i + 1) * block, :]
        dt[:, at] = turn(rows.astype(F32))
        for h in range(2):
            dom[h, at, :] = jnp.where(lanes[h], rows, zero)
    for copy in copies[2:5]:
        copy.wait()
    for i in range(count):
        fixed = slice(i * block, (i + 1) * block)
        qt[:, fixed] = turn(q[fixed, :].astype(F32))
        for h in range(2):
            km[h, fixed, :] = jnp.where(lanes[h], k[fixed, :], zero)
            vm[h, fixed, :] = jnp.where(lanes[h], v[fixed, :], zero)
            qm[h, fixed, :] = jnp.where(lanes[h], q[fixed, :], zero)

    def one_block(j, carry):
        cols = in_place_of(j, block)
        for span in key_spans(count):
            @pl.when(plan[SLOTS + 4 * count + j] == span)
            def _():
                rows = pl.ds(pl.multiple_of(plan[SLOTS + 3 * count + j] * (block // 2), block // 2), span * (block // 2))
                same = spread(segk_ref[rows, :], block) == segq_ref[0:1, cols]
                for p in range(pairs):
                    pair = slice(p * LANES, (p + 1) * LANES)
                    dk_add, dv_add, dq_add = 0.0, 0.0, 0.0
                    for h in range(2):
                        n = 2 * p + h
                        s = jnp.where(same, dot(km[h, rows, pair], qt[pair, cols]), MASKED)
                        e = jnp.exp(s - lse_ref[n:n + 1, cols])
                        weighed = e * dot(vm[h, rows, pair], dt[pair, cols])
                        ds = (weighed - e * jnp.sum(weighed, axis=0, keepdims=True)).astype(LOW)
                        dv_add += dot(e.astype(LOW), dom[h, cols, pair])
                        dk_add += dot(ds, qm[h, cols, pair])
                        dq_add += dot_tn(ds, km[h, rows, pair])
                    dv[rows, pair] += dv_add
                    dk[rows, pair] += dk_add
                    dq[cols, pair] = dq_add * HEAD_DIM ** (-0.5)
        return carry

    lax.fori_loop(0, count, one_block, 0)
    small_ref[...] = jnp.zeros(small_ref.shape, F32)
    for i in range(count):
        at = in_place_of(plan[SLOTS + i], block)
        parts = [a[at, :].astype(LOW) for a in (dq, dk, dv)]
        small_ref[0:1, :] += jnp.sum(parts[0].astype(F32), axis=0, keepdims=True)
        small_ref[1:2, :] += jnp.sum(parts[2].astype(F32), axis=0, keepdims=True)
        columns = jnp.concatenate(
            [a[:, p * LANES:(p + 1) * LANES] for p in range(pairs) for a in parts], axis=1)
        joined[i * block:(i + 1) * block, :] = columns
    leaving = [pltpu.make_async_copy(joined.at[head], gm_ref, sem.at[count + 5]),
               pltpu.make_async_copy(joined.at[tail], go_ref, sem.at[count + 6])]
    for copy in leaving:
        copy.start()
    for copy in copies[5:]:
        copy.wait()
    made = dot_tn(hidden[...], joined[...]).astype(LOW)
    for copy in leaving:
        copy.wait()
    if owned:
        half = gw_refs[0].shape[1]
        gw_refs[0][...] = made[:, :half]
        gw_refs[1][:, :3 * width - half] = made[:, half:]
        gw_refs[1][:, 3 * width - half:] = jnp.zeros((made.shape[0], LANES), LOW)
        for t in range(width // owned):
            piece = jnp.pad(small_ref[0:2, t * owned:(t + 1) * owned], ((0, 14), (0, LANES - owned)))
            at = pl.multiple_of((plan[first] * (width // owned) + t) * owned, 16)
            gw_refs[1][pl.ds(at, 16), 3 * width - half:] = piece.astype(LOW)
    else:
        gw_refs[0][...] = made


def attend_back(plan, chunks, q, k, v, d_mine, d_others, lse, pairs, near, owned, first):
    block = chunks[0].shape[0]
    count = len(chunks)
    tokens = block * count
    width = pairs * LANES
    dim = chunks[0].shape[1]
    low = lambda *s: pltpu.VMEM(s, LOW)
    wide = lambda *s: pltpu.VMEM(s, F32)
    anywhere = pl.BlockSpec(memory_space=pl.ANY)
    return kernel_call(
        functools.partial(attend_back_kernel, block=block, count=count, near=near, pairs=pairs, owned=owned, first=first),
        "attend_back", (1,),
        (*chunks, q, k, v, d_mine, d_others, lse),
        [anywhere] * (count + 5) + [whole(lse)],
        [
            hbm((d_mine.shape[0], 3 * width)), hbm((d_others.shape[0], 3 * width)),
            ((8, width), F32, None, None),
        ] + [((dim, n), LOW, None, None) for n in ([(3 * width + LANES) // 2] * 2 if owned else [3 * width])],
        [low(tokens, dim), low(tokens, width), low(tokens, width), low(tokens, width), low(tokens, width),
         low(width, tokens), low(width, tokens), low(2, tokens, width), low(2, tokens, width),
         low(2, tokens, width), low(2, tokens, width),
         wide(tokens, width), wide(tokens, width), wide(tokens, width), low(tokens, 3 * width),
         pltpu.VMEM((tokens, LANES), jnp.int32), pltpu.VMEM((8, tokens), jnp.int32), pltpu.SemaphoreType.DMA((count + 7,))],
        10 * tokens * tokens * width, 30 * tokens * width, 2 * tokens * tokens * pairs, (plan,), 50)


def input_kernel(plan, *refs, group, runs, pairs, first):
    n = group * len(runs)
    d_ins, (w_in, dh_in, own_ref, sent_ref), held, (w_held, total, sem) = refs[:n], refs[n:n + 4], refs[n + 4:2 * n + 4], refs[2 * n + 4:]
    dim = w_in.shape[0]
    w_copies, copies = [], []
    for e in range(group):
        base = pl.multiple_of(plan[first + e] * pairs * LANES, LANES)
        for i in range(3):
            w_copies.append(pltpu.make_async_copy(
                w_in.at[:, pl.ds(base + i * dim, pairs * LANES)], w_held.at[3 * e + i], sem.at[3 * e + i]))
    for i in range(n):
        copies.append(pltpu.make_async_copy(d_ins[i], held[i], sem.at[3 * group + i]))
    last = pltpu.make_async_copy(dh_in, total, sem.at[3 * group + n])
    per = len(runs)
    for e in range(group):
        for copy in w_copies[3 * e:3 * e + 3] + copies[per * e:per * e + per]:
            copy.start()
    last.start()
    made = 0.0
    for e in range(group):
        for copy in w_copies[3 * e:3 * e + 3] + copies[per * e:per * e + per]:
            copy.wait()
        d = jnp.concatenate([held[per * e + r][...] for r in range(per)], axis=1)
        w = jnp.concatenate(
            [w_held[3 * e + i, :, j * LANES:(j + 1) * LANES] for j in range(pairs) for i in range(3)], axis=1)
        made += dot_nt(d, w)
    last.wait()
    made += total[...]
    chunk = own_ref.shape[0]
    own_ref[...] = made[:chunk]
    sent_ref[...] = made[chunk:].astype(LOW)


def input_grads(plan, d_parts, runs, w, dh, pairs, chunk, first):
    tokens, dim = dh.shape
    group = len(d_parts)
    ins = (*[d for parts in d_parts for d in parts], w, dh)
    return kernel_call(
        functools.partial(input_kernel, group=group, runs=runs, pairs=pairs, first=first), "input_grads", (1,), ins,
        [pl.BlockSpec(memory_space=pltpu.HBM)] * len(ins),
        [((chunk, dim), F32, None, None), ((tokens - chunk, dim), LOW, None, None)],
        [pltpu.VMEM(d.shape, LOW) for parts in d_parts for d in parts]
        + [pltpu.VMEM((3 * group, dim, pairs * LANES), LOW), pltpu.VMEM((tokens, dim), F32),
           pltpu.SemaphoreType.DMA((len(ins) - 2 + 3 * group + 1,))],
        6 * tokens * dim * dim, 6 * dim * dim + 10 * tokens * dim, 0, (plan,), 60)


def row_mean(values):
    return jnp.mean(values, axis=-1, keepdims=True)


def normal(values):
    centre = values - row_mean(values)
    scale = lax.rsqrt(row_mean(centre * centre) + EPS)
    return centre * scale, scale


def normal_back(hat, scale, grads):
    return scale * (grads - row_mean(grads) - hat * row_mean(grads * hat))


def head_rows(ref, owner, cols):
    return ref[pl.ds(pl.multiple_of(owner * cols, 16), cols), :]


def token_kernel(plan, *refs, group, cols, chunk, first_bias, first, count, fine):
    x_refs, o_refs, refs = refs[:2], refs[2:2 + group], refs[2 + group:]
    wa_ref, vec_ref, wi_ref, wo_ref, go_ref, gg_ref, own_ref, sent_ref, dh_ref = refs[:9]
    do_refs, refs = refs[9:9 + group], refs[9 + group:]
    if fine:
        dest_out, refs = refs[:3 * group], refs[3 * group:]
        held, sem, refs = refs[-1 - 3 * group:-1], refs[-1], refs[:-1 - 3 * group]
        dest = [held[3 * e:3 * e + 3] for e in range(group)]
    else:
        (outer_ref, inner_ref, attn_ref, vector_ref), refs = refs[:4], refs[4:]
    yl, acc, g, slope, hat1, scale1, dz, attn, vectors = refs
    step = pl.program_id(0)
    tokens, dim = acc.shape
    total = lambda values: jnp.sum(values, axis=0, keepdims=True)

    def put(refs, d, r, rows, first_col, values):
        third, end = refs[0].shape[3], first_col + values.shape[1]
        for i, ref in enumerate(refs):
            low, high = max(first_col, i * third), min(end, (i + 1) * third)
            if low < high:
                ref[d, r, rows, low - i * third:high - i * third] = values[:, low - first_col:high - first_col]

    @pl.when(step == 0)
    def _():
        x = jnp.concatenate([r[...] for r in x_refs], axis=0)
        h1 = x.astype(F32) + vec_ref[0:1, :]
        for e in range(group):
            h1 += dot(o_refs[e][:, :cols], head_rows(wa_ref, plan[first + e], cols))
        hat, scale = normal(h1)
        y1 = hat * vec_ref[1:2, :] + vec_ref[2:3, :]
        hat1[...] = hat
        scale1[...] = jnp.broadcast_to(scale, scale1.shape)
        yl[...] = y1.astype(LOW)
        acc[...] = y1 + vec_ref[3:4, :]
        vectors[...] = jnp.zeros(vectors.shape, F32)

    @pl.when(step < count)
    def _():
        u = dot(yl[...], wi_ref[...]) + vec_ref[pl.ds(first_bias + step, 1), :]
        cdf = 0.5 * (1.0 + lax.erf(u * HALF_ROOT))
        low = (u * cdf).astype(LOW)
        g[step] = low
        slope[step] = (cdf + u * (PHI_SCALE * jnp.exp(-0.5 * u * u))).astype(LOW)
        acc[...] += dot(low, wo_ref[...])

    @pl.when(step == count - 1)
    def _():
        hat, scale = normal(acc[...])
        gain = vec_ref[4:5, :]
        out = hat * gain + vec_ref[5:6, :]
        high = out.astype(LOW)
        own_ref[...] = out[:chunk]
        slots = sent_ref.shape[0] - (tokens - chunk)
        place = lax.broadcasted_iota(jnp.int32, (slots, tokens), 0)
        segs = jnp.concatenate(
            [segments(plan, (slots, chunk), 1, plan[SLOTS + i] * chunk) for i in range(tokens // chunk)], axis=1)
        onehot = (place == segs).astype(LOW)
        rest = (out - high.astype(F32)).astype(LOW)
        sent_ref[:tokens - chunk, :] = high[chunk:]
        sent_ref[tokens - chunk:, :] = (dot(onehot, high) + dot(onehot, rest)).astype(LOW)
        dy = jnp.concatenate([go_ref[0], gg_ref[...]], axis=0).astype(F32)
        dh = normal_back(hat, scale, dy * gain)
        low = dh.astype(LOW)
        dz[...] = low
        acc[...] = dh
        vectors[0:1, :] = total(dy * hat)
        vectors[1:2, :] = total(dy)
        vectors[2:3, :] = total(low.astype(F32))

    @pl.when(step >= count)
    def _():
        b = plan[first + group + 1 + step - count]
        du = (dot_nt(dz[...], wo_ref[...]) * slope[b].astype(F32)).astype(LOW)
        vectors[pl.ds(8 + b, 1), :] = total(du.astype(F32))
        inner = dot_tn(yl[...], du).astype(LOW)
        if fine:
            per, unit, width = count // group, dest[0][0].shape[2] - 32, dest[0][0].shape[3] * 3 // 2
            share = unit // 2
            for e in range(group):
                member_cols = pl.ds(pl.multiple_of(plan[first + e] * (dim // group), LANES), dim // group)
                outer = dot_tn(dz[:, member_cols], g[b]).astype(LOW)
                for i in range(dim // width):
                    for r in range(per):
                        put(dest[e], b * (dim // width) + i, r, slice(0, unit), 0,
                            outer[r * unit:(r + 1) * unit, i * width:(i + 1) * width])

                @pl.when((step - count) // per == group - 1 - e)
                def _():
                    r = lax.rem(step - count, per)
                    for d in range(dest[e][0].shape[0]):
                        for half in range(2):
                            put(dest[e], d, r, slice(half * share, (half + 1) * share), width,
                                inner[d * share:(d + 1) * share, half * width:(half + 1) * width])
        else:
            outer_ref[b] = dot_tn(dz[...], g[b]).astype(LOW)
            inner_ref[b] = inner
        acc[...] += dot_nt(du, wi_ref[...])

    def leave(rows, start):
        return [pltpu.make_async_copy(a.at[:, :, rows], b.at[:, :, rows], sem.at[start + i])
                for i, (a, b) in enumerate(zip(held, dest_out))]

    @pl.when(step == pl.num_programs(0) - 1)
    def _():
        if fine:
            unit = held[0].shape[2] - 32
            copies = leave(pl.ds(0, unit), 0)
            for copy in copies:
                copy.start()
        hat = hat1[...]
        dy = acc[...]
        dh = normal_back(hat, scale1[:, 0:1], dy * vec_ref[1:2, :])
        dh_ref[...] = dh
        da = dh.astype(LOW)
        for e in range(group):
            made = dot_nt(da, head_rows(wa_ref, plan[first + e], cols)).astype(LOW)
            if do_refs[e].shape[1] > cols:
                do_refs[e][...] = jnp.zeros(do_refs[e].shape, LOW)
            do_refs[e][:, :cols] = made
            attn[pl.ds(pl.multiple_of(plan[first + e] * cols, 8), cols), :] = dot_tn(o_refs[e][:, :cols], da)
        vectors[3:4, :] = total(dy * hat)
        vectors[4:5, :] = total(dy)
        vectors[5:6, :] = total(da.astype(F32))
        if fine:
            n_dp, sides, unit = dest[0][0].shape[0], dest[0][0].shape[1], dest[0][0].shape[2] - 32
            for e in range(group):
                for d in range(n_dp):
                    for r in range(sides):
                        at = d * (dim // n_dp) + plan[first + e] * (24 * sides) + r * 24
                        tail = vectors[8 * r:8 * r + 8, :] if e == 0 else jnp.zeros((8, dim), F32)
                        both = jnp.concatenate([attn[pl.ds(pl.multiple_of(at, 8), 24), :], tail], axis=0)
                        put(dest[e], d, r, slice(unit, unit + 32), 0, both.astype(LOW))
            copies += leave(pl.ds(unit, 32), 3 * group)
            for copy in copies[3 * group:]:
                copy.start()
            for copy in copies:
                copy.wait()
        else:
            attn_ref[...] = attn[...].astype(LOW)
            vector_ref[...] = vectors[...]


def token_work(plan, x_parts, o_parts, wa, vec, wi, wo, grad_out, grad_got, cols, padded, first_bias, first, n_dp, fine):
    chunk, dim = x_parts[0].shape
    tokens = 2 * chunk
    wide = wi.shape[1]
    block = dim
    count = wide // block
    group = len(o_parts)
    ins = (*x_parts, *o_parts, wa, vec, wi, wo, grad_out, grad_got)
    specs = [whole(a) for a in ins]
    which = lambda i, n: jnp.where(i < count, i, n[first + group + 1 + jnp.maximum(i - count, 0)])
    specs[-4] = pl.BlockSpec((dim, block), lambda i, n: (0, which(i, n)))
    specs[-3] = pl.BlockSpec((block, dim), lambda i, n: (which(i, n), 0))
    specs[-2] = pl.BlockSpec((1, chunk, dim), lambda i, n: (n[first + group], 0, 0))
    outs = [
        ((chunk, dim), F32, None, None),
        ((tokens - chunk + 16, dim), LOW, None, None),
        ((tokens, dim), F32, None, None),
    ] + [((tokens, padded), LOW, None, None)] * group
    if fine:
        made = (n_dp, 2, dim // group // 2 + 32, 2 * (wide // n_dp) // 3)
        outs += [hbm(made)] * (3 * group)
    else:
        outs += [((count, dim, block), LOW, None, None)] * 2 + [((dim, dim), LOW, None, None), ((16, dim), F32, None, None)]
    own = lambda *s: pltpu.VMEM(s, F32)
    low = lambda *s: pltpu.VMEM(s, LOW)
    return kernel_call(
        functools.partial(token_kernel, group=group, cols=cols, chunk=chunk, first_bias=first_bias, first=first, count=count, fine=fine),
        "token_work", (2 * count,), ins, specs, outs,
        [low(tokens, dim), own(tokens, dim), low(count, tokens, block), low(count, tokens, block), own(tokens, dim),
         own(tokens, LANES), low(tokens, dim), own(dim, dim), own(16, dim)]
        + ([low(*made)] * (3 * group) + [pltpu.SemaphoreType.DMA((6 * group,))] if fine else []),
        12 * tokens * dim * wide, 8 * dim * wide, 2 * tokens * wide, (plan,), 50)


def swap(values, name, mask):
    size = lax.axis_size(name)
    return lax.ppermute(values, name, [(i, i ^ mask) for i in range(size)])


def after(value, *first):
    return lax.optimization_barrier((value,) + first)[0]


def add_up(parts):
    return sum(p.astype(F32) for p in parts)


def split_bits(size):
    return (2,) * (size.bit_length() - 1)


class Cut:
    def __init__(self, array, kept=()):
        self.array, self.kept = array, dict(kept)

    def pick(self, axis, index):
        return Cut(self.array, {**self.kept, axis: index})

    def value(self):
        shape = [1 if d in self.kept else n for d, n in enumerate(self.array.shape)]
        return lax.dynamic_slice(self.array, [self.kept.get(d, 0) for d in range(len(shape))], shape)


class Halving:
    def __init__(self, parts, bits):
        self.parts = [[Cut(a) for a in (p if isinstance(p, list) else [p])] for p in parts]
        self.bits = bits
        self.sides = []

    def send(self, name, mask, *first):
        axis = self.bits[name, mask]
        bit = (lax.axis_index(name) // mask) % 2
        self.sent = self.join(self.parts, first, axis, 1 - bit)
        self.got = swap(self.sent, name, mask)
        self.parts = [[c.pick(axis, bit) for c in p] for p in self.parts] + [[Cut(self.got)]]
        if name == "seq":
            self.sides.append((mask, axis))

    def join(self, parts, first=(), axis=None, index=None):
        parts = [[c if axis is None else c.pick(axis, index) for c in p] for p in parts]
        if first:
            parts[0][0] = Cut(after(parts[0][0].array, *first), parts[0][0].kept)
        fine = max(parts, key=len)
        widths = [c.array.shape[-1] for c in fine]
        edges = [sum(widths[:i]) for i in range(len(widths) + 1)]

        def cut(p, i):
            at = 0
            for c in p:
                width = c.array.shape[-1]
                if at <= edges[i] and edges[i + 1] <= at + width:
                    value = c.value()
                    return value if width == widths[i] else value[..., edges[i] - at:edges[i + 1] - at]
                at += width
            raise ValueError(widths)

        sums = [add_up([cut(p, i) for p in parts]).astype(LOW) for i in range(len(widths))]
        return sums[0] if len(sums) == 1 else jnp.concatenate(sums, axis=-1)

    def finish(self, *first):
        return self.join(self.parts, first)

    def spread(self, piece):
        for mask, axis in reversed(self.sides):
            got = swap(piece, "seq", mask)
            bit = (lax.axis_index("seq") // mask) % 2
            piece = jnp.concatenate([jnp.where(bit == 0, piece, got), jnp.where(bit == 0, got, piece)], axis=axis)
        return piece


def abreast(*chains):
    both = Halving([[c.finish() for c in chains]], chains[0].bits)
    both.sides = list(chains[0].sides)
    return both


def join_kernel(plan, *refs, moves, merged, n_outs):
    n = sum(len(m) for m in moves)
    ins, refs = refs[:n], refs[n:]
    outs, held, sem = refs[:n_outs], refs[n_outs:n_outs + n], refs[-1]
    copies = []
    for i, (ref, (index, cols)) in enumerate(zip(ins, [p for m in moves for p in m])):
        at = tuple(
            slice(None) if k is None else pl.ds(0, 1) if k == 0 else pl.ds(lax.rem(plan[k[0]] + k[1], 2), 1) for k in index)
        copies.append(pltpu.make_async_copy(ref.at[at + (slice(None), cols)], held[i], sem.at[i]))
    for copy in copies:
        copy.start()
    at, col = 0, 0
    for i, parts in enumerate(moves):
        for copy in copies[at:at + len(parts)]:
            copy.wait()
        total = sum(r[...].astype(F32) for r in held[at:at + len(parts)]).astype(LOW)
        at += len(parts)
        if merged:
            outs[0][..., col:col + total.shape[-1]] = total
            col += total.shape[-1]
        else:
            outs[i][...] = total


def join_all(plan, chains, dims, merged=False, first=()):
    ins, outs, moves, scratch = [], [], [], []
    if first:
        plan = after(plan, *first)
    for chain, dim in zip(chains, dims):
        parts = [p[0] for p in chain.parts]
        kept = dict(parts[0].kept)
        if dim is not None:
            kept[dim[0]] = dim[1]
        shape = parts[0].array.shape
        size = tuple(1 if d in kept else n for d, n in enumerate(shape[:-2])) + shape[-2:]
        move = []
        for part in parts:
            array = part.array
            index = tuple(0 if array.shape[d] == 1 else kept.get(d) for d in range(array.ndim - 2))
            same = array.shape[-1] == shape[-1]
            move.append((index, slice(None) if same else pl.ds(len(moves) * shape[-1], shape[-1])))
            ins.append(array)
            scratch.append(pltpu.VMEM(size, LOW))
        moves.append(move)
        outs.append(size)
    if merged:
        outs = [outs[0][:-1] + (sum(o[-1] for o in outs),)]
    big = len(chains) > 2
    return pl.pallas_call(
        functools.partial(join_kernel, moves=moves, merged=merged, n_outs=len(outs)),
        grid_spec=pltpu.PrefetchScalarGridSpec(
            num_scalar_prefetch=1, grid=(1,), in_specs=[pl.BlockSpec(memory_space=pl.ANY)] * len(ins),
            out_specs=[pl.BlockSpec(o, lambda *_, n=len(o): (0,) * n, pipeline_mode=pl.Buffered(1)) for o in outs],
            scratch_shapes=scratch + [pltpu.SemaphoreType.DMA((len(ins),))]),
        out_shape=[jax.ShapeDtypeStruct(o, LOW) for o in outs],
        compiler_params=pltpu.CompilerParams(vmem_limit_bytes=(60 if big else 28) * MIB),
        cost_estimate=pl.CostEstimate(flops=1, bytes_accessed=1, transcendentals=0),
        name="join",
    )(plan, *ins)


def exchange(plan, places, chains, moves, *first):
    axes = [c.bits[m] for c, m in zip(chains, moves)]
    sents = join_all(plan, chains, [(axis, (places[m], 1)) for axis, m in zip(axes, moves)], first=first)
    for chain, (name, mask), axis, sent in zip(chains, moves, axes, sents):
        got = swap(sent, name, mask)
        chain.parts = [[c.pick(axis, (places[name, mask], 0)) for c in p] for p in chain.parts] + [[Cut(got)]]
    return sents


def exchange_merged(plan, places, chains, move, *first):
    axis = chains[0].bits[move]
    sent = join_all(plan, chains, [(axis, (places[move], 1))] * len(chains), merged=True, first=first)[0]
    got = swap(sent, *move)
    for chain in chains:
        chain.parts = [[c.pick(axis, (places[move], 0)) for c in p] for p in chain.parts] + [[Cut(got)]]
    return sent


def finish_kernel(plan, *refs, first, sources, pairs, unit):
    n = len(sources)
    pieces, rests, refs = refs[:n], refs[n:2 * n], refs[2 * n:]
    outer_ref, inner_ref, attn_ref, qkv_ref, bq_ref, bv_ref, *line_refs, vec_ref, turned, vec_qv = refs
    width, dim = outer_ref.shape
    share = attn_ref.shape[0]
    top, part = unit + 32, share // 2
    vec_ref[...] = jnp.zeros(vec_ref.shape, F32)
    vec_qv[...] = jnp.zeros(vec_qv.shape, F32)
    for (e, d), ref, rest in zip(sources, pieces, rests):
        member, side = plan[first + e], lax.rem(plan[first + 2] + d, 2)
        owner = member * 2 + side
        turned[pl.ds(pl.multiple_of(owner * unit, 8), unit), :] = ref[:unit, :width].astype(F32)
        for half in range(2):
            inner_ref[:, pl.ds(pl.multiple_of(owner * 2 * width + half * width, LANES), width)] = (
                ref[half * share:(half + 1) * share, width:].astype(F32))
        attn_ref[pl.ds(pl.multiple_of(owner * 24, 8), 24), :] = ref[unit:unit + 24, :].astype(F32)
        vec_ref[pl.ds(pl.multiple_of(side * 8, 8), 8), :] += ref[unit:top, :].astype(F32)[24:, :]
        rows = pl.ds(pl.multiple_of(side * part, 8), part)
        for block in range(3 * pairs + 1):
            values = rest[:, block * LANES:(block + 1) * LANES].astype(F32)
            if block == 3 * pairs:
                vec_qv[rows, :] += values
            else:
                j, i = divmod(block, 3)
                to = pl.multiple_of(i * dim + (member * pairs + j) * LANES, LANES)
                qkv_ref[rows, pl.ds(to, LANES)] = values
    outer_ref[...] = turned[...].T
    dp = plan[first + 3 + 4 + 4]
    here = pltpu.roll(vec_ref[...], lax.rem(dim - dp * share, dim), 1)
    for i, ref in enumerate(line_refs[:6]):
        ref[...] = here[i, :share]
    per = dim // width
    line_refs[6][...] = vec_ref[pl.ds(8 + dp // per, 1), pl.ds(pl.multiple_of(lax.rem(dp, per) * width, LANES), width)][0]
    bq_ref[...] = vec_qv[0, :share]
    bv_ref[...] = vec_qv[1, :share]


def finish(plan, pieces, rests, sources, first, pairs, unit, width, share, wide):
    dim = pieces[0].shape[1]
    return kernel_call(
        functools.partial(finish_kernel, first=first, sources=sources, pairs=pairs, unit=unit),
        "finish", (1,), (*pieces, *rests), [whole(a) for a in (*pieces, *rests)],
        [((width, dim), F32, None, None), ((share, wide), F32, None, None), ((share, dim), F32, None, None),
         ((share, 3 * dim), F32, None, None)]
        + [((share,), F32, None, None)] * 8 + [((width,), F32, None, None)],
        [pltpu.VMEM((16, dim), F32), pltpu.VMEM((dim, width), F32), pltpu.VMEM((share, LANES), F32)],
        0, 10 * dim * width, 0, (plan,), 16)


def by_owner(parts, member):
    stack = jnp.stack(parts)
    return [lax.dynamic_index_in_dim(stack, member ^ m, 0, keepdims=False) for m in range(len(parts))]


def body(hidden_in, passage_lengths, w_qkv, b_query, b_value, w_attn_out, b_attn_out, gain_attn,
         bias_attn, w_inner, b_inner, w_outer, b_outer, gain_ffn, bias_ffn, grad_out):
    rows, chunk, dim = hidden_in.shape
    n_dp, n_seq = lax.axis_size("dp"), lax.axis_size("seq")
    wide = w_inner.shape[1]
    slots = passage_lengths.shape[1]
    assert slots == SLOTS
    group = n_seq // rows
    seq = lax.axis_index("seq")
    side, member = seq // group, seq % group
    tokens = group * rows * chunk
    cols = HEADS // group * HEAD_DIM
    pairs = -(-cols // LANES)
    padded = pairs * LANES
    aligned = cols % LANES == 0
    count = rows * group
    share = dim // n_dp
    row_at = lambda a, d: lax.dynamic_index_in_dim(a, side ^ d, 0, keepdims=False)

    send = row_at(hidden_in, 1)
    got = swap(send, "seq", group)
    own = row_at(hidden_in, 0)
    cot_send = after(row_at(grad_out, 1), got)
    cot_got = swap(cot_send, "seq", group)

    start = jnp.stack([(side ^ d) * group + (member ^ e) for e in range(group) for d in range(rows)]).astype(jnp.int32)
    ends = jnp.cumsum(row_at(passage_lengths, 0), dtype=jnp.int32)
    segment = lambda p: jnp.sum((p[..., None] >= ends).astype(jnp.int32), axis=-1, dtype=jnp.int32)
    index = jnp.arange(count, dtype=jnp.int32)
    half = chunk // 2
    units = jnp.arange(2 * count, dtype=jnp.int32)
    low_seg, high_seg = segment(index * chunk), segment(index * chunk + (chunk - 1))
    low_key, high_key = segment(units * half), segment(units * half + (half - 1))
    meets = jnp.maximum(low_seg[:, None], low_key[None, :]) <= jnp.minimum(high_seg[:, None], high_key[None, :])
    first_key = jnp.min(jnp.where(meets, units[None, :], 2 * count), axis=1)
    spans = jnp.max(jnp.where(meets, units[None, :], -1), axis=1) + 1 - first_key
    rounded = functools.reduce(lambda r, n: jnp.where(spans <= n, n, r), reversed(key_spans(count)), 2 * count)
    first_key = jnp.minimum(first_key, 2 * count - rounded)
    reorder = lambda a: jnp.sum(jnp.where(start[:, None] == index[None, :], a[None, :], 0), axis=1)
    per = wide // dim // group
    turns = [(member ^ e) * per + r for e in reversed(range(group)) for r in range(per)]
    moves = [("dp", 1 << b) for b in range(len(split_bits(n_dp)))] + [("seq", group)]
    members = jnp.stack([member ^ e for e in range(group)] + [side] + turns
                        + [(lax.axis_index(name) // mask) % 2 for name, mask in moves] + [lax.axis_index("dp")])
    plan = jnp.concatenate([ends, start, reorder(first_key), reorder(rounded), first_key, rounded, members]).astype(jnp.int32)
    first = SLOTS + 5 * count
    places = {m: first + group + 1 + len(turns) + i for i, m in enumerate(moves)}
    first_bias = 8
    vec = jnp.concatenate(
        [b_attn_out, gain_attn, bias_attn, b_outer, gain_ffn, bias_ffn, b_query, b_value, b_inner]
    ).astype(F32).reshape(-1, dim)
    if aligned:
        weights = [w_qkv] * 3, [lambda j, n, i=i: (0, i * group + n[first]) for i in range(3)] + [lambda j, n: (0, n[first])]
        vec_heads = vec
    else:
        widen = lambda a: jnp.pad(a, ((0, 0), (0, padded - cols)))
        weights_of = lambda m: [widen(lax.dynamic_slice_in_dim(w_qkv, m * cols + i * dim, cols, 1)) for i in range(3)]
        vec_heads = widen(lax.dynamic_slice_in_dim(vec, member * cols, cols, 1))
        weights = weights_of(member), [lambda j, n: (0, 0)] * 4

    chunks = [own, got]
    for e in range(1, group):
        chunks += [swap(own, "seq", e), swap(after(got, plan, vec), "seq", e)]

    o_mine, o_send, lse, q, k, v = attend(
        plan, chunks, weights, vec_heads, pairs, rows)
    apart = lambda a: [a] if group == 2 else [a[i * rows * chunk:(i + 1) * rows * chunk] for i in range(group - 1)]
    together = lambda a: a[0] if len(a) == 1 else jnp.concatenate(a, axis=0)
    o_parts = [o_mine] + [swap(a, "seq", e) for e, a in enumerate(apart(o_send), 1)]
    fine = aligned and (wide // n_dp) % LANES == 0 and share % 16 == 0 and per == rows and share == 24 * rows * group
    out_own, out_send, dh1, *made = token_work(
        plan, chunks[:rows], o_parts, w_attn_out, vec, w_inner, w_outer, grad_out, cot_got, cols, padded,
        first_bias, first, n_dp, fine)
    do_parts, made = made[:group], made[group:]
    do_gots = [swap(do_parts[e], "seq", e) for e in range(1, group)]
    out_got = swap(out_send, "seq", group)

    dp_masks = [1 << b for b in range(len(split_bits(n_dp)))]
    bit_shape = split_bits(n_dp) + split_bits(rows)
    bits = {("dp", m): len(dp_masks) - 1 - i for i, m in enumerate(dp_masks)}
    bits["seq", group] = len(dp_masks)

    unit, width = dim // group // rows, wide // n_dp
    if fine:
        feed_parts = made
    else:
        raw_outer, raw_inner, raw_attn, raw_vectors = made
        flat = lambda a: a.reshape(group, n_dp, rows, -1)
        feed_all = jnp.concatenate([
            flat(raw_outer.transpose(1, 0, 2).reshape(group, rows, unit, n_dp, width).transpose(0, 3, 1, 2, 4)),
            flat(raw_inner.transpose(1, 0, 2).reshape(n_dp, share, group, rows, -1).transpose(2, 0, 3, 1, 4)),
            flat(raw_attn.reshape(n_dp, group, rows, -1, dim).transpose(1, 0, 2, 3, 4))], axis=3)
        vectors = jnp.broadcast_to(raw_vectors.reshape(1, rows, -1), (n_dp, rows, 16 * dim // rows)).astype(LOW)
        feed_parts = [
            jnp.concatenate([lax.dynamic_index_in_dim(feed_all, member ^ e, 0, keepdims=False),
                             vectors if e == 0 else jnp.zeros_like(vectors)], axis=2).reshape(n_dp, rows, -1, LANES)
            for e in range(group)]
    ways = 3 if fine else 1
    shaped = lambda a: a.reshape(bit_shape + a.shape[2:])
    by_way = [[feed_parts[e * ways + i] for e in range(group)] for i in range(ways)]
    feeds = [Halving([shaped(p[0])] + [shaped(swap(p[e], "seq", e)) for e in range(1, group)], bits) for p in by_way]
    stages = [("dp", 1), ("seq", group), ("dp", 2)]

    def feed_stage(n, *before):
        moves = [stages[(n + i) % 3] for i in range(ways)]
        if fine:
            return exchange(plan, places, feeds, moves, *before)
        for f, move in zip(feeds, moves):
            f.send(*move, *before)
        return [f.sent for f in feeds]

    if fine:
        sent = []
        for f, move in zip(feeds, stages):
            sent = exchange(plan, places, [f], [move], *sent, *([out_got] + do_gots if f is feeds[-1] else []))
    else:
        sent = feed_stage(0)

    runs = [(0, pairs)]
    part = share // rows
    packed_grads = lambda a: a.reshape(bit_shape + (part, a.shape[-1]))
    d_mine, d_other, small_qkv, *grad_qkv = attend_back(
        plan, chunks, q, k, v, do_parts[0], after(together(do_gots), *sent), lse, pairs, rows,
        share if fine else 0, first)
    if fine:
        rests = [Halving([packed_grads(a)], bits) for a in grad_qkv]
    else:
        heads = lax.dynamic_update_slice_in_dim(jnp.zeros((2, dim), F32), small_qkv[:2, :cols], member * cols, 1)
        vectors = heads.reshape(2, n_dp, -1).transpose(1, 0, 2)
        vectors = jnp.pad(vectors, ((0, 0), (0, rows * part - 2), (0, LANES - share))).astype(LOW).reshape(n_dp, rows, part, LANES)
        rests = [Halving([[packed_grads(grad_qkv[0]), vectors.reshape(bit_shape + vectors.shape[2:])]], bits)]
    rest_moves = [[("dp", 2), ("dp", 1)], [("seq", group), ("dp", 2)], [("dp", 1), ("seq", group)]]
    dp_stages = [("dp", m) for m in dp_masks]

    def rest_stage(n, *before):
        moves = rest_moves[n] if n < 3 else [dp_stages[n - 1]] * 2
        if fine:
            return exchange(plan, places, rests, moves, *before)
        rests[0].send(*moves[0], *before)
        return [rests[0].sent]

    sent = feed_stage(1, d_mine)
    d_gots = [swap(after(a, *sent), "seq", e) for e, a in enumerate(apart(d_other), 1)]
    rest_sent = rest_stage(0, *sent)
    out_first = rest_sent

    runs_of = [[a] for a in [d_mine] + d_gots]
    if aligned:
        in_own, in_send = input_grads(plan, runs_of, runs, w_qkv, after(dh1, *rest_sent), pairs, chunk, first)
    else:
        grad_hidden = dh1
        for e, parts in enumerate(runs_of):
            w = weights_of(member ^ e)
            d = jnp.concatenate(parts, axis=1)
            for j in range(pairs):
                w_pair = jnp.concatenate([a[:, j * LANES:(j + 1) * LANES] for a in w], axis=1)
                grad_hidden = grad_hidden + dot_nt(d[:, j * 3 * LANES:(j + 1) * 3 * LANES], w_pair)
        in_own, in_send = grad_hidden[:chunk], grad_hidden[chunk:].astype(LOW)

    def in_place(own, got):
        return jnp.where(side == 0, jnp.stack([own, got]), jnp.stack([got, own]))

    sent = feed_stage(2, in_send)
    early = [feeds[0].parts[-1][0].array] if fine else sent
    if fine:
        last = ("dp", dp_masks[-1])
        rest_sent = rest_stage(1, *early)
        sent = exchange_merged(plan, places, feeds, last, *rest_sent)
        early = [sent]
        in_got = swap(after(in_send, sent), "seq", group)
        rest_stage(2, sent)
        late = [exchange_merged(plan, places, rests, last)]
    else:
        rest_sent = rest_stage(1, *sent)
        feed = feeds[0]
        in_got = swap(in_send, "seq", group)
        rest_sent = rest_stage(2, *rest_sent)
        for i, mask in enumerate(dp_masks[2:]):
            feed.send("dp", mask, *rest_sent)
            rest_sent = rest_stage(3 + i, feed.sent)
        late = rest_sent
        feed_piece, rest_piece = feed.finish(*late), rests[0].finish()
    out = in_place(after(out_own, *early), out_got[:chunk].astype(F32))
    sums = in_place(after(out_send, *early)[chunk:chunk + slots], out_got[chunk:chunk + slots])
    sums = add_up([sums] + [swap(sums, "seq", e) for e in range(1, group)])
    pooled = sums / jnp.maximum(passage_lengths.astype(F32), 1.0)[:, :, None]
    grad_in = in_place(after(in_own, *early), in_got.astype(F32))

    def everyone(piece):
        gots = [piece] + [swap(piece, "seq", e) for e in range(1, group)]
        return by_owner(gots, member)

    here = lambda a: lax.dynamic_slice_in_dim(a.reshape(-1), lax.axis_index("dp") * (a.size // n_dp), a.size // n_dp)
    if fine:
        sources = [(0, 0), (0, 1), (1, 0), (1, 1)]

        def from_all(piece):
            piece = piece.reshape(piece.shape[-2:])
            got = swap(piece, "seq", group)
            return [piece, got, swap(piece, "seq", 1), swap(got, "seq", 1)]

        feed_piece = join_all(plan, feeds, [None] * ways, merged=True, first=late + [grad_in, pooled, out])[0]
        pieces_of = [from_all(feed_piece)]
        rest_piece = join_all(plan, rests, [None] * 2, merged=True, first=[pieces_of[0][1]])[0]
        pieces_of.append(from_all(rest_piece))
        (grad_w_outer, grad_w_inner, grad_w_attn_out, grad_w_qkv, grad_b_query, grad_b_value, grad_gain_ffn,
         grad_bias_ffn, grad_b_outer, grad_gain_attn, grad_bias_attn, grad_b_attn_out, grad_b_inner) = finish(
            plan, pieces_of[0], pieces_of[1], sources, first, pairs, unit, width, share, wide)
    else:
        feed_pieces = everyone(feed.spread(feed_piece))
        sizes = [unit * width, share * (wide // group // rows), share * dim // group // rows, 16 * dim // rows]
        ends_of = [sum(sizes[:i]) for i in range(5)]
        cut = lambda a, i: a.reshape(rows, -1)[:, ends_of[i]:ends_of[i + 1]]
        grad_w_outer = jnp.concatenate([cut(a, 0).reshape(rows * unit, width) for a in feed_pieces]).T.astype(F32)
        grad_w_inner = jnp.concatenate(
            [cut(a, 1).reshape(rows, share, -1)[r] for a in feed_pieces for r in range(rows)], axis=1).astype(F32)
        grad_w_attn_out = jnp.concatenate([cut(a, 2).reshape(-1, dim) for a in feed_pieces], axis=0).astype(F32)
        totals = add_up([cut(a, 3) for a in feed_pieces]).reshape(16, dim)
        rest_pieces = [a.reshape(share, -1) for a in everyone(rests[0].spread(rest_piece))]
        grad_w_qkv = jnp.concatenate(
            [jnp.concatenate([a[:, (3 * j + i) * LANES:(3 * j + i + 1) * LANES] for j in range(pairs)], axis=1)[:, :cols]
             for i in range(3) for a in rest_pieces], axis=1).astype(F32)
        sums_qv = add_up([a[:, 3 * padded:] for a in rest_pieces])
        (grad_gain_ffn, grad_bias_ffn, grad_b_outer, grad_gain_attn, grad_bias_attn, grad_b_attn_out) = [
            here(totals[i]) for i in range(6)]
        grad_b_inner = here(totals[8:8 + wide // dim])
        grad_b_query, grad_b_value = sums_qv[0, :share], sums_qv[1, :share]

    return (out, pooled, grad_in, grad_w_qkv, grad_b_query, grad_b_value, grad_w_attn_out,
            grad_b_attn_out, grad_gain_attn, grad_bias_attn, grad_w_inner, grad_b_inner,
            grad_w_outer, grad_b_outer, grad_gain_ffn, grad_bias_ffn)


def solution(mesh):
    tokens, rows, all_of = P("dp", "seq", None), P("dp", None), P()
    vector, cube = P("dp"), P("dp", None, None)
    return jax.shard_map(
        body,
        mesh=mesh,
        in_specs=(tokens, rows) + (all_of,) * 13 + (tokens,),
        out_specs=(tokens, cube, tokens, rows, vector, vector, rows, vector, vector, vector, rows,
                   vector, rows, vector, vector, vector),
        check_vma=False,
    )
```
